32 devices in a mesh: dp: 16 (over z, y, x), mp: 2 (over core).
Axes of the slice: x: 2, y: 2, z: 4, core: 2. Of those that a mesh axis runs over, the one named last changes fastest.
Arguments:
- tokens_short: bfloat16 [16, 128, 768], P('dp'), may hold values from -6 to 6
- tokens_middle: bfloat16 [16, 256, 768], P('dp'), may hold values from -6 to 6
- tokens_long: bfloat16 [16, 512, 768], P('dp'), may hold values from -6 to 6
- live_short: int32 [16], P('dp'), may hold values from 1 to 1, as said below
- live_middle: int32 [16], P('dp'), may hold values from 0 to 1, as said below
- live_long: int32 [16], P('dp'), may hold values from 0 to 1, as said below
- first_gain: float32 [768], replicated, may hold values from 0.5 to 1.5
- first_shift: float32 [768], replicated, may hold values from -1.75 to 1.75
- hidden_weight: bfloat16 [12, 768, 768], P('mp'), may hold values from -0.21875 to 0.21875
- hidden_bias: float32 [12, 768], P('mp'), may hold values from -1.75 to 1.75
- score_weight: bfloat16 [12, 768, 512], P('mp'), may hold values from -0.625 to 0.625
- score_bias: float32 [12, 512], P('mp'), may hold values from -6 to 6
- value_weight: bfloat16 [768, 768], P(None, 'mp'), may hold values from -0.21875 to 0.21875
- value_bias: float32 [768], P('mp'), may hold values from -1.75 to 1.75
- output_weight: bfloat16 [768, 768], P('mp'), may hold values from -0.875 to 0.875
- output_bias: float32 [768], replicated, may hold values from -1.75 to 1.75
- second_gain: float32 [768], replicated, may hold values from 0.5 to 1.5
- second_shift: float32 [768], replicated, may hold values from -1.75 to 1.75
- expand_weight: bfloat16 [768, 3072], P(None, 'mp'), may hold values from -0.21875 to 0.21875
- expand_bias: float32 [3072], P('mp'), may hold values from -1.75 to 1.75
- reduce_weight: bfloat16 [3072, 768], P('mp'), may hold values from -0.109375 to 0.109375
- reduce_bias: float32 [768], replicated, may hold values from -1.75 to 1.75
- cotangent_short: bfloat16 [16, 128, 768], P('dp'), may hold values from -6 to 6
- cotangent_middle: bfloat16 [16, 256, 768], P('dp'), may hold values from -6 to 6
- cotangent_long: bfloat16 [16, 512, 768], P('dp'), may hold values from -6 to 6
Outputs:
- output_short: bfloat16 [16, 128, 768], P('dp')
- output_middle: bfloat16 [16, 256, 768], P('dp')
- output_long: bfloat16 [16, 512, 768], P('dp')
- gradient_short: bfloat16 [16, 128, 768], P('dp')
- gradient_middle: bfloat16 [16, 256, 768], P('dp')
- gradient_long: bfloat16 [16, 512, 768], P('dp')
- first_gain_gradient: float32 [768], replicated
- first_shift_gradient: float32 [768], replicated
- hidden_weight_gradient: float32 [7077888], P(('mp', 'dp'))
- hidden_bias_gradient: float32 [12, 768], P('mp')
- score_weight_gradient: float32 [4718592], P(('mp', 'dp'))
- score_bias_gradient: float32 [12, 512], P('mp')
- value_weight_gradient: float32 [589824], P(('mp', 'dp'))
- value_bias_gradient: float32 [768], P('mp')
- output_weight_gradient: float32 [589824], P(('mp', 'dp'))
- output_bias_gradient: float32 [768], replicated
- second_gain_gradient: float32 [768], replicated
- second_shift_gradient: float32 [768], replicated
- expand_weight_gradient: float32 [2359296], P(('mp', 'dp'))
- expand_bias_gradient: float32 [3072], P('mp')
- reduce_weight_gradient: float32 [2359296], P(('mp', 'dp'))
- reduce_bias_gradient: float32 [768], replicated
The draws below stay inside these ranges and needn't reach their ends.
Inputs may be any that keep to these rules, and one draw needn't show every extreme that they name: On dp index i the slots 0 to live_short[i] - 1 of the first bucket hold sequences, the others padding; some dp index has all 1 slots live. `live_middle`: likewise for the 1 slots of the second bucket; some dp index has all of them live. `live_long`: likewise for the 1 slots of the third bucket; some dp index has all of them live.
All inputs are finite; a program needn't handle non-finite values.
Results may differ from the reference program's by a relative error of at most 0.012.
The reference program's roundings to bfloat16 on the way count: a program that leaves them out, or rounds other values in their place, can miss the bound.
Values sent between devices are 32-bit elements; how exact they have to be, the bound alone decides.
A program may use at most 192 MiB of HBM per device.

```python
from functools import partial
import jax
import jax.numpy as jnp
from jax import lax

D = 768
HEADS = 12
FF = 3072
LEN_A = 128
LEN_B = 256
LEN_C = 512
SLOT_A = 1
SLOT_B = 1
SLOT_C = 1
SEQ_A = 16
SEQ_B = 16
SEQ_C = 16
N_DP = 16


def count_draw(key, slot_count, floor_value):
    picked = jax.random.randint(key, (N_DP,), slot_count // 2, slot_count + 1)
    picked = jnp.maximum(picked, floor_value)
    full_device = jax.random.randint(jax.random.fold_in(key, 7), (), 0, N_DP)
    return jnp.where(jnp.arange(N_DP) == full_device, slot_count, picked).astype(jnp.int32)


def draw_live_short(key, part):
    key = jax.random.fold_in(key, 11)
    return count_draw(key, SLOT_A, 1)


def draw_live_middle(key, part):
    key = jax.random.fold_in(key, 12)
    return count_draw(key, SLOT_B, 0)


def draw_live_long(key, part):
    key = jax.random.fold_in(key, 13)
    return count_draw(key, SLOT_C, 0)


def with_spikes(values, own_key, source, target, parts, factor):
    def block_of(position):
        return (jnp.arange(values.shape[position]) // (values.shape[position] // parts)).reshape((-1,) + (1,) * (values.ndim - 1 - position))

    first = jax.random.permutation(own_key, parts)[block_of(target)]
    far = (block_of(target) + parts // 2) % parts
    return jnp.where((block_of(source) == first) | (block_of(source) == far), factor * values, values)


def level_of(key, extent, split, smallest, top_value):
    factor_of = 1.0
    for axis_at, shards_of in split:
        draws = jax.random.uniform(jax.random.fold_in(jax.random.fold_in(key, 6), axis_at), (shards_of,), jnp.float32, smallest / len(split), top_value / len(split))
        factor_of = factor_of * jnp.repeat(jnp.exp(draws), extent[axis_at] // shards_of).reshape((-1,) + (1,) * (len(extent) - 1 - axis_at))
    return factor_of


def bell_draw(rng, extent, width, bound, split=(), kind=jnp.bfloat16):
    level = level_of(rng, extent, split, -0.22, 0.18) if split else 1.0
    drawn = jax.random.normal(rng, extent, jnp.float32) * width * level
    return jnp.minimum(jnp.maximum(drawn, -bound), bound).astype(kind)


def heavy_noise(own_key, extent, scale, most, pieces, heavy, dtype=jnp.bfloat16):
    values = scale * jax.random.normal(own_key, extent, jnp.float32)
    if pieces:
        values = values * level_of(own_key, extent, pieces, -0.22, 0.18)
    return jnp.clip(with_spikes(values, jax.random.fold_in(own_key, 3), *heavy), -most, most).astype(dtype)


def setup_inputs(seed: int = 0) -> dict:
    seeds = jax.random.split(jax.random.key(seed), 26)
    return {
        "tokens_short": heavy_noise(seeds[0], (SEQ_A, LEN_A, D), 1.0, 6.0, ((0, 16),), (0, 2, 16, 2.0)),
        "tokens_middle": heavy_noise(seeds[1], (SEQ_B, LEN_B, D), 1.0, 6.0, ((0, 16),), (0, 2, 16, 2.0)),
        "tokens_long": heavy_noise(seeds[2], (SEQ_C, LEN_C, D), 1.0, 6.0, ((0, 16),), (0, 2, 16, 2.0)),
        "live_short": draw_live_short(jax.random.fold_in(seeds[25], 71), 0),
        "live_middle": draw_live_middle(jax.random.fold_in(seeds[25], 71), 0),
        "live_long": draw_live_long(jax.random.fold_in(seeds[25], 71), 0),
        "first_gain": jnp.clip(1.0 + 0.1 * jax.random.normal(seeds[6], (D,), jnp.float32), 0.5, 1.5),
        "first_shift": bell_draw(seeds[7], (D,), 0.3, 1.75, (), jnp.float32),
        "hidden_weight": bell_draw(seeds[8], (HEADS, D, D), D ** -0.5, 0.21875, ((0, 2),)),
        "hidden_bias": bell_draw(seeds[9], (HEADS, D), 0.3, 1.75, ((0, 2),), jnp.float32),
        "score_weight": bell_draw(seeds[10], (HEADS, D, LEN_C), (D // 8) ** -0.5, 0.625, ((0, 2),)),
        "score_bias": bell_draw(seeds[11], (HEADS, LEN_C), 1.0, 6.0, ((0, 2),), jnp.float32),
        "value_weight": bell_draw(seeds[12], (D, D), D ** -0.5, 0.21875, ((1, 2),)),
        "value_bias": bell_draw(seeds[13], (D,), 0.3, 1.75, ((0, 2),), jnp.float32),
        "output_weight": bell_draw(seeds[14], (D, D), (D // 16) ** -0.5, 0.875, ((0, 2),)),
        "output_bias": bell_draw(seeds[15], (D,), 0.3, 1.75, (), jnp.float32),
        "second_gain": jnp.clip(1.0 + 0.1 * jax.random.normal(seeds[16], (D,), jnp.float32), 0.5, 1.5),
        "second_shift": bell_draw(seeds[17], (D,), 0.3, 1.75, (), jnp.float32),
        "expand_weight": bell_draw(seeds[18], (D, FF), D ** -0.5, 0.21875, ((1, 2),)),
        "expand_bias": bell_draw(seeds[19], (FF,), 0.3, 1.75, ((0, 2),), jnp.float32),
        "reduce_weight": bell_draw(seeds[20], (FF, D), FF ** -0.5, 0.109375, ((0, 2),)),
        "reduce_bias": bell_draw(seeds[21], (D,), 0.3, 1.75, (), jnp.float32),
        "cotangent_short": heavy_noise(seeds[22], (SEQ_A, LEN_A, D), 1.0, 6.0, ((0, 16),), (0, 2, 16, 2.0)),
        "cotangent_middle": heavy_noise(seeds[23], (SEQ_B, LEN_B, D), 1.0, 6.0, ((0, 16),), (0, 2, 16, 2.0)),
        "cotangent_long": heavy_noise(seeds[24], (SEQ_C, LEN_C, D), 1.0, 6.0, ((0, 16),), (0, 2, 16, 2.0)),
    }


epsilon = 1e-05
HIGHEST = lax.Precision.HIGHEST

@jax.custom_vjp
def low(v):
    return lax.optimization_barrier(v.astype(jnp.bfloat16)).astype(jnp.float32)

@jax.custom_vjp
def low_back(v):
    return v

def low_keep(v):
    return (low(v), None)

def low_pass(kept, grad):
    return (grad,)

def back_keep(v):
    return (v, None)

def back_low(kept, grad):
    return (low(grad),)
low.defvjp(low_keep, low_pass)
low_back.defvjp(back_keep, back_low)

def layer_norm(values, gains, offset):
    centred = values - lax.optimization_barrier(jnp.mean(values, axis=-1, keepdims=True))
    variance = lax.optimization_barrier(jnp.mean(centred * centred, axis=-1, keepdims=True))
    return centred * lax.rsqrt(variance + epsilon) * gains + offset

def product(form, left, right):
    return jnp.einsum(form, left, right, precision=HIGHEST)

def group_forward(params, inputs, live_rows):
    first_gain, first_shift, hidden_weight, hidden_bias, score_weight, score_bias, value_weight, value_bias, output_weight, output_bias, second_gain, second_shift, expand_weight, expand_bias, reduce_weight, reduce_bias = params
    features = inputs[0].shape[2]
    head_count = hidden_weight.shape[0]
    head_width = value_weight.shape[1] // head_count
    tokens = jnp.concatenate([piece.reshape(-1, features) for piece in inputs], axis=0)
    normed = low(layer_norm(tokens, first_gain, first_shift))
    hidden_input = low_back(product('td,hde->hte', normed, hidden_weight) + hidden_bias[:, None, :])
    hidden = low(jax.nn.gelu(hidden_input))
    values = low(low_back(product('td,dc->tc', normed, value_weight) + value_bias))
    mixing_parts = []
    row_start = 0
    for bucket in range(3):
        slot_count = inputs[bucket].shape[0]
        length = inputs[bucket].shape[1]
        row_count = slot_count * length
        block_hidden = hidden[:, row_start:row_start + row_count]
        scores = low_back(product('hnd,hdk->hnk', block_hidden, score_weight[:, :, :length]) + score_bias[:, None, :length])
        attention = low(jax.nn.softmax(scores, axis=-1)).reshape(head_count, slot_count, length, length)
        block_values = values[row_start:row_start + row_count].reshape(slot_count, length, head_count, head_width)
        mixing = low(low_back(product('hsqk,skhe->sqhe', attention, block_values)))
        mixing_parts.append(mixing.reshape(row_count, head_count * head_width))
        row_start = row_start + row_count
    mixing = jnp.concatenate(mixing_parts, axis=0)
    attended = low_back(product('tc,cd->td', mixing, output_weight) + output_bias)
    middle = tokens + attended
    second = low(layer_norm(middle, second_gain, second_shift))
    expand_input = low_back(product('td,df->tf', second, expand_weight) + expand_bias)
    activated = low(jax.nn.gelu(expand_input))
    branch = low_back(product('tf,fd->td', activated, reduce_weight) + reduce_bias)
    return live_rows[:, None] * (middle + branch)

def reference(tokens_short, tokens_middle, tokens_long, live_short, live_middle, live_long, first_gain, first_shift, hidden_weight, hidden_bias, score_weight, score_bias, value_weight, value_bias, output_weight, output_bias, second_gain, second_shift, expand_weight, expand_bias, reduce_weight, reduce_bias, cotangent_short, cotangent_middle, cotangent_long):
    params = tuple((member.astype(jnp.float32) for member in (first_gain, first_shift, hidden_weight, hidden_bias, score_weight, score_bias, value_weight, value_bias, output_weight, output_bias, second_gain, second_shift, expand_weight, expand_bias, reduce_weight, reduce_bias)))
    slot_list = (SLOT_A, SLOT_B, SLOT_C)
    length_list = (LEN_A, LEN_B, LEN_C)

    def regroup(array, bucket):
        return array.astype(jnp.float32).reshape(N_DP, slot_list[bucket], length_list[bucket], D)
    group_inputs = tuple((regroup(piece, bucket) for bucket, piece in enumerate((tokens_short, tokens_middle, tokens_long))))
    group_cotangents = tuple((regroup(piece, bucket) for bucket, piece in enumerate((cotangent_short, cotangent_middle, cotangent_long))))
    group_counts = jnp.stack([live_short, live_middle, live_long], axis=1).astype(jnp.int32)

    def step(totals, group):
        inputs, cotangents, counts = group
        live_rows = jnp.concatenate([jnp.repeat((jnp.arange(slot_list[bucket]) < counts[bucket]).astype(jnp.float32), length_list[bucket]) for bucket in range(3)])
        outputs, pullback = jax.vjp(partial(group_forward, live_rows=live_rows), params, inputs)
        cotangent_rows = jnp.concatenate([piece.reshape(-1, D) for piece in cotangents], axis=0)
        param_grads, input_grads = pullback(cotangent_rows)
        return (jax.tree.map(jnp.add, totals, param_grads), (outputs, input_grads))
    totals, (outputs, input_grads) = lax.scan(step, jax.tree.map(jnp.zeros_like, params), (group_inputs, group_cotangents, group_counts))
    first_end = SLOT_A * LEN_A
    second_end = first_end + SLOT_B * LEN_B
    output_short = outputs[:, :first_end].reshape(SEQ_A, LEN_A, D).astype(jnp.bfloat16)
    output_middle = outputs[:, first_end:second_end].reshape(SEQ_B, LEN_B, D).astype(jnp.bfloat16)
    output_long = outputs[:, second_end:].reshape(SEQ_C, LEN_C, D).astype(jnp.bfloat16)
    gradient_short = input_grads[0].reshape(SEQ_A, LEN_A, D).astype(jnp.bfloat16)
    gradient_middle = input_grads[1].reshape(SEQ_B, LEN_B, D).astype(jnp.bfloat16)
    gradient_long = input_grads[2].reshape(SEQ_C, LEN_C, D).astype(jnp.bfloat16)
    return (output_short, output_middle, output_long, gradient_short, gradient_middle, gradient_long, totals[0], totals[1], totals[2].reshape(-1), totals[3], totals[4].reshape(-1), totals[5], jnp.transpose(totals[6]).reshape(-1), totals[7], totals[8].reshape(-1), totals[9], totals[10], totals[11], jnp.transpose(totals[12]).reshape(-1), totals[13], totals[14].reshape(-1), totals[15])
```

```python
import jax
import jax.numpy as jnp
from jax import lax
from jax.experimental import pallas as pl
from jax.experimental.pallas import tpu as pltpu
from jax.sharding import PartitionSpec as P

epsilon = 1e-05


SLOTS = 4
ITEMS = 15
LAGS = 5
HALF = 144
EDGE = 24
WIDE = 48
FIRST = EDGE + WIDE
SMALL_ROWS = 112
MESH_ID = pl.DeviceIdType.MESH


def dot_rows(left, right):
    return lax.dot_general(
        left, right, (((0,), (0,)), ((), ())), preferred_element_type=jnp.float32
    )


def scatter_kernel(
    active_h, branch_h, grown_h, second_h, value_h, normed_h, mixing_h, attended_h,
    hidden_h, score_a_h, score_b_h, score_c_h, input_h, small_ref,
    out_ref, small_out,
    active, branch, grown, second, value, normed, mixing, attended,
    hidden, score_a, score_b, score_c, inputs, flipped,
    own, first_x, first_y, next_x, next_y, middle, middle_up, middle_down,
    edge, edge_up, edge_down, last_x, last_y,
    small_x, small_sum, small_y, small_z,
    load_sems, first_sems, next_sems, middle_sems, edge_sems, last_sems, small_sems,
):
    spot = lax.axis_index("dp")
    x, y, z = spot % 2, (spot // 2) % 2, spot // 4
    to_x = {"dp": spot + 1 - 2 * x}
    to_y = {"dp": spot + 2 - 4 * y}
    to_up = {"dp": spot + 4}
    to_down = {"dp": spot - 4}

    loads = []
    for number, (source, target) in enumerate(
        (
            (active_h, active), (branch_h, branch), (grown_h, grown), (second_h, second),
            (value_h, value), (normed_h, normed), (mixing_h, mixing), (attended_h, attended),
            (hidden_h, hidden), (score_a_h, score_a), (score_b_h, score_b), (score_c_h, score_c),
            (input_h, inputs),
        )
    ):
        loads.append(pltpu.make_async_copy(source, target, load_sems.at[number]))
    for load in loads:
        load.start()

    barrier = pltpu.get_barrier_semaphore()
    pl.semaphore_signal(barrier, inc=1, device_id=to_x, device_id_type=MESH_ID)
    pl.semaphore_signal(barrier, inc=1, device_id=to_y, device_id_type=MESH_ID)

    @pl.when(z < 3)
    def _():
        pl.semaphore_signal(barrier, inc=1, device_id=to_up, device_id_type=MESH_ID)

    @pl.when(z > 0)
    def _():
        pl.semaphore_signal(barrier, inc=1, device_id=to_down, device_id_type=MESH_ID)

    inner = (z > 0) & (z < 3)

    @pl.when(inner)
    def _():
        pl.semaphore_wait(barrier, 4)

    @pl.when(jnp.logical_not(inner))
    def _():
        pl.semaphore_wait(barrier, 3)

    def remote(source, target, sems, slot, device):
        return pltpu.make_async_remote_copy(
            src_ref=source,
            dst_ref=target,
            send_sem=sems.at[0, slot],
            recv_sem=sems.at[1, slot],
            device_id=device,
            device_id_type=MESH_ID,
        )

    def put(slot, dest, row, block):
        z_at, y_at, x_at = dest // 4, (dest // 2) % 2, dest % 2
        end = row + block.shape[0]
        for half in range(2):
            low, high = max(row, HALF * half), min(end, HALF * (half + 1))
            if low < high:
                own[slot, half, z_at, y_at, x_at, low - HALF * half : high - HALF * half, :] = block[
                    low - row : high - row
                ]

    def produce(item):
        slot = item % 2

        @pl.when(item == 0)
        def _():
            loads[0].wait()
            loads[1].wait()

        @pl.when(item == 2)
        def _():
            loads[2].wait()
            loads[3].wait()

        @pl.when(item == 4)
        def _():
            for number in range(4, 8):
                loads[number].wait()

        @pl.when(item == 5)
        def _():
            for number in range(8, 12):
                loads[number].wait()

        @pl.when(item == 9)
        def _():
            loads[12].wait()
            flipped[...] = normed[...].T

        def feed_forward(left, right, column):
            for piece in range(3):
                block = dot_rows(
                    left[...], right[:, pl.ds(pl.multiple_of(column + 128 * piece, 128), 128)]
                )
                for dest in range(16):
                    put(slot, dest, 96 * piece, block[96 * dest : 96 * dest + 96])

        @pl.when(item < 2)
        def _():
            feed_forward(active, branch, 384 * item)

        @pl.when((item >= 2) & (item < 4))
        def _():
            feed_forward(grown, second, 384 * (item - 2))

        @pl.when(item == 4)
        def _():
            for start, left, right in ((0, value, normed), (HALF, mixing, attended)):
                block = dot_rows(left[...], right[...])
                for dest in range(16):
                    for piece in range(6):
                        put(
                            slot, dest, start + 24 * piece,
                            block[24 * dest : 24 * dest + 24, 128 * piece : 128 * piece + 128],
                        )

        def put_head(head, block):
            for piece in range(8):
                unit = 8 * head + piece
                put(slot, unit // 3, 96 * (unit % 3), block[96 * piece : 96 * piece + 96])

        @pl.when(item == 5)
        def _():
            for head in range(6):
                block = dot_rows(hidden[head, 0:128], score_a[head])
                block += dot_rows(hidden[head, 128:384], score_b[head, :, 0:128])
                block += dot_rows(hidden[head, 384:896], score_c[head, :, 0:128])
                put_head(head, block)

        @pl.when(item == 6)
        def _():
            for head in range(6):
                block = dot_rows(hidden[head, 128:384], score_b[head, :, 128:256])
                block += dot_rows(hidden[head, 384:896], score_c[head, :, 128:256])
                put_head(head, block)

        @pl.when((item == 7) | (item == 8))
        def _():
            column = pl.multiple_of(128 * (item - 5), 128)
            for head in range(6):
                put_head(
                    head, dot_rows(hidden[head, 384:896], score_c[head, :, pl.ds(column, 128)])
                )

        @pl.when(item >= 9)
        def _():
            column = pl.multiple_of(128 * (item - 9), 128)
            for head in range(6):
                put_head(
                    head,
                    jnp.dot(
                        flipped[...],
                        inputs[head, :, pl.ds(column, 128)],
                        preferred_element_type=jnp.float32,
                    ),
                )

    def home(i):
        return own.at[(i // 2) % 2, i % 2], i % SLOTS

    def first_copies(i):
        held, slot = home(i)
        return (
            remote(held.at[:, :, 1 - x, 0:FIRST], first_x.at[slot], first_sems.at[0], slot, to_x),
            remote(held.at[:, 1 - y, :, FIRST:HALF], first_y.at[slot], first_sems.at[1], slot, to_y),
        )

    def next_copies(i):
        held, slot = home(i)
        return (
            remote(held.at[:, y, 1 - x, FIRST : FIRST + EDGE], next_x.at[slot], next_sems.at[0], slot, to_x),
            remote(held.at[:, 1 - y, x, 0:EDGE], next_y.at[slot], next_sems.at[1], slot, to_y),
        )

    def last_copies(i):
        slot = i % SLOTS
        return (
            remote(middle.at[slot, z, 3 - x], last_x.at[slot], last_sems.at[0], slot, to_x),
            remote(middle.at[slot, z, 1 - y], last_y.at[slot], last_sems.at[1], slot, to_y),
        )

    def line_up(kept, landing, sems, slot, place):
        return remote(kept.at[slot, place + 1 : 4], landing.at[slot, place:3], sems.at[0], slot, to_up)

    def line_down(kept, landing, sems, slot, place):
        return remote(kept.at[slot, 0:place], landing.at[slot, 0:place], sems.at[1], slot, to_down)

    def line_hop(kept, landing_up, landing_down, sems, i, hop):
        slot = i % SLOTS
        for place in range(4):
            if place == hop:

                @pl.when(z == place)
                def _():
                    if place > 0:
                        line_up(kept, landing_up, sems, slot, place - 1).wait_recv()
                        kept[slot, place:4] += landing_up[slot, place - 1 : 3]
                    if place < 3:
                        line_up(kept, landing_up, sems, slot, place).start()

            if 3 - place == hop:

                @pl.when(z == place)
                def _():
                    if place < 3:
                        line_down(kept, landing_down, sems, slot, place + 1).wait_recv()
                        kept[slot, 0 : place + 1] += landing_down[slot, 0 : place + 1]
                    if place > 0:
                        line_down(kept, landing_down, sems, slot, place).start()

    def line_sent(kept, landing_up, landing_down, sems, i):
        slot = i % SLOTS
        for place in range(4):

            @pl.when(z == place)
            def _():
                if place < 3:
                    line_up(kept, landing_up, sems, slot, place).wait_send()
                if place > 0:
                    line_down(kept, landing_down, sems, slot, place).wait_send()

    middle_line = (middle, middle_up, middle_down, middle_sems)
    edge_line = (edge, edge_up, edge_down, edge_sems)

    def small_steps(t):
        def copy(number, source, target, device):
            return pltpu.make_async_remote_copy(
                src_ref=source, dst_ref=target, send_sem=small_sems.at[0, number],
                recv_sem=small_sems.at[1, number], device_id=device, device_id_type=MESH_ID,
            )

        over_x = copy(0, small_ref, small_x, to_x)
        over_y = copy(1, small_sum, small_y, to_y)

        def up(place):
            part = small_z.at[0 : place + 1]
            return copy(2, part, part, to_up)

        def down(place):
            part = small_z.at[place:4]
            return copy(3, part, part, to_down)

        @pl.when(t == 0)
        def _():
            over_x.start()

        @pl.when(t == 1)
        def _():
            over_x.wait()
            small_sum[...] = small_ref[...] + small_x[...]
            over_y.start()

        @pl.when(t == 2)
        def _():
            over_y.wait()
            small_z[z] = small_sum[...] + small_y[...]

        for place in range(4):

            @pl.when((z == place) & (t == 2 + place))
            def _():
                if place > 0:
                    up(place - 1).wait_recv()
                if place < 3:
                    up(place).start()

            @pl.when((z == place) & (t == 5 - place))
            def _():
                if place < 3:
                    down(place + 1).wait_recv()
                if place > 0:
                    down(place).start()

        @pl.when(t == 6)
        def _():
            small_out[...] = ((small_z[0] + small_z[1]) + small_z[2]) + small_z[3]
            for place in range(4):

                @pl.when(z == place)
                def _():
                    if place < 3:
                        up(place).wait_send()
                    if place > 0:
                        down(place).wait_send()

    steps = 2 * ITEMS
    produce(0)

    def step(t, carry):
        def at_lag(lag):
            i = t - lag
            return i, (i >= 0) & (i < steps)

        @pl.when(t < steps)
        def _():
            for copy in first_copies(t):
                copy.start()

        small_steps(t)

        i, alive = at_lag(5)

        @pl.when(alive)
        def _():
            held, slot = home(i)
            for copy in last_copies(i):
                copy.wait()
            line_hop(*edge_line, i, 3)
            line_sent(*middle_line, i)
            line_sent(*edge_line, i)
            done = out_ref.at[i // 2, i % 2]
            done[0:EDGE] = edge[slot, z, 0]
            done[EDGE:FIRST] = middle[slot, z, y] + last_y[slot]
            done[FIRST : FIRST + EDGE] = edge[slot, z, 1]
            done[FIRST + EDGE : HALF] = middle[slot, z, 2 + x] + last_x[slot]

        i, alive = at_lag(4)

        @pl.when(alive)
        def _():
            line_hop(*middle_line, i, 3)
            for copy in last_copies(i):
                copy.start()
            line_hop(*edge_line, i, 2)

        i, alive = at_lag(3)

        @pl.when(alive)
        def _():
            line_hop(*middle_line, i, 2)
            line_hop(*edge_line, i, 1)

        i, alive = at_lag(2)

        @pl.when(alive)
        def _():
            held, slot = home(i)
            line_hop(*middle_line, i, 1)
            for copy in next_copies(i):
                copy.wait()
            edge[slot, :, 0] = held[:, y, x, 0:EDGE] + next_y[slot]
            edge[slot, :, 1] = held[:, y, x, FIRST : FIRST + EDGE] + next_x[slot]
            line_hop(*edge_line, i, 0)

        i, alive = at_lag(1)

        @pl.when(alive)
        def _():
            held, slot = home(i)
            for copy in first_copies(i):
                copy.wait()
            middle[slot, :, 0:2] = (
                held[:, :, x, EDGE:FIRST] + first_x[slot, :, :, EDGE:FIRST]
            )
            middle[slot, :, 2:4] = (
                held[:, y, :, FIRST + EDGE : HALF] + first_y[slot, :, :, EDGE:FIRST]
            )
            line_hop(*middle_line, i, 0)
            held[:, :, x, 0:EDGE] += first_x[slot, :, :, 0:EDGE]
            held[:, y, :, FIRST : FIRST + EDGE] += first_y[slot, :, :, 0:EDGE]
            for copy in next_copies(i):
                copy.start()

        @pl.when((t % 2 == 1) & (t < steps - 1))
        def _():
            produce(t // 2 + 1)

        return carry

    lax.fori_loop(0, steps + LAGS, step, 0)


def scatter_call(operands, small):
    f32 = jnp.float32
    scratch = [pltpu.VMEM(member.shape, member.dtype) for member in operands]
    normed = operands[5]
    scratch += [
        pltpu.VMEM((normed.shape[1], normed.shape[0]), normed.dtype),
        pltpu.VMEM((2, 2, 4, 2, 2, HALF, 128), f32),
        pltpu.VMEM((SLOTS, 4, 2, FIRST, 128), f32),
        pltpu.VMEM((SLOTS, 4, 2, FIRST, 128), f32),
        pltpu.VMEM((SLOTS, 4, EDGE, 128), f32),
        pltpu.VMEM((SLOTS, 4, EDGE, 128), f32),
        pltpu.VMEM((SLOTS, 4, 4, WIDE, 128), f32),
        pltpu.VMEM((SLOTS, 3, 4, WIDE, 128), f32),
        pltpu.VMEM((SLOTS, 3, 4, WIDE, 128), f32),
        pltpu.VMEM((SLOTS, 4, 2, EDGE, 128), f32),
        pltpu.VMEM((SLOTS, 3, 2, EDGE, 128), f32),
        pltpu.VMEM((SLOTS, 3, 2, EDGE, 128), f32),
        pltpu.VMEM((SLOTS, WIDE, 128), f32),
        pltpu.VMEM((SLOTS, WIDE, 128), f32),
        pltpu.VMEM((SMALL_ROWS, 128), f32),
        pltpu.VMEM((SMALL_ROWS, 128), f32),
        pltpu.VMEM((SMALL_ROWS, 128), f32),
        pltpu.VMEM((4, SMALL_ROWS, 128), f32),
        pltpu.SemaphoreType.DMA((len(operands),)),
        pltpu.SemaphoreType.DMA((2, 2, SLOTS)),
        pltpu.SemaphoreType.DMA((2, 2, SLOTS)),
        pltpu.SemaphoreType.DMA((2, 2, SLOTS)),
        pltpu.SemaphoreType.DMA((2, 2, SLOTS)),
        pltpu.SemaphoreType.DMA((2, 2, SLOTS)),
        pltpu.SemaphoreType.DMA((2, 4)),
    ]
    return pl.pallas_call(
        scatter_kernel,
        out_shape=(
            jax.ShapeDtypeStruct((ITEMS, 2, HALF, 128), f32),
            jax.ShapeDtypeStruct((SMALL_ROWS, 128), f32),
        ),
        in_specs=[pl.BlockSpec(memory_space=pl.ANY)] * len(operands)
        + [pl.BlockSpec(memory_space=pltpu.VMEM)],
        out_specs=(pl.BlockSpec(memory_space=pltpu.VMEM),) * 2,
        scratch_shapes=scratch,
        compiler_params=pltpu.CompilerParams(
            collective_id=1, has_side_effects=True, vmem_limit_bytes=60 * 2**20
        ),
        name="weight_gradient_scatter",
    )(*operands, small)


def layer_norm(values, gains, offset):
    centred = values - jnp.mean(values, axis=-1, keepdims=True)
    variance = jnp.mean(centred * centred, axis=-1, keepdims=True)
    return centred * lax.rsqrt(variance + epsilon) * gains + offset


def product(form, left, right):
    return jnp.einsum(form, left, right, preferred_element_type=jnp.float32)


def gelu_backward(inputs, upstream):
    return jax.vjp(jax.nn.gelu, inputs)[1](upstream)[0]


def live_flags(count_array, slot_count, length):
    flags = (jnp.arange(slot_count) < count_array[0]).astype(jnp.float32)
    return jnp.repeat(flags, length)


def pair_sum(part):
    size = lax.axis_size("mp")
    if size != 2:
        return lax.psum(part, "mp")
    return part + lax.ppermute(part, "mp", [(0, 1), (1, 0)])


def plain_sums(operands, partial_sums):
    active, branch, grown, second, value, normed, mixing, attended, hidden = operands[:9]
    score_parts, inputs = operands[9:12], operands[12]
    full_length = score_parts[2].shape[2]
    score_total = 0.0
    row_start = 0
    for part in score_parts:
        rows, length = part.shape[1:]
        block = product("hnd,hnk->hdk", hidden[:, row_start : row_start + rows], part)
        score_total = score_total + jnp.pad(block, ((0, 0), (0, 0), (0, full_length - length)))
        row_start = row_start + rows
    gradients = (
        product("td,hte->hde", normed, inputs),
        score_total,
        product("tc,td->cd", value, normed),
        product("tc,td->cd", mixing, attended),
        product("tf,td->fd", grown, second),
        product("tf,td->fd", active, branch),
    )
    shares = [
        lax.psum_scatter(member.reshape(-1), "dp", scatter_dimension=0, tiled=True)
        for member in gradients
    ]
    return shares, lax.psum(partial_sums, "dp")


def grid_sums(operands, partial_sums):
    flat = jnp.concatenate([member.reshape(-1) for member in partial_sums])
    small = jnp.pad(flat, (0, SMALL_ROWS * 128 - flat.size)).reshape(SMALL_ROWS, 128)
    shares, small = scatter_call(operands, small)
    shares = shares.reshape(ITEMS, 2 * HALF, 128)

    def tall(part):
        return part.transpose(1, 0, 2).reshape(-1)

    def grouped(part, rows):
        return part.reshape(-1, rows, 128).transpose(1, 0, 2).reshape(-1)

    weight_gradients = (
        tall(shares[9:15]),
        tall(shares[5:9]),
        grouped(shares[4, :HALF], 24),
        grouped(shares[4, HALF:], 24),
        grouped(shares[2:4], 96),
        grouped(shares[0:2], 96),
    )
    flat = small.reshape(-1)
    totals = []
    start = 0
    for member in partial_sums:
        totals.append(flat[start : start + member.size].reshape(member.shape))
        start = start + member.size
    return weight_gradients, totals


def body(
    tokens_short,
    tokens_middle,
    tokens_long,
    live_short,
    live_middle,
    live_long,
    first_gain,
    first_shift,
    hidden_weight,
    hidden_bias,
    score_weight,
    score_bias,
    value_weight,
    value_bias,
    output_weight,
    output_bias,
    second_gain,
    second_shift,
    expand_weight,
    expand_bias,
    reduce_weight,
    reduce_bias,
    cotangent_short,
    cotangent_middle,
    cotangent_long,
):
    pieces = (tokens_short, tokens_middle, tokens_long)
    cotangents = (cotangent_short, cotangent_middle, cotangent_long)
    live_counts = (live_short, live_middle, live_long)
    features = tokens_short.shape[2]
    head_count = hidden_weight.shape[0]
    head_width = value_weight.shape[1] // head_count
    full_length = score_weight.shape[2]
    lengths = [piece.shape[1] for piece in pieces]
    slot_counts = [piece.shape[0] for piece in pieces]
    row_counts = [slot_counts[bucket] * lengths[bucket] for bucket in range(3)]
    row_starts = [0, row_counts[0], row_counts[0] + row_counts[1]]
    tokens = jnp.concatenate([piece.reshape(-1, features) for piece in pieces], axis=0)
    token_values = tokens.astype(jnp.float32)
    live_rows = jnp.concatenate(
        [
            live_flags(live_counts[bucket], slot_counts[bucket], lengths[bucket])
            for bucket in range(3)
        ]
    )[:, None]
    upstream = (
        jnp.concatenate([piece.reshape(-1, features) for piece in cotangents], axis=0).astype(
            jnp.float32
        )
        * live_rows
    )
    normed = layer_norm(token_values, first_gain, first_shift).astype(jnp.bfloat16)
    hidden_input = product("td,hde->hte", normed, hidden_weight) + hidden_bias[:, None, :]
    hidden_input, hidden = (hidden_input, jax.nn.gelu(hidden_input).astype(jnp.bfloat16))
    values = (product("td,dc->tc", normed, value_weight) + value_bias).astype(jnp.bfloat16)
    mixing_parts = []
    log_totals = []
    for bucket in range(3):
        length = lengths[bucket]
        row_start = row_starts[bucket]
        row_count = row_counts[bucket]
        slot_count = slot_counts[bucket]
        block_hidden = hidden[:, row_start : row_start + row_count]
        scores = (
            product("hnd,hdk->hnk", block_hidden, score_weight[:, :, :length])
            + score_bias[:, None, :length]
        )
        log_total = jax.nn.logsumexp(scores, axis=-1, keepdims=True)
        attention = (
            jnp.exp(scores - log_total)
            .astype(jnp.bfloat16)
            .reshape(head_count, slot_count, length, length)
        )
        block_values = values[row_start : row_start + row_count].reshape(
            slot_count, length, head_count, head_width
        )
        mixing = product("hsqk,skhe->sqhe", attention, block_values)
        mixing_parts.append(mixing.reshape(row_count, head_count * head_width).astype(jnp.bfloat16))
        log_totals.append(log_total)
    mixing = jnp.concatenate(mixing_parts, axis=0)
    attended = pair_sum(product("tc,cd->td", mixing, output_weight)) + output_bias
    middle = token_values + attended
    second = layer_norm(middle, second_gain, second_shift).astype(jnp.bfloat16)
    expand_input = product("td,df->tf", second, expand_weight) + expand_bias
    activated = jax.nn.gelu(expand_input).astype(jnp.bfloat16)
    branch = pair_sum(product("tf,fd->td", activated, reduce_weight)) + reduce_bias
    result = live_rows * (middle + branch)
    branch_gradient = upstream.astype(jnp.bfloat16)
    reduce_bias_gradient = jnp.sum(branch_gradient.astype(jnp.float32), axis=0)
    expand_gradient = gelu_backward(
        expand_input, product("td,fd->tf", branch_gradient, reduce_weight)
    ).astype(jnp.bfloat16)
    expand_bias_gradient = jnp.sum(expand_gradient.astype(jnp.float32), axis=0)
    second_gradient = pair_sum(product("tf,df->td", expand_gradient, expand_weight))
    middle_norm, second_gain_gradient, second_shift_gradient = jax.vjp(
        layer_norm, middle, second_gain, second_shift
    )[1](second_gradient)
    middle_gradient = upstream + middle_norm
    attended_gradient = middle_gradient.astype(jnp.bfloat16)
    output_bias_gradient = jnp.sum(attended_gradient.astype(jnp.float32), axis=0)
    mixing_gradient = product("td,cd->tc", attended_gradient, output_weight).astype(jnp.bfloat16)
    score_bias_gradient = jnp.zeros(score_bias.shape, jnp.float32)
    hidden_parts = []
    score_parts = []
    value_parts = []
    for bucket in range(3):
        length = lengths[bucket]
        row_start = row_starts[bucket]
        row_count = row_counts[bucket]
        slot_count = slot_counts[bucket]
        block_hidden = hidden[:, row_start : row_start + row_count]
        block_weight = score_weight[:, :, :length]
        scores = product("hnd,hdk->hnk", block_hidden, block_weight) + score_bias[:, None, :length]
        softmax_full = jnp.exp(scores - log_totals[bucket])
        attention = softmax_full.astype(jnp.bfloat16).reshape(
            head_count, slot_count, length, length
        )
        block_values = values[row_start : row_start + row_count].reshape(
            slot_count, length, head_count, head_width
        )
        block_gradient = mixing_gradient[row_start : row_start + row_count].reshape(
            slot_count, length, head_count, head_width
        )
        attention_gradient = product("sqhe,skhe->hsqk", block_gradient, block_values).reshape(
            head_count, row_count, length
        )
        value_parts.append(
            product("hsqk,sqhe->skhe", attention, block_gradient).reshape(
                row_count, head_count * head_width
            )
        )
        score_gradient = softmax_full * (
            attention_gradient - jnp.sum(attention_gradient * softmax_full, axis=-1, keepdims=True)
        )
        score_gradient = score_gradient.astype(jnp.bfloat16)
        padding = full_length - length
        score_bias_gradient = score_bias_gradient + jnp.pad(
            jnp.sum(score_gradient.astype(jnp.float32), axis=1), ((0, 0), (0, padding))
        )
        score_parts.append(score_gradient)
        hidden_parts.append(product("hnk,hdk->hnd", score_gradient, block_weight))
    hidden_gradient = jnp.concatenate(hidden_parts, axis=1)
    value_gradient = jnp.concatenate(value_parts, axis=0).astype(jnp.bfloat16)
    value_bias_gradient = jnp.sum(value_gradient.astype(jnp.float32), axis=0)
    input_gradient_hidden = gelu_backward(hidden_input, hidden_gradient).astype(jnp.bfloat16)
    hidden_bias_gradient = jnp.sum(input_gradient_hidden.astype(jnp.float32), axis=1)
    normed_part = product("hte,hde->td", input_gradient_hidden, hidden_weight) + product(
        "tc,dc->td", value_gradient, value_weight
    )
    normed_gradient = pair_sum(normed_part)
    input_norm, first_gain_gradient, first_shift_gradient = jax.vjp(
        layer_norm, token_values, first_gain, first_shift
    )[1](normed_gradient)
    input_gradient = middle_gradient + input_norm
    operands = (
        activated, branch_gradient, expand_gradient, second,
        value_gradient, normed, mixing, attended_gradient,
        hidden, *score_parts, input_gradient_hidden,
    )
    partial_sums = (
        first_gain_gradient,
        first_shift_gradient,
        hidden_bias_gradient,
        score_bias_gradient,
        value_bias_gradient,
        output_bias_gradient,
        second_gain_gradient,
        second_shift_gradient,
        expand_bias_gradient,
        reduce_bias_gradient,
    )
    fits = lax.axis_size("dp") == 16 and lengths == [128, 256, 512] and slot_counts == [1, 1, 1]
    weight_gradients, total_sums = (grid_sums if fits else plain_sums)(operands, partial_sums)
    (
        hidden_weight_gradient,
        score_weight_gradient,
        value_weight_gradient,
        output_weight_gradient,
        expand_weight_gradient,
        reduce_weight_gradient,
    ) = weight_gradients
    (
        first_gain_gradient,
        first_shift_gradient,
        hidden_bias_gradient,
        score_bias_gradient,
        value_bias_gradient,
        output_bias_gradient,
        second_gain_gradient,
        second_shift_gradient,
        expand_bias_gradient,
        reduce_bias_gradient,
    ) = total_sums
    outputs = []
    gradients = []
    for bucket in range(3):
        row_start = row_starts[bucket]
        row_count = row_counts[bucket]
        outputs.append(
            result[row_start : row_start + row_count]
            .reshape(slot_counts[bucket], lengths[bucket], features)
            .astype(jnp.bfloat16)
        )
        gradients.append(
            input_gradient[row_start : row_start + row_count]
            .reshape(slot_counts[bucket], lengths[bucket], features)
            .astype(jnp.bfloat16)
        )
    return (
        outputs[0],
        outputs[1],
        outputs[2],
        gradients[0],
        gradients[1],
        gradients[2],
        first_gain_gradient,
        first_shift_gradient,
        hidden_weight_gradient,
        hidden_bias_gradient,
        score_weight_gradient,
        score_bias_gradient,
        value_weight_gradient,
        value_bias_gradient,
        output_weight_gradient,
        output_bias_gradient,
        second_gain_gradient,
        second_shift_gradient,
        expand_weight_gradient,
        expand_bias_gradient,
        reduce_weight_gradient,
        reduce_bias_gradient,
    )


def solution(mesh):
    placed = (
        P("dp", None, None),
        P("dp", None, None),
        P("dp", None, None),
        P("dp"),
        P("dp"),
        P("dp"),
        P(),
        P(),
        P("mp", None, None),
        P("mp", None),
        P("mp", None, None),
        P("mp", None),
        P(None, "mp"),
        P("mp"),
        P("mp", None),
        P(),
        P(),
        P(),
        P(None, "mp"),
        P("mp"),
        P("mp", None),
        P(),
        P("dp", None, None),
        P("dp", None, None),
        P("dp", None, None),
    )
    return jax.shard_map(
        body,
        mesh=mesh,
        in_specs=placed,
        out_specs=(
            P("dp", None, None),
            P("dp", None, None),
            P("dp", None, None),
            P("dp", None, None),
            P("dp", None, None),
            P("dp", None, None),
            P(),
            P(),
            P(("mp", "dp")),
            P("mp", None),
            P(("mp", "dp")),
            P("mp", None),
            P(("mp", "dp")),
            P("mp"),
            P(("mp", "dp")),
            P(),
            P(),
            P(),
            P(("mp", "dp")),
            P("mp"),
            P(("mp", "dp")),
            P(),
        ),
        check_vma=False,
    )
```

```python
import jax
import jax.numpy as jnp
from jax import lax
from jax.experimental import pallas as pl
from jax.experimental.pallas import tpu as pltpu
from jax.sharding import PartitionSpec as P

epsilon = 1e-05


def layer_norm(values, gains, offset):
    centred = values - jnp.mean(values, axis=-1, keepdims=True)
    variance = jnp.mean(centred * centred, axis=-1, keepdims=True)
    return centred * lax.rsqrt(variance + epsilon) * gains + offset


def product(form, left, right):
    return jnp.einsum(form, left, right, preferred_element_type=jnp.float32)


def gelu_backward(inputs, upstream):
    return jax.vjp(jax.nn.gelu, inputs)[1](upstream)[0]


def live_flags(count_array, slot_count, length):
    flags = (jnp.arange(slot_count) < count_array[0]).astype(jnp.float32)
    return jnp.repeat(flags, length)


BUCKETS = ((0, 128), (128, 256), (384, 512))
HEADS = 6
WIDTH = 64
ROOT = 0.7978845608028654
CUBE = 0.044715


def dot_rows(left, right):
    return lax.dot_general(
        left, right, (((0,), (0,)), ((), ())), preferred_element_type=jnp.float32
    )


def dot_last(left, right):
    return lax.dot_general(
        left, right, (((1,), (1,)), ((), ())), preferred_element_type=jnp.float32
    )


def dot_plain(left, right):
    return jnp.dot(left, right, preferred_element_type=jnp.float32)


def wide(lines):
    return jnp.concatenate([lines[at : at + 1] for at in range(lines.shape[0])], axis=1)


def normalise(rows):
    centred = rows - jnp.mean(rows, axis=-1, keepdims=True)
    scale = lax.rsqrt(jnp.mean(centred * centred, axis=-1, keepdims=True) + epsilon)
    return centred * scale, scale


def gelu_pair(inputs):
    square = inputs * inputs
    curve = jnp.tanh(inputs * (ROOT + ROOT * CUBE * square))
    half = 0.5 + 0.5 * curve
    slope = half + (0.5 * inputs) * (1.0 - curve * curve) * (ROOT + 3.0 * ROOT * CUBE * square)
    return inputs * half, slope


def attention_forward(
    tokens_a, tokens_b, tokens_c, gain, shift, hidden_weight_h, hidden_bias,
    score_weight_h, score_bias, value_weight, value_bias,
    normed, hidden_h, slope_h, full_a_h, full_b_h, full_c_h, values, mixing,
    hidden_weight, score_weight, hidden, slope, full_a, full_b, full_c, load_sems, save_sems,
):
    loads = []
    for head in range(HEADS):
        loads.append(
            (
                pltpu.make_async_copy(
                    hidden_weight_h.at[head], hidden_weight.at[head], load_sems.at[0, head]
                ),
                pltpu.make_async_copy(
                    score_weight_h.at[head], score_weight.at[head], load_sems.at[1, head]
                ),
            )
        )
    for pair in loads:
        for load in pair:
            load.start()
    for (start, length), tokens in zip(BUCKETS, (tokens_a, tokens_b, tokens_c)):
        for row in range(0, length, 128):
            unit, _ = normalise(tokens[0, row : row + 128].astype(jnp.float32))
            normed[start + row : start + row + 128] = (unit * wide(gain) + wide(shift)).astype(
                jnp.bfloat16
            )
    values[...] = (dot_plain(normed[...], value_weight[...]) + wide(value_bias)).astype(jnp.bfloat16)
    saves = []
    for head in range(HEADS):
        slot = head % 2
        if head >= 2:
            for save in saves[head - 2]:
                save.wait()
        loads[head][0].wait()
        for start, length in ((0, 384), (384, 512)):
            rows = slice(start, start + length)
            inputs = dot_plain(normed[rows], hidden_weight[head]) + hidden_bias[head : head + 1]
            gelu, steep = gelu_pair(inputs)
            hidden[slot, rows] = gelu.astype(jnp.bfloat16)
            slope[slot, rows] = steep
        loads[head][1].wait()
        columns = slice(WIDTH * head, WIDTH * head + WIDTH)
        for (start, length), full in zip(BUCKETS, (full_a, full_b, full_c)):
            rows = slice(start, start + length)
            scores = (
                dot_plain(hidden[slot, rows], score_weight[head, :, 0:length])
                + score_bias[head : head + 1, 0:length]
            )
            powers = jnp.exp(scores - jnp.max(scores, axis=-1, keepdims=True))
            softmax = powers / jnp.sum(powers, axis=-1, keepdims=True)
            full[slot] = softmax
            mixed = dot_plain(softmax.astype(jnp.bfloat16), values[rows, columns])
            mixing[rows, columns] = mixed.astype(jnp.bfloat16)
        saves.append(
            [
                pltpu.make_async_copy(source.at[slot], target.at[head], save_sems.at[number, slot])
                for number, (source, target) in enumerate(
                    (
                        (hidden, hidden_h), (slope, slope_h), (full_a, full_a_h),
                        (full_b, full_b_h), (full_c, full_c_h),
                    )
                )
            ]
        )
        for save in saves[head]:
            save.start()
    for head in (HEADS - 2, HEADS - 1):
        for save in saves[head]:
            save.wait()


def attention_forward_call(
    tokens, gain, shift, hidden_weight, hidden_bias, score_weight, score_bias, value_weight, value_bias
):
    f32, bf16 = jnp.float32, jnp.bfloat16
    rows, features = 896, 768
    far, near = pl.BlockSpec(memory_space=pl.ANY), pl.BlockSpec(memory_space=pltpu.VMEM)
    squares = [(HEADS, length, length) for _, length in BUCKETS]
    return pl.pallas_call(
        attention_forward,
        out_shape=(
            jax.ShapeDtypeStruct((rows, features), bf16),
            jax.ShapeDtypeStruct((HEADS, rows, features), bf16),
            jax.ShapeDtypeStruct((HEADS, rows, features), f32),
            *(jax.ShapeDtypeStruct(square, f32) for square in squares),
            jax.ShapeDtypeStruct((rows, HEADS * WIDTH), bf16),
            jax.ShapeDtypeStruct((rows, HEADS * WIDTH), bf16),
        ),
        in_specs=[near] * 5 + [far, near, far, near, near, near],
        out_specs=(near, far, far, far, far, far, near, near),
        scratch_shapes=[
            pltpu.VMEM(hidden_weight.shape, bf16),
            pltpu.VMEM(score_weight.shape, bf16),
            pltpu.VMEM((2, rows, features), bf16),
            pltpu.VMEM((2, rows, features), f32),
            *(pltpu.VMEM((2, *square[1:]), f32) for square in squares),
            pltpu.SemaphoreType.DMA((2, HEADS)),
            pltpu.SemaphoreType.DMA((5, 2)),
        ],
        compiler_params=pltpu.CompilerParams(vmem_limit_bytes=56 * 2**20),
        name="attention_forward",
    )(
        *tokens, gain.reshape(-1, 128), shift.reshape(-1, 128), hidden_weight, hidden_bias,
        score_weight, score_bias, value_weight, value_bias.reshape(-1, 128),
    )


SLOTS = 4
AHEAD = 6
ITEMS = 15
LAGS = 5
PARTS = 3
ROWS = 96
EDGE = 16
WIDE = 32
FIRST = EDGE + WIDE
STEPS = PARTS * ITEMS
PAIR_ROWS = 224
SMALL_ROWS = 112
FIRST_GAIN, FIRST_SHIFT, HIDDEN_BIAS, SCORE_BIAS, VALUE_BIAS = 0, 6, 12, 48, 72
OUTPUT_BIAS, SECOND_GAIN, SECOND_SHIFT, EXPAND_BIAS, REDUCE_BIAS = 75, 81, 87, 93, 105
SMALL_PLACES = (
    (FIRST_GAIN, 6), (FIRST_SHIFT, 6), (HIDDEN_BIAS, 36), (SCORE_BIAS, 24), (VALUE_BIAS, 3),
    (OUTPUT_BIAS, 6), (SECOND_GAIN, 6), (SECOND_SHIFT, 6), (EXPAND_BIAS, 12), (REDUCE_BIAS, 6),
)
BRANCH_AT, HEADS_AT, RESULT_AT, NORMED_AT, PAIR_AT, INPUT_AT, SMALL_AT = 3, 5, 9, 10, 22, 24, 32
MESH_ID = pl.DeviceIdType.MESH


def layer_kernel(
    mixing_h, normed_h, values_h, hidden_h, slope_h, full_a_h, full_b_h, full_c_h,
    tokens_a_h, tokens_b_h, tokens_c_h, branch_a_h, branch_b_h, branch_c_h,
    hidden_weight_h, score_weight_h, value_weight_h, output_weight_h, expand_weight_h,
    reduce_weight_h,
    live_a, live_b, live_c, first_gain, output_bias, second_gain, second_shift, expand_bias,
    reduce_bias,
    result_a, result_b, result_c, gradient_a, gradient_b, gradient_c,
    out_hidden, out_score, out_value, out_output, out_expand, out_reduce, *rest,
):
    small_out, rest = rest[:10], rest[10:]
    middle_h, branch_own_h, branch_far_h, rest = rest[0], rest[1], rest[2], rest[3:]
    (
        arena, branch, second, attended, tokens, flipped, mixing, values, mixed, value,
        output_weight, value_weight, score_weight, slope, full_a, full_b, full_c,
        score_a, score_b, score_c, hidden, residual, pair_out, pair_in, stage, pieces, finished,
        own, first_x, first_y, next_x, next_y, middle, middle_up, middle_down,
        edge, edge_up, edge_down, last_x, last_y, done,
        small, small_x, small_sum, small_y, small_z,
        load_sems, head_sems, hidden_sems, weight_sems, pair_sems, far_sems, near_sems, piece_sems,
        finished_sems, first_sems, next_sems, middle_sems, edge_sems, last_sems, small_sems,
        pair_free,
    ) = rest
    f32, bf16 = jnp.float32, jnp.bfloat16
    spot = lax.axis_index("dp")
    x, y, z = spot % 2, (spot // 2) % 2, spot // 4
    to_x = {"dp": spot + 1 - 2 * x}
    to_y = {"dp": spot + 2 - 4 * y}
    to_up = {"dp": spot + 4}
    to_down = {"dp": spot - 4}
    to_mate = {"mp": 1 - lax.axis_index("mp")}

    loads = []
    for number, (source, target) in enumerate(
        (
            (mixing_h, mixing), (output_weight_h, output_weight),
            (tokens_a_h.at[0], tokens.at[0:128]), (tokens_b_h.at[0], tokens.at[128:384]),
            (tokens_c_h.at[0], tokens.at[384:896]),
            (expand_weight_h.at[:, 0:768], arena.at[4, 0:768]),
            (expand_weight_h.at[:, 768:1536], arena.at[5, 0:768]),
            (branch_a_h.at[0], branch.at[0:128]), (branch_b_h.at[0], branch.at[128:384]),
            (branch_c_h.at[0], branch.at[384:896]),
            (reduce_weight_h.at[0:768], arena.at[2, 0:768]),
            (reduce_weight_h.at[768:1536], arena.at[3, 0:768]),
            (values_h, values), (value_weight_h, value_weight),
        )
    ):
        loads.append(pltpu.make_async_copy(source, target, load_sems.at[number]))
    normed_load = pltpu.make_async_copy(normed_h, second, load_sems.at[14])
    middle_save = pltpu.make_async_copy(residual, middle_h, load_sems.at[15])

    def head_loads(head, group, side):
        if group == 0:
            pairs = (
                (slope_h.at[head, 0:384], slope.at[0:384]), (full_a_h.at[head], full_a),
                (full_b_h.at[head], full_b),
            )
        elif group == 1:
            pairs = ((slope_h.at[head, 384:896], slope.at[384:896]), (full_c_h.at[head], full_c))
        else:
            pairs = ((score_weight_h.at[head], score_weight.at[side]),)
        return [
            pltpu.make_async_copy(source, target, head_sems.at[group + side * (group // 2), at])
            for at, (source, target) in enumerate(pairs)
        ]

    def hidden_load(turn):
        slot = turn % 2
        return pltpu.make_async_copy(
            hidden_h.at[turn % HEADS], hidden.at[slot], hidden_sems.at[slot]
        )

    def weight_load(head):
        slot = head % 2
        return pltpu.make_async_copy(
            hidden_weight_h.at[head], arena.at[6 + slot, 0:768], weight_sems.at[slot]
        )

    for load in loads:
        load.start()
    for group in range(3):
        for load in head_loads(0, group, 0):
            load.start()
    for load in head_loads(1, 2, 1):
        load.start()
    for number in (0, 1):
        hidden_load(number).start()

    barrier = pltpu.get_barrier_semaphore()
    for device in (to_x, to_y, to_mate):
        pl.semaphore_signal(barrier, inc=1, device_id=device, device_id_type=MESH_ID)

    @pl.when(z < 3)
    def _():
        pl.semaphore_signal(barrier, inc=1, device_id=to_up, device_id_type=MESH_ID)

    @pl.when(z > 0)
    def _():
        pl.semaphore_signal(barrier, inc=1, device_id=to_down, device_id_type=MESH_ID)

    inner = (z > 0) & (z < 3)

    @pl.when(inner)
    def _():
        pl.semaphore_wait(barrier, 5)

    @pl.when(jnp.logical_not(inner))
    def _():
        pl.semaphore_wait(barrier, 4)

    def remote(source, target, sems, slot, device):
        return pltpu.make_async_remote_copy(
            src_ref=source,
            dst_ref=target,
            send_sem=sems.at[0, slot],
            recv_sem=sems.at[1, slot],
            device_id=device,
            device_id_type=MESH_ID,
        )

    def span(at, rows):
        return pl.ds(pl.multiple_of(at * rows, 16), rows)

    def repeat(first, last, body):
        def turn(at, carry):
            body(at)
            return carry

        lax.fori_loop(first, last, turn, 0)

    def pair_copy(at):
        rows = span(at, PAIR_ROWS)
        return remote(pair_out.at[rows], pair_in.at[rows], pair_sems, at, to_mate)

    def pair_ready(chunk):
        for at in range(4):

            @pl.when(chunk == (0, 1, 3, 5)[at])
            def _():
                pair_copy(at).wait_recv()

    def pair_done(spare):
        repeat(0, 4, lambda at: pair_copy(at).wait_send())
        if spare:
            pl.semaphore_signal(pair_free, inc=1, device_id=to_mate, device_id_type=MESH_ID)

    def live_of(chunk):
        count = jnp.where(chunk == 0, live_a[0], jnp.where(chunk < 3, live_b[0], live_c[0]))
        return jnp.where(count > 0, 1.0, 0.0).astype(f32)

    def add_line(row, line):
        for tile in range(line.shape[1] // 128):
            small[pl.ds(row + tile, 1)] += line[:, 128 * tile : 128 * tile + 128]

    def column_sum(block):
        return jnp.sum(block.astype(f32), axis=0, keepdims=True)

    def put(slot, dest, row, block):
        z_at, y_at, x_at = dest // 4, (dest // 2) % 2, dest % 2
        rows = block.shape[0]
        own[slot, row // ROWS, z_at, y_at, x_at, row % ROWS : row % ROWS + rows, :] = block

    def produce(item, third):
        slot = item % 3

        def feed_forward(left, right, column):
            column = pl.multiple_of(column, 128)

            def part(half):
                block = dot_rows(arena[left + half], right[:, pl.ds(column, 128)])
                for at in range(8):
                    own[slot, third, 2 * half + at // 4, at // 2 % 2, at % 2] = block[
                        96 * at : 96 * at + 96
                    ]

            repeat(0, 2, part)

        @pl.when(item < 2)
        def _():
            feed_forward(0, branch, 384 * item + 128 * third)

        @pl.when((item >= 2) & (item < 4))
        def _():
            feed_forward(6, second, 384 * (item - 2) + 128 * third)

        def heads(block_of):
            def part(head):
                block = block_of(head)
                for piece in range(8):
                    unit = 8 * head + piece
                    own[slot, unit % 3, unit // 12, unit // 6 % 2, unit // 3 % 2] = block[
                        96 * piece : 96 * piece + 96
                    ]

            repeat(2 * third, 2 * third + 2, part)

        def score_heads(block_of):
            def part(head):
                turn = HEADS * (item - 4) + head
                hidden_load(turn).wait()
                return block_of(head, hidden.at[turn % 2])

            heads(part)

            for turn in (0, 1):
                after = HEADS * (item - 4) + 2 * third + 2 + turn

                @pl.when(after < 4 * HEADS)
                def _():
                    hidden_load(after).start()

        @pl.when(item == 4)
        def _():
            score_heads(
                lambda head, rows: dot_rows(rows[0:128], score_a[head])
                + dot_rows(rows[128:384], score_b[head, :, 0:128])
                + dot_rows(rows[384:896], score_c[head, :, 0:128])
            )

        @pl.when(item == 5)
        def _():
            score_heads(
                lambda head, rows: dot_rows(rows[128:384], score_b[head, :, 128:256])
                + dot_rows(rows[384:896], score_c[head, :, 128:256])
            )

        @pl.when((item == 6) | (item == 7))
        def _():
            column = pl.multiple_of(128 * (item - 4), 128)
            score_heads(
                lambda head, rows: dot_rows(rows[384:896], score_c[head, :, pl.ds(column, 128)])
            )

        @pl.when((item == 8) & (third == 0))
        def _():
            normed_load.wait()
            flipped[...] = second[...].T

        @pl.when((item >= 8) & (item < 14))
        def _():
            column = pl.multiple_of(128 * (item - 8), 128)
            heads(lambda head: dot_plain(flipped[...], arena[head, :, pl.ds(column, 128)]))

        for part, (left, right) in enumerate(((value, second), (mixing, attended))):

            @pl.when((item == 14) & (third == part))
            def _():
                block = dot_rows(left[...], right[...])
                for dest in range(16):
                    for piece in range(6):
                        put(
                            slot, dest, 144 * part + 24 * piece,
                            block[24 * dest : 24 * dest + 24, 128 * piece : 128 * piece + 128],
                        )

    def deliver(item):
        def spread(target, tiles, first):
            for part in range(PARTS):
                target[pl.ds(first + tiles * ROWS * part, ROWS, stride=tiles), :] = done[part]

        def stack(target, first):
            for part in range(PARTS):
                target[pl.ds(first + part, ROWS, stride=6), :] = done[part]

        @pl.when(item < 2)
        def _():
            stack(out_reduce, 3 * item)

        @pl.when((item >= 2) & (item < 4))
        def _():
            stack(out_expand, 3 * (item - 2))

        @pl.when((item >= 4) & (item < 8))
        def _():
            spread(out_score, 4, item - 4)

        @pl.when((item >= 8) & (item < 14))
        def _():
            spread(out_hidden, 6, item - 8)

        @pl.when(item == 14)
        def _():
            for start, target in ((0, out_value), (144, out_output)):
                for piece in range(6):
                    row = start + 24 * piece
                    target[pl.ds(piece, 24, stride=6), :] = done[
                        row // ROWS, row % ROWS : row % ROWS + 24
                    ]

    def home(i):
        return own.at[(i // PARTS) % 3, i % PARTS], i % SLOTS

    def first_copies(i):
        held, slot = home(i)[0], i % AHEAD
        return (
            remote(held.at[:, :, 1 - x, 0:FIRST], first_x.at[slot], first_sems.at[0], slot, to_x),
            remote(held.at[:, 1 - y, :, FIRST:ROWS], first_y.at[slot], first_sems.at[1], slot, to_y),
        )

    def next_copies(i):
        held, slot = home(i)
        return (
            remote(held.at[:, y, 1 - x, FIRST : FIRST + EDGE], next_x.at[slot], next_sems.at[0], slot, to_x),
            remote(held.at[:, 1 - y, x, 0:EDGE], next_y.at[slot], next_sems.at[1], slot, to_y),
        )

    def last_copies(i):
        slot = i % SLOTS
        return (
            remote(middle.at[slot, z, 3 - x], last_x.at[slot], last_sems.at[0], slot, to_x),
            remote(middle.at[slot, z, 1 - y], last_y.at[slot], last_sems.at[1], slot, to_y),
        )

    def line_up(kept, landing, sems, slot, place):
        return remote(kept.at[slot, place + 1 : 4], landing.at[slot, place:3], sems.at[0], slot, to_up)

    def line_down(kept, landing, sems, slot, place):
        return remote(kept.at[slot, 0:place], landing.at[slot, 0:place], sems.at[1], slot, to_down)

    def line_hop(kept, landing_up, landing_down, sems, i, hop):
        slot = i % SLOTS
        for place in range(4):
            if place == hop:

                @pl.when(z == place)
                def _():
                    if place > 0:
                        line_up(kept, landing_up, sems, slot, place - 1).wait_recv()
                        kept[slot, place:4] += landing_up[slot, place - 1 : 3]
                    if place < 3:
                        line_up(kept, landing_up, sems, slot, place).start()

            if 3 - place == hop:

                @pl.when(z == place)
                def _():
                    if place < 3:
                        line_down(kept, landing_down, sems, slot, place + 1).wait_recv()
                        kept[slot, 0 : place + 1] += landing_down[slot, 0 : place + 1]
                    if place > 0:
                        line_down(kept, landing_down, sems, slot, place).start()

    def line_sent(kept, landing_up, landing_down, sems, i):
        slot = i % SLOTS
        for place in range(4):

            @pl.when(z == place)
            def _():
                if place < 3:
                    line_up(kept, landing_up, sems, slot, place).wait_send()
                if place > 0:
                    line_down(kept, landing_down, sems, slot, place).wait_send()

    middle_line = (middle, middle_up, middle_down, middle_sems)
    edge_line = (edge, edge_up, edge_down, edge_sems)

    def small_steps(t):
        def copy(number, source, target, device):
            return pltpu.make_async_remote_copy(
                src_ref=source, dst_ref=target, send_sem=small_sems.at[0, number],
                recv_sem=small_sems.at[1, number], device_id=device, device_id_type=MESH_ID,
            )

        over_x = copy(0, small, small_x, to_x)
        over_y = copy(1, small_sum, small_y, to_y)

        def up(place):
            part = small_z.at[0 : place + 1]
            return copy(2, part, part, to_up)

        def down(place):
            part = small_z.at[place:4]
            return copy(3, part, part, to_down)

        @pl.when(t == 0)
        def _():
            over_x.start()

        @pl.when(t == 1)
        def _():
            over_x.wait()
            small_sum[...] = small[...] + small_x[...]
            over_y.start()

        @pl.when(t == 2)
        def _():
            over_y.wait()
            small_z[z] = small_sum[...] + small_y[...]

        for place in range(4):

            @pl.when((z == place) & (t == 2 + place))
            def _():
                if place > 0:
                    up(place - 1).wait_recv()
                if place < 3:
                    up(place).start()

            @pl.when((z == place) & (t == 5 - place))
            def _():
                if place < 3:
                    down(place + 1).wait_recv()
                if place > 0:
                    down(place).start()

        @pl.when(t == 6)
        def _():
            small_sum[...] = ((small_z[0] + small_z[1]) + small_z[2]) + small_z[3]
            for (row, rows), target in zip(SMALL_PLACES, small_out):
                columns = target.shape[1] // 128
                for at in range(rows):
                    line, tile = at // columns, at % columns
                    target[line : line + 1, 128 * tile : 128 * tile + 128] = small_sum[
                        row + at : row + at + 1
                    ]
            for place in range(4):

                @pl.when(z == place)
                def _():
                    if place < 3:
                        up(place).wait_send()
                    if place > 0:
                        down(place).wait_send()

    def expand_of(quarter, rows):
        column = pl.multiple_of(quarter % 2 * 384, 128)
        bias = [expand_bias[pl.ds(3 * quarter + at, 1)] for at in range(3)]
        return dot_plain(
            second[rows], arena[4 + quarter // 2, 0:768, pl.ds(column, 384)]
        ) + jnp.concatenate(bias, axis=1)

    def activate(turn):
        quarter, rows = turn // 2, span(turn % 2, 448)
        gelu, _ = gelu_pair(expand_of(quarter, rows))
        column = pl.multiple_of(quarter % 2 * 384, 128)
        arena[quarter // 2, rows, pl.ds(column, 384)] = gelu.astype(bf16)

    def expand_gradient(turn):
        quarter, rows = turn // 2, span(turn % 2, 448)
        column = pl.multiple_of(quarter % 2 * 384, 128)
        _, steep = gelu_pair(expand_of(quarter, rows))
        spread = dot_last(branch[rows], arena[2 + quarter // 2, pl.ds(column, 384)])
        grown = (steep * spread).astype(bf16)
        arena[6 + quarter // 2, rows, pl.ds(column, 384)] = grown
        add_line(EXPAND_BIAS + 3 * quarter, column_sum(grown))

    def second_gradient(at):
        rows = span(at, PAIR_ROWS)
        pair_out[rows] = dot_last(arena[6, rows], arena[4, 0:768]) + dot_last(
            arena[7, rows], arena[5, 0:768]
        )
        pair_copy(at).start()

    def branch_away(at):
        return remote(
            stage.at[at % 2], branch_far_h.at[span(at, PAIR_ROWS)], far_sems, at, to_mate
        )

    def branch_save(at):
        return pltpu.make_async_copy(
            stage.at[at % 2], branch_own_h.at[span(at, PAIR_ROWS)], near_sems.at[at]
        )

    def branch_sent(at):
        branch_away(at).wait_send()
        branch_save(at).wait()

    def branch_part(at):
        rows = span(at, PAIR_ROWS)

        @pl.when(at >= 2)
        def _():
            branch_sent(at - 2)

        stage[at % 2] = dot_plain(arena[0, rows], arena[2, 0:768]) + dot_plain(
            arena[1, rows], arena[3, 0:768]
        )
        branch_away(at).start()
        branch_save(at).start()

    def middle_gradient(chunk):
        rows = span(chunk, 128)
        pair_ready(chunk)
        total = pair_out[rows] + pair_in[rows]
        unit, scale = normalise(residual[rows])
        add_line(SECOND_GAIN, column_sum(total * unit))
        add_line(SECOND_SHIFT, column_sum(total))
        scaled = total * wide(second_gain)
        mean = jnp.mean(scaled, axis=-1, keepdims=True)
        inner = jnp.mean(scaled * unit, axis=-1, keepdims=True)
        result = branch[rows].astype(f32) + (scaled - mean - unit * inner) * scale
        residual[rows] = result
        rounded = result.astype(bf16)
        attended[rows] = rounded
        add_line(OUTPUT_BIAS, column_sum(rounded))

    def head_gradients(turn):
        both = pl.ds(pl.multiple_of(128 * turn, 128), 128)
        kept = [[], [], []]
        for side in range(2):
            head = 2 * turn + side
            columns = slice(WIDTH * side, WIDTH * side + WIDTH)
            for load in head_loads(head, 2, side):
                load.wait()
            for bucket, ((start, length), full, score) in enumerate(
                zip(BUCKETS, (full_a, full_b, full_c), (score_a, score_b, score_c))
            ):
                if bucket != 1:
                    for load in head_loads(head, bucket // 2, side):
                        load.wait()
                rows = slice(start, start + length)
                softmax = full[...]
                upstream = mixed[rows, both][:, columns]
                attention_gradient = dot_last(upstream, values[rows, both][:, columns])
                kept[bucket].append(dot_rows(softmax.astype(bf16), upstream).astype(bf16))
                inner = jnp.sum(attention_gradient * softmax, axis=-1, keepdims=True)
                gradient = (softmax * (attention_gradient - inner)).astype(bf16)
                score[head] = gradient
                add_line(SCORE_BIAS + 4 * head, column_sum(gradient))
                spread = dot_last(gradient, score_weight[side, :, 0:length])
                grown = (slope[rows] * spread).astype(bf16)
                arena[head, rows] = grown
                add_line(HIDDEN_BIAS + 6 * head, column_sum(grown))
                if bucket > 0:

                    @pl.when(head + 1 < HEADS)
                    def _():
                        for load in head_loads(head + 1, bucket - 1, side):
                            load.start()

            @pl.when(head + 2 < HEADS)
            def _():
                for load in head_loads(head + 2, 2, side):
                    load.start()

        for (start, length), pair in zip(BUCKETS, kept):
            value[start : start + length, both] = jnp.concatenate(pair, axis=1)

    def piece_loads(chunk):
        rows = span(chunk, 128)
        return [
            pltpu.make_async_copy(source.at[rows], pieces.at[at], piece_sems.at[at])
            for at, source in enumerate((middle_h, branch_own_h, branch_far_h))
        ]

    def finish(chunk, block, targets):
        def copy(number):
            bucket = (0, 1, 1, 2, 2, 2, 2)[number]
            row = 128 * (number - (0, 1, 3)[bucket])
            return pltpu.make_async_copy(
                finished.at[number % 2], targets[bucket].at[0, row : row + 128],
                finished_sems.at[number % 2],
            )

        for number in range(2, 7):

            @pl.when(chunk == number)
            def _():
                copy(number - 2).wait()

        finished[chunk % 2] = block.astype(bf16)
        for number in range(7):

            @pl.when(chunk == number)
            def _():
                copy(number).start()
                if number == 6:
                    copy(5).wait()
                    copy(6).wait()

    def result_rows(chunk):
        for load in piece_loads(chunk):
            load.wait()
        total = live_of(chunk) * (pieces[0] + ((pieces[1] + pieces[2]) + wide(reduce_bias)))
        finish(chunk, total, (result_a, result_b, result_c))

        @pl.when(chunk < 6)
        def _():
            for load in piece_loads(chunk + 1):
                load.start()

    def normed_gradient(head):
        weight_load(head).wait()

        def part(half):
            rows = span(half, 448)
            block = dot_last(arena[head, rows], arena[6 + head % 2, 0:768])
            pair_out[rows] = jnp.where(head == 0, 0.0, pair_out[rows]) + block

        repeat(0, 2, part)

        @pl.when(head + 2 < HEADS)
        def _():
            weight_load(head + 2).start()

    def input_gradient(chunk):
        rows = span(chunk, 128)
        pair_ready(chunk)
        total = pair_out[rows] + pair_in[rows]
        unit, scale = normalise(tokens[rows].astype(f32))
        add_line(FIRST_GAIN, column_sum(total * unit))
        add_line(FIRST_SHIFT, column_sum(total))
        scaled = total * wide(first_gain)
        mean = jnp.mean(scaled, axis=-1, keepdims=True)
        inner = jnp.mean(scaled * unit, axis=-1, keepdims=True)
        result = residual[rows] + (scaled - mean - unit * inner) * scale
        finish(chunk, result, (gradient_a, gradient_b, gradient_c))

    def layer_steps(t):
        def between(first, count):
            return (t >= first) & (t < first + count)

        @pl.when(t == 0)
        def _():
            loads[10].wait()
            loads[11].wait()

        @pl.when(between(0, 2))
        def _():
            repeat(4 * t, 4 * t + 4, expand_gradient)

        @pl.when(t == 2)
        def _():
            pl.semaphore_wait(pair_free, 1)
            repeat(0, 4, second_gradient)

        @pl.when(t == BRANCH_AT)
        def _():
            repeat(0, 4, branch_part)
            middle_save.wait()

        @pl.when(between(BRANCH_AT, 2))
        def _():
            late = t - BRANCH_AT
            repeat(3 * late, 3 + 4 * late, middle_gradient)

        @pl.when(t == BRANCH_AT + 1)
        def _():
            pair_done(True)
            mixed[...] = dot_last(attended[...], output_weight[...]).astype(bf16)
            repeat(2, 4, branch_sent)
            loads[12].wait()

        @pl.when(between(HEADS_AT, 3))
        def _():
            head_gradients(t - HEADS_AT)

        @pl.when(t == HEADS_AT + 3)
        def _():
            add_line(VALUE_BIAS, column_sum(value[...]))

        @pl.when(t == RESULT_AT - 1)
        def _():
            normed_load.start()
            weight_load(0).start()
            weight_load(1).start()
            repeat(0, 4, lambda at: branch_away(at).wait_recv())
            for load in piece_loads(0):
                load.start()

        @pl.when(between(RESULT_AT, 7))
        def _():
            result_rows(t - RESULT_AT)

        @pl.when(between(NORMED_AT, 12) & ((t - NORMED_AT) % 2 == 0))
        def _():
            normed_gradient((t - NORMED_AT) // 2)

        @pl.when(t == PAIR_AT)
        def _():
            loads[13].wait()
            pair_out[...] += dot_last(value[...], value_weight[...])
            pl.semaphore_wait(pair_free, 1)
            repeat(0, 4, lambda at: pair_copy(at).start())

        @pl.when(between(INPUT_AT, 7))
        def _():
            input_gradient(t - INPUT_AT)

        @pl.when(t == INPUT_AT + 7)
        def _():
            pair_done(False)

    small[...] = jnp.zeros_like(small)
    loads[0].wait()
    loads[1].wait()

    def attend(at):
        rows = span(at, PAIR_ROWS)
        pair_out[rows] = dot_plain(mixing[rows], output_weight[...])
        pair_copy(at).start()

    repeat(0, 4, attend)
    for number in range(2, 5):
        loads[number].wait()
    for number in range(7, 10):
        loads[number].wait()

    def mask(chunk):
        rows = span(chunk, 128)
        upstream = (live_of(chunk) * branch[rows].astype(f32)).astype(bf16)
        branch[rows] = upstream
        add_line(REDUCE_BIAS, column_sum(upstream))

    def second_norm(chunk):
        rows = span(chunk, 128)
        pair_ready(chunk)
        total = tokens[rows].astype(f32) + ((pair_out[rows] + pair_in[rows]) + wide(output_bias))
        residual[rows] = total
        unit, _ = normalise(total)
        second[rows] = (unit * wide(second_gain) + wide(second_shift)).astype(bf16)

    repeat(0, 7, mask)
    repeat(0, 7, second_norm)
    pair_done(True)
    middle_save.start()
    loads[5].wait()
    loads[6].wait()
    repeat(0, 8, activate)

    def step(turn, carry):
        t = turn - 4

        def at_lag(lag):
            i = t - lag
            return i, (i >= 0) & (i < STEPS)

        @pl.when((turn >= 3) & (turn < STEPS + 3))
        def _():
            for copy in first_copies(turn - 3):
                copy.start()

        small_steps(t - SMALL_AT)

        i, alive = at_lag(5)

        @pl.when(alive)
        def _():
            slot = i % SLOTS
            for copy in last_copies(i):
                copy.wait()
            line_hop(*edge_line, i, 3)
            line_sent(*middle_line, i)
            line_sent(*edge_line, i)
            part = done.at[i % PARTS]
            part[0:EDGE] = edge[slot, z, 0]
            part[EDGE:FIRST] = middle[slot, z, y] + last_y[slot]
            part[FIRST : FIRST + EDGE] = edge[slot, z, 1]
            part[FIRST + EDGE : ROWS] = middle[slot, z, 2 + x] + last_x[slot]

            @pl.when(i % PARTS == PARTS - 1)
            def _():
                deliver(i // PARTS)

        i, alive = at_lag(4)

        @pl.when(alive)
        def _():
            line_hop(*middle_line, i, 3)
            for copy in last_copies(i):
                copy.start()
            line_hop(*edge_line, i, 2)

        i, alive = at_lag(3)

        @pl.when(alive)
        def _():
            line_hop(*middle_line, i, 2)
            line_hop(*edge_line, i, 1)

        i, alive = at_lag(2)

        @pl.when(alive)
        def _():
            held, slot = home(i)
            line_hop(*middle_line, i, 1)
            for copy in next_copies(i):
                copy.wait()
            edge[slot, :, 0] = held[:, y, x, 0:EDGE] + next_y[slot]
            edge[slot, :, 1] = held[:, y, x, FIRST : FIRST + EDGE] + next_x[slot]
            line_hop(*edge_line, i, 0)

        i, alive = at_lag(1)

        @pl.when(alive)
        def _():
            held, slot = home(i)
            came = i % AHEAD
            for copy in first_copies(i):
                copy.wait()
            middle[slot, :, 0:2] = held[:, :, x, EDGE:FIRST] + first_x[came, :, :, EDGE:FIRST]
            middle[slot, :, 2:4] = (
                held[:, y, :, FIRST + EDGE : ROWS] + first_y[came, :, :, EDGE:FIRST]
            )
            line_hop(*middle_line, i, 0)
            held[:, :, x, 0:EDGE] += first_x[came, :, :, 0:EDGE]
            held[:, y, :, FIRST : FIRST + EDGE] += first_y[came, :, :, 0:EDGE]
            for copy in next_copies(i):
                copy.start()

        item, third = turn // PARTS, turn % PARTS

        @pl.when(item < ITEMS)
        def _():
            produce(item, third)

        layer_steps(t)
        return carry

    lax.fori_loop(0, STEPS + LAGS + 4, step, 0)


def layer_call(kept, pieces, cotangents, weights, lives, vectors):
    f32, bf16 = jnp.float32, jnp.bfloat16
    rows, features = 896, 768
    far, near = pl.BlockSpec(memory_space=pl.ANY), pl.BlockSpec(memory_space=pltpu.VMEM)
    scalar = pl.BlockSpec(memory_space=pltpu.SMEM)
    narrow = HEADS * WIDTH
    pair, signal = pltpu.SemaphoreType.DMA((2, 2, SLOTS)), pltpu.SemaphoreType.DMA
    block = pltpu.VMEM((rows, features), bf16)
    slim = pltpu.VMEM((rows, narrow), bf16)
    tall = pltpu.VMEM((rows, features), f32)
    squares = [length for _, length in BUCKETS]
    scratch = [
        pltpu.VMEM((8, rows, features), bf16),
        block, block, block, block,
        pltpu.VMEM((features, rows), bf16),
        slim, slim, slim, slim,
        pltpu.VMEM((narrow, features), bf16),
        pltpu.VMEM((features, narrow), bf16),
        pltpu.VMEM((2, features, 512), bf16),
        tall,
        *(pltpu.VMEM((length, length), f32) for length in squares),
        *(pltpu.VMEM((HEADS, length, length), bf16) for length in squares),
        pltpu.VMEM((2, rows, features), bf16),
        tall, tall, tall,
        pltpu.VMEM((2, PAIR_ROWS, features), f32),
        pltpu.VMEM((3, 128, features), f32),
        pltpu.VMEM((2, 128, features), bf16),
        pltpu.VMEM((3, PARTS, 4, 2, 2, ROWS, 128), f32),
        pltpu.VMEM((AHEAD, 4, 2, FIRST, 128), f32),
        pltpu.VMEM((AHEAD, 4, 2, FIRST, 128), f32),
        pltpu.VMEM((SLOTS, 4, EDGE, 128), f32),
        pltpu.VMEM((SLOTS, 4, EDGE, 128), f32),
        pltpu.VMEM((SLOTS, 4, 4, WIDE, 128), f32),
        pltpu.VMEM((SLOTS, 3, 4, WIDE, 128), f32),
        pltpu.VMEM((SLOTS, 3, 4, WIDE, 128), f32),
        pltpu.VMEM((SLOTS, 4, 2, EDGE, 128), f32),
        pltpu.VMEM((SLOTS, 3, 2, EDGE, 128), f32),
        pltpu.VMEM((SLOTS, 3, 2, EDGE, 128), f32),
        pltpu.VMEM((SLOTS, WIDE, 128), f32),
        pltpu.VMEM((SLOTS, WIDE, 128), f32),
        pltpu.VMEM((PARTS, ROWS, 128), f32),
        *([pltpu.VMEM((SMALL_ROWS, 128), f32)] * 4),
        pltpu.VMEM((4, SMALL_ROWS, 128), f32),
        signal((16,)), signal((4, 3)), signal((2,)), signal((2,)), signal((2, 4)), signal((2, 4)),
        signal((4,)), signal((3,)), signal((2,)),
        pltpu.SemaphoreType.DMA((2, 2, AHEAD)), pair, pair, pair, pair,
        signal((2, 4)),
        pltpu.SemaphoreType.REGULAR,
    ]
    results = [jax.ShapeDtypeStruct(member.shape, bf16) for member in pieces] * 2
    shares = [jax.ShapeDtypeStruct((lines, 128), f32) for lines in (1728, 1152, 144, 144, 576, 576)]
    sums = [
        jax.ShapeDtypeStruct(member, f32)
        for member in (
            (6, 128), (6, 128), (HEADS, features), (HEADS, 512), (3, 128),
            (6, 128), (6, 128), (6, 128), (12, 128), (6, 128),
        )
    ]
    spare = [jax.ShapeDtypeStruct((rows, features), f32)] * 3
    outs = pl.pallas_call(
        layer_kernel,
        out_shape=(*results, *shares, *sums, *spare),
        in_specs=[far] * 20 + [scalar] * 3 + [near] * 6,
        out_specs=(far,) * 6 + (near,) * 16 + (far,) * 3,
        scratch_shapes=scratch,
        compiler_params=pltpu.CompilerParams(
            collective_id=1, has_side_effects=True, vmem_limit_bytes=63 * 2**20
        ),
        name="layer_and_gradient_scatter",
    )(*kept, *pieces, *cotangents, *weights, *lives, *vectors)
    return outs[:22]


def copy_kernel(*refs):
    count = (len(refs) - 1) // 3
    sources, targets, rooms, sems = refs[:count], refs[count:2*count], refs[2*count:-1], refs[-1]
    loads = [
        pltpu.make_async_copy(source, room, sems.at[0, at])
        for at, (source, room) in enumerate(zip(sources, rooms))
    ]
    saves = [
        pltpu.make_async_copy(room, target, sems.at[1, at])
        for at, (room, target) in enumerate(zip(rooms, targets))
    ]
    for load in loads:
        load.start()
    for load, save in zip(loads, saves):
        load.wait()
        save.start()
    for save in saves:
        save.wait()


def copy_call(members):
    far = pl.BlockSpec(memory_space=pl.ANY)
    return pl.pallas_call(
        copy_kernel,
        out_shape=tuple(jax.ShapeDtypeStruct(member.shape, member.dtype) for member in members),
        in_specs=[far] * len(members),
        out_specs=(far,) * len(members),
        scratch_shapes=[
            *(pltpu.VMEM(member.shape, member.dtype) for member in members),
            pltpu.SemaphoreType.DMA((2, len(members))),
        ],
        name="copy_out",
    )(*members)


def lines(vector):
    return vector.reshape(-1, 128)


def grid_body(
    tokens_short,
    tokens_middle,
    tokens_long,
    live_short,
    live_middle,
    live_long,
    first_gain,
    first_shift,
    hidden_weight,
    hidden_bias,
    score_weight,
    score_bias,
    value_weight,
    value_bias,
    output_weight,
    output_bias,
    second_gain,
    second_shift,
    expand_weight,
    expand_bias,
    reduce_weight,
    reduce_bias,
    cotangent_short,
    cotangent_middle,
    cotangent_long,
):
    pieces = (tokens_short, tokens_middle, tokens_long)
    normed, hidden, slope, full_a, full_b, full_c, values, mixing = attention_forward_call(
        pieces, first_gain, first_shift, hidden_weight, hidden_bias, score_weight, score_bias,
        value_weight, value_bias,
    )
    outs = layer_call(
        (mixing, normed, values, hidden, slope, full_a, full_b, full_c),
        pieces,
        (cotangent_short, cotangent_middle, cotangent_long),
        (hidden_weight, score_weight, value_weight, output_weight, expand_weight, reduce_weight),
        (live_short, live_middle, live_long),
        (
            lines(first_gain), lines(output_bias), lines(second_gain), lines(second_shift),
            lines(expand_bias), lines(reduce_bias),
        ),
    )
    outs = copy_call(outs)
    hidden_share, score_share, value_share, output_share, expand_share, reduce_share = (
        member.reshape(-1) for member in outs[6:12]
    )
    sums = [
        member if member.shape[1] > 128 else member.reshape(-1) for member in outs[12:]
    ]
    return (
        *outs[:6],
        sums[0],
        sums[1],
        hidden_share,
        sums[2],
        score_share,
        sums[3],
        value_share,
        sums[4],
        output_share,
        *sums[5:8],
        expand_share,
        sums[8],
        reduce_share,
        sums[9],
    )


def plain_body(
    tokens_short,
    tokens_middle,
    tokens_long,
    live_short,
    live_middle,
    live_long,
    first_gain,
    first_shift,
    hidden_weight,
    hidden_bias,
    score_weight,
    score_bias,
    value_weight,
    value_bias,
    output_weight,
    output_bias,
    second_gain,
    second_shift,
    expand_weight,
    expand_bias,
    reduce_weight,
    reduce_bias,
    cotangent_short,
    cotangent_middle,
    cotangent_long,
):
    pieces = (tokens_short, tokens_middle, tokens_long)
    cotangents = (cotangent_short, cotangent_middle, cotangent_long)
    live_counts = (live_short, live_middle, live_long)
    features = tokens_short.shape[2]
    head_count = hidden_weight.shape[0]
    head_width = value_weight.shape[1] // head_count
    full_length = score_weight.shape[2]
    lengths = [piece.shape[1] for piece in pieces]
    slot_counts = [piece.shape[0] for piece in pieces]
    row_counts = [slot_counts[bucket] * lengths[bucket] for bucket in range(3)]
    row_starts = [0, row_counts[0], row_counts[0] + row_counts[1]]
    tokens = jnp.concatenate([piece.reshape(-1, features) for piece in pieces], axis=0)
    token_values = tokens.astype(jnp.float32)
    live_rows = jnp.concatenate(
        [
            live_flags(live_counts[bucket], slot_counts[bucket], lengths[bucket])
            for bucket in range(3)
        ]
    )[:, None]
    upstream = (
        jnp.concatenate([piece.reshape(-1, features) for piece in cotangents], axis=0).astype(
            jnp.float32
        )
        * live_rows
    )
    normed = layer_norm(token_values, first_gain, first_shift).astype(jnp.bfloat16)
    hidden_input = product("td,hde->hte", normed, hidden_weight) + hidden_bias[:, None, :]
    hidden_input, hidden = (hidden_input, jax.nn.gelu(hidden_input).astype(jnp.bfloat16))
    values = (product("td,dc->tc", normed, value_weight) + value_bias).astype(jnp.bfloat16)
    mixing_parts = []
    log_totals = []
    for bucket in range(3):
        length = lengths[bucket]
        row_start = row_starts[bucket]
        row_count = row_counts[bucket]
        slot_count = slot_counts[bucket]
        block_hidden = hidden[:, row_start : row_start + row_count]
        scores = (
            product("hnd,hdk->hnk", block_hidden, score_weight[:, :, :length])
            + score_bias[:, None, :length]
        )
        log_total = jax.nn.logsumexp(scores, axis=-1, keepdims=True)
        attention = (
            jnp.exp(scores - log_total)
            .astype(jnp.bfloat16)
            .reshape(head_count, slot_count, length, length)
        )
        block_values = values[row_start : row_start + row_count].reshape(
            slot_count, length, head_count, head_width
        )
        mixing = product("hsqk,skhe->sqhe", attention, block_values)
        mixing_parts.append(mixing.reshape(row_count, head_count * head_width).astype(jnp.bfloat16))
        log_totals.append(log_total)
    mixing = jnp.concatenate(mixing_parts, axis=0)
    attended = lax.psum(product("tc,cd->td", mixing, output_weight), "mp") + output_bias
    middle = token_values + attended
    second = layer_norm(middle, second_gain, second_shift).astype(jnp.bfloat16)
    expand_input = product("td,df->tf", second, expand_weight) + expand_bias
    activated = jax.nn.gelu(expand_input).astype(jnp.bfloat16)
    branch = lax.psum(product("tf,fd->td", activated, reduce_weight), "mp") + reduce_bias
    result = live_rows * (middle + branch)
    branch_gradient = upstream.astype(jnp.bfloat16)
    reduce_bias_gradient = jnp.sum(branch_gradient.astype(jnp.float32), axis=0)
    reduce_weight_gradient = product("tf,td->fd", activated, branch_gradient).reshape(-1)
    expand_gradient = gelu_backward(
        expand_input, product("td,fd->tf", branch_gradient, reduce_weight)
    ).astype(jnp.bfloat16)
    expand_bias_gradient = jnp.sum(expand_gradient.astype(jnp.float32), axis=0)
    expand_weight_gradient = product("tf,td->fd", expand_gradient, second).reshape(-1)
    second_gradient = lax.psum(product("tf,df->td", expand_gradient, expand_weight), "mp")
    middle_norm, second_gain_gradient, second_shift_gradient = jax.vjp(
        layer_norm, middle, second_gain, second_shift
    )[1](second_gradient)
    middle_gradient = upstream + middle_norm
    attended_gradient = middle_gradient.astype(jnp.bfloat16)
    output_bias_gradient = jnp.sum(attended_gradient.astype(jnp.float32), axis=0)
    output_weight_gradient = product("tc,td->cd", mixing, attended_gradient).reshape(-1)
    mixing_gradient = product("td,cd->tc", attended_gradient, output_weight).astype(jnp.bfloat16)
    score_weight_gradient = jnp.zeros(score_weight.shape, jnp.float32)
    score_bias_gradient = jnp.zeros(score_bias.shape, jnp.float32)
    hidden_parts = []
    value_parts = []
    for bucket in range(3):
        length = lengths[bucket]
        row_start = row_starts[bucket]
        row_count = row_counts[bucket]
        slot_count = slot_counts[bucket]
        block_hidden = hidden[:, row_start : row_start + row_count]
        block_weight = score_weight[:, :, :length]
        scores = product("hnd,hdk->hnk", block_hidden, block_weight) + score_bias[:, None, :length]
        softmax_full = jnp.exp(scores - log_totals[bucket])
        attention = softmax_full.astype(jnp.bfloat16).reshape(
            head_count, slot_count, length, length
        )
        block_values = values[row_start : row_start + row_count].reshape(
            slot_count, length, head_count, head_width
        )
        block_gradient = mixing_gradient[row_start : row_start + row_count].reshape(
            slot_count, length, head_count, head_width
        )
        attention_gradient = product("sqhe,skhe->hsqk", block_gradient, block_values).reshape(
            head_count, row_count, length
        )
        value_parts.append(
            product("hsqk,sqhe->skhe", attention, block_gradient).reshape(
                row_count, head_count * head_width
            )
        )
        score_gradient = softmax_full * (
            attention_gradient - jnp.sum(attention_gradient * softmax_full, axis=-1, keepdims=True)
        )
        score_gradient = score_gradient.astype(jnp.bfloat16)
        padding = full_length - length
        score_bias_gradient = score_bias_gradient + jnp.pad(
            jnp.sum(score_gradient.astype(jnp.float32), axis=1), ((0, 0), (0, padding))
        )
        score_weight_gradient = score_weight_gradient + jnp.pad(
            product("hnd,hnk->hdk", block_hidden, score_gradient), ((0, 0), (0, 0), (0, padding))
        )
        hidden_parts.append(product("hnk,hdk->hnd", score_gradient, block_weight))
    hidden_gradient = jnp.concatenate(hidden_parts, axis=1)
    value_gradient = jnp.concatenate(value_parts, axis=0).astype(jnp.bfloat16)
    value_bias_gradient = jnp.sum(value_gradient.astype(jnp.float32), axis=0)
    value_weight_gradient = product("tc,td->cd", value_gradient, normed).reshape(-1)
    input_gradient_hidden = gelu_backward(hidden_input, hidden_gradient).astype(jnp.bfloat16)
    hidden_bias_gradient = jnp.sum(input_gradient_hidden.astype(jnp.float32), axis=1)
    hidden_weight_gradient = product("td,hte->hde", normed, input_gradient_hidden).reshape(-1)
    score_weight_gradient = score_weight_gradient.reshape(-1)
    normed_part = product("hte,hde->td", input_gradient_hidden, hidden_weight) + product(
        "tc,dc->td", value_gradient, value_weight
    )
    normed_gradient = lax.psum(normed_part, "mp")
    input_norm, first_gain_gradient, first_shift_gradient = jax.vjp(
        layer_norm, token_values, first_gain, first_shift
    )[1](normed_gradient)
    input_gradient = middle_gradient + input_norm
    (
        hidden_weight_gradient,
        score_weight_gradient,
        value_weight_gradient,
        output_weight_gradient,
        expand_weight_gradient,
        reduce_weight_gradient,
    ) = (
        lax.psum_scatter(hidden_weight_gradient, "dp", scatter_dimension=0, tiled=True),
        lax.psum_scatter(score_weight_gradient, "dp", scatter_dimension=0, tiled=True),
        lax.psum_scatter(value_weight_gradient, "dp", scatter_dimension=0, tiled=True),
        lax.psum_scatter(output_weight_gradient, "dp", scatter_dimension=0, tiled=True),
        lax.psum_scatter(expand_weight_gradient, "dp", scatter_dimension=0, tiled=True),
        lax.psum_scatter(reduce_weight_gradient, "dp", scatter_dimension=0, tiled=True),
    )
    (
        first_gain_gradient,
        first_shift_gradient,
        hidden_bias_gradient,
        score_bias_gradient,
        value_bias_gradient,
        output_bias_gradient,
        second_gain_gradient,
        second_shift_gradient,
        expand_bias_gradient,
        reduce_bias_gradient,
    ) = lax.psum(
        (
            first_gain_gradient,
            first_shift_gradient,
            hidden_bias_gradient,
            score_bias_gradient,
            value_bias_gradient,
            output_bias_gradient,
            second_gain_gradient,
            second_shift_gradient,
            expand_bias_gradient,
            reduce_bias_gradient,
        ),
        "dp",
    )
    outputs = []
    gradients = []
    for bucket in range(3):
        row_start = row_starts[bucket]
        row_count = row_counts[bucket]
        outputs.append(
            result[row_start : row_start + row_count]
            .reshape(slot_counts[bucket], lengths[bucket], features)
            .astype(jnp.bfloat16)
        )
        gradients.append(
            input_gradient[row_start : row_start + row_count]
            .reshape(slot_counts[bucket], lengths[bucket], features)
            .astype(jnp.bfloat16)
        )
    return (
        outputs[0],
        outputs[1],
        outputs[2],
        gradients[0],
        gradients[1],
        gradients[2],
        first_gain_gradient,
        first_shift_gradient,
        hidden_weight_gradient,
        hidden_bias_gradient,
        score_weight_gradient,
        score_bias_gradient,
        value_weight_gradient,
        value_bias_gradient,
        output_weight_gradient,
        output_bias_gradient,
        second_gain_gradient,
        second_shift_gradient,
        expand_weight_gradient,
        expand_bias_gradient,
        reduce_weight_gradient,
        reduce_bias_gradient,
    )


def solution(mesh):
    placed = (
        P("dp", None, None),
        P("dp", None, None),
        P("dp", None, None),
        P("dp"),
        P("dp"),
        P("dp"),
        P(),
        P(),
        P("mp", None, None),
        P("mp", None),
        P("mp", None, None),
        P("mp", None),
        P(None, "mp"),
        P("mp"),
        P("mp", None),
        P(),
        P(),
        P(),
        P(None, "mp"),
        P("mp"),
        P("mp", None),
        P(),
        P("dp", None, None),
        P("dp", None, None),
        P("dp", None, None),
    )
    fits = mesh.shape["dp"] == 16 and mesh.shape["mp"] == 2
    return jax.shard_map(
        grid_body if fits else plain_body,
        mesh=mesh,
        in_specs=placed,
        out_specs=(
            P("dp", None, None),
            P("dp", None, None),
            P("dp", None, None),
            P("dp", None, None),
            P("dp", None, None),
            P("dp", None, None),
            P(),
            P(),
            P(("mp", "dp")),
            P("mp", None),
            P(("mp", "dp")),
            P("mp", None),
            P(("mp", "dp")),
            P("mp"),
            P(("mp", "dp")),
            P(),
            P(),
            P(),
            P(("mp", "dp")),
            P("mp"),
            P(("mp", "dp")),
            P(),
        ),
        check_vma=False,
    )
```

```python
import jax
import jax.numpy as jnp
from jax import lax
from jax.experimental import pallas as pl
from jax.experimental.pallas import tpu as pltpu
from jax.sharding import PartitionSpec as P

epsilon = 1e-05


def layer_norm(values, gains, offset):
    centred = values - jnp.mean(values, axis=-1, keepdims=True)
    variance = jnp.mean(centred * centred, axis=-1, keepdims=True)
    return centred * lax.rsqrt(variance + epsilon) * gains + offset


def product(form, left, right):
    return jnp.einsum(form, left, right, preferred_element_type=jnp.float32)


def gelu_backward(inputs, upstream):
    return jax.vjp(jax.nn.gelu, inputs)[1](upstream)[0]


def live_flags(count_array, slot_count, length):
    flags = (jnp.arange(slot_count) < count_array[0]).astype(jnp.float32)
    return jnp.repeat(flags, length)


BUCKETS = ((0, 128), (128, 256), (384, 512))
HEADS = 6
WIDTH = 64
ROOT = 0.7978845608028654
CUBE = 0.044715


def dot_rows(left, right):
    return lax.dot_general(
        left, right, (((0,), (0,)), ((), ())), preferred_element_type=jnp.float32
    )


def dot_last(left, right):
    return lax.dot_general(
        left, right, (((1,), (1,)), ((), ())), preferred_element_type=jnp.float32
    )


def dot_plain(left, right):
    return jnp.dot(left, right, preferred_element_type=jnp.float32)


def wide(lines):
    return jnp.concatenate([lines[at : at + 1] for at in range(lines.shape[0])], axis=1)


def normalise(rows):
    centred = rows - jnp.mean(rows, axis=-1, keepdims=True)
    scale = lax.rsqrt(jnp.mean(centred * centred, axis=-1, keepdims=True) + epsilon)
    return centred * scale, scale


def gelu_pair(inputs):
    square = inputs * inputs
    curve = jnp.tanh(inputs * (ROOT + ROOT * CUBE * square))
    half = 0.5 + 0.5 * curve
    gelu = inputs * half
    slope = half + (gelu * (1.0 - half)) * (2.0 * ROOT + 6.0 * ROOT * CUBE * square)
    return gelu, slope


def attention_forward(
    tokens_a, tokens_b, tokens_c, gain, shift, hidden_weight_h, hidden_bias,
    score_weight_h, score_bias, value_weight, value_bias,
    normed, hidden_h, slope_h, full_a_h, full_b_h, full_c_h, values, mixing,
    hidden_weight, score_weight, hidden, slope, full_a, full_b, full_c, load_sems, save_sems,
):
    loads = []
    for head in range(HEADS):
        loads.append(
            (
                pltpu.make_async_copy(
                    hidden_weight_h.at[head], hidden_weight.at[head], load_sems.at[0, head]
                ),
                pltpu.make_async_copy(
                    score_weight_h.at[head], score_weight.at[head], load_sems.at[1, head]
                ),
            )
        )
    for pair in loads[:2]:
        for load in pair:
            load.start()
    for (start, length), tokens in zip(BUCKETS, (tokens_a, tokens_b, tokens_c)):
        for row in range(0, length, 128):
            unit, _ = normalise(tokens[0, row : row + 128].astype(jnp.float32))
            normed[start + row : start + row + 128] = (unit * wide(gain) + wide(shift)).astype(
                jnp.bfloat16
            )
    values[...] = (dot_plain(normed[...], value_weight[...]) + wide(value_bias)).astype(jnp.bfloat16)

    def hidden_rows(head, start, length):
        rows, slot = slice(start, start + length), head % 3
        inputs = dot_plain(normed[rows], hidden_weight[head]) + hidden_bias[head : head + 1]
        gelu, steep = gelu_pair(inputs)
        hidden[slot, rows] = gelu.astype(jnp.bfloat16)
        slope[slot, rows] = steep.astype(jnp.bfloat16)

    def mixing_rows(head, bucket, row, count):
        slot, columns = head % 3, slice(WIDTH * head, WIDTH * head + WIDTH)
        first, length = BUCKETS[bucket]
        full = (full_a, full_b, full_c)[bucket]
        rows = slice(first + row, first + row + count)
        scores = (
            dot_plain(hidden[slot, rows], score_weight[head, :, 0:length])
            + score_bias[head : head + 1, 0:length]
        )
        powers = jnp.exp(scores - jnp.max(scores, axis=-1, keepdims=True))
        softmax = powers * (1.0 / jnp.sum(powers, axis=-1, keepdims=True))
        attention = softmax.astype(jnp.bfloat16)
        full[slot, row : row + count] = attention
        mixed = dot_plain(attention, values[first : first + length, columns])
        mixing[rows, columns] = mixed.astype(jnp.bfloat16)

    def save_of(head):
        slot = head % 3
        return [
            pltpu.make_async_copy(source.at[slot], target.at[head], save_sems.at[number, slot])
            for number, (source, target) in enumerate(
                (
                    (hidden, hidden_h), (slope, slope_h), (full_a, full_a_h),
                    (full_b, full_b_h), (full_c, full_c_h),
                )
            )
        ]

    loads[0][0].wait()
    for row in range(0, 896, 128):
        hidden_rows(0, row, 128)
    for save in save_of(0)[:2]:
        save.start()
    for head in range(HEADS):
        last = head + 1 == HEADS
        loads[head][1].wait()
        if not last:
            loads[head + 1][0].wait()
            if head >= 2:
                for save in save_of(head - 2)[:2]:
                    save.wait()
        if head >= 3:
            for save in save_of(head - 3)[2:]:
                save.wait()
        if head + 2 < HEADS:
            for load in loads[head + 2]:
                load.start()
        for bucket, (_, length) in enumerate(BUCKETS):
            mixing_rows(head, bucket, 0, length)
        for save in save_of(head)[2:]:
            save.start()
        if not last:
            for row in range(0, 896, 128):
                hidden_rows(head + 1, row, 128)
            for save in save_of(head + 1)[:2]:
                save.start()
    for save in save_of(HEADS - 3) + save_of(HEADS - 2) + save_of(HEADS - 1):
        save.wait()


def attention_forward_call(
    tokens, gain, shift, hidden_weight, hidden_bias, score_weight, score_bias, value_weight, value_bias
):
    bf16 = jnp.bfloat16
    rows, features = 896, 768
    far, near = pl.BlockSpec(memory_space=pl.ANY), pl.BlockSpec(memory_space=pltpu.VMEM)
    squares = [(HEADS, length, length) for _, length in BUCKETS]
    return pl.pallas_call(
        attention_forward,
        out_shape=(
            jax.ShapeDtypeStruct((rows, features), bf16),
            jax.ShapeDtypeStruct((HEADS, rows, features), bf16),
            jax.ShapeDtypeStruct((HEADS, rows, features), bf16),
            *(jax.ShapeDtypeStruct(square, bf16) for square in squares),
            jax.ShapeDtypeStruct((rows, HEADS * WIDTH), bf16),
            jax.ShapeDtypeStruct((rows, HEADS * WIDTH), bf16),
        ),
        in_specs=[near] * 5 + [far, near, far, near, near, near],
        out_specs=(near, far, far, far, far, far, near, near),
        scratch_shapes=[
            pltpu.VMEM(hidden_weight.shape, bf16),
            pltpu.VMEM(score_weight.shape, bf16),
            pltpu.VMEM((3, rows, features), bf16),
            pltpu.VMEM((3, rows, features), bf16),
            *(pltpu.VMEM((3, *square[1:]), bf16) for square in squares),
            pltpu.SemaphoreType.DMA((2, HEADS)),
            pltpu.SemaphoreType.DMA((5, 3)),
        ],
        compiler_params=pltpu.CompilerParams(vmem_limit_bytes=56 * 2**20),
        name="attention_forward",
    )(
        *tokens, gain.reshape(-1, 128), shift.reshape(-1, 128), hidden_weight, hidden_bias,
        score_weight, score_bias, value_weight, value_bias.reshape(-1, 128),
    )


SLOTS = 4
AHEAD = 6
ITEMS = 15
LAGS = 5
PARTS = 3
ROWS = 96
EDGE = 16
WIDE = 32
FIRST = EDGE + WIDE
STEPS = PARTS * ITEMS
PAIR_ROWS = 224
SMALL_ROWS = 112
FIRST_GAIN, FIRST_SHIFT, HIDDEN_BIAS, SCORE_BIAS, VALUE_BIAS = 0, 6, 12, 48, 72
OUTPUT_BIAS, SECOND_GAIN, SECOND_SHIFT, EXPAND_BIAS, REDUCE_BIAS = 75, 81, 87, 93, 105
SMALL_PLACES = (
    (FIRST_GAIN, 6), (FIRST_SHIFT, 6), (HIDDEN_BIAS, 36), (SCORE_BIAS, 24), (VALUE_BIAS, 3),
    (OUTPUT_BIAS, 6), (SECOND_GAIN, 6), (SECOND_SHIFT, 6), (EXPAND_BIAS, 12), (REDUCE_BIAS, 6),
)
BRANCH_AT, HEADS_AT, RESULT_AT, NORMED_AT, PAIR_AT, INPUT_AT, SMALL_AT = 2, 4, 11, 12, 24, 26, 34
MESH_ID = pl.DeviceIdType.MESH


def layer_kernel(
    mixing_h, normed_h, values_h, hidden_h, slope_h, full_a_h, full_b_h, full_c_h,
    tokens_a_h, tokens_b_h, tokens_c_h, branch_a_h, branch_b_h, branch_c_h,
    hidden_weight_h, score_weight_h, value_weight_h, output_weight_h, expand_weight_h,
    reduce_weight_h,
    live_a_h, live_b_h, live_c_h, first_gain, output_bias, second_gain, second_shift, expand_bias,
    reduce_bias,
    result_a, result_b, result_c, gradient_a, gradient_b, gradient_c,
    hidden_out_h, score_out_h, value_out_h, output_out_h, expand_out_h, reduce_out_h, *rest,
):
    small_out, rest = rest[:10], rest[10:]
    middle_h, branch_own_h, branch_far_h, rest = rest[0], rest[1], rest[2], rest[3:]
    (
        out_hidden, out_score, out_value, out_output, out_expand, out_reduce,
        live_a, live_b, live_c,
        arena, branch, second, attended, tokens, flipped, mixing, values, mixed, value,
        output_weight, value_weight, score_weight, slope, full_a, full_b, full_c,
        score_a, score_b, score_c, hidden, residual, pair_out, pair_in, stage, pieces, finished,
        own, first_x, first_y, next_x, next_y, middle, middle_up, middle_down,
        edge, edge_up, edge_down, last_x, last_y, done,
        small, small_x, small_sum, small_y, small_z,
        load_sems, head_sems, hidden_sems, weight_sems, pair_sems, far_sems, near_sems, piece_sems,
        finished_sems, first_sems, next_sems, middle_sems, edge_sems, last_sems, small_sems,
        share_sems, pair_free,
    ) = rest
    f32, bf16 = jnp.float32, jnp.bfloat16
    spot = lax.axis_index("dp")
    x, y, z = spot % 2, (spot // 2) % 2, spot // 4
    to_x = {"dp": spot + 1 - 2 * x}
    to_y = {"dp": spot + 2 - 4 * y}
    to_up = {"dp": spot + 4}
    to_down = {"dp": spot - 4}
    to_mate = {"mp": 1 - lax.axis_index("mp")}

    loads = []
    for number, (source, target) in enumerate(
        (
            (mixing_h, mixing), (output_weight_h, output_weight),
            (tokens_a_h.at[0], tokens.at[0:128]), (tokens_b_h.at[0], tokens.at[128:384]),
            (tokens_c_h.at[0], tokens.at[384:896]),
            (expand_weight_h.at[:, 0:768], arena.at[4, 0:768]),
            (expand_weight_h.at[:, 768:1536], arena.at[5, 0:768]),
            (branch_a_h.at[0], branch.at[0:128]), (branch_b_h.at[0], branch.at[128:384]),
            (branch_c_h.at[0], branch.at[384:896]),
            (reduce_weight_h.at[0:768], arena.at[2, 0:768]),
            (reduce_weight_h.at[768:1536], arena.at[3, 0:768]),
            (values_h, values), (value_weight_h, value_weight),
            (live_a_h, live_a), (live_b_h, live_b), (live_c_h, live_c),
        )
    ):
        loads.append(pltpu.make_async_copy(source, target, load_sems.at[number]))
    normed_load = pltpu.make_async_copy(normed_h, second, load_sems.at[20])
    middle_save = pltpu.make_async_copy(residual, middle_h, load_sems.at[21])

    def share_save(number):
        source, target = (
            (out_reduce, reduce_out_h), (out_expand, expand_out_h), (out_score, score_out_h),
            (out_hidden, hidden_out_h), (out_value, value_out_h), (out_output, output_out_h),
        )[number]
        return pltpu.make_async_copy(source, target, share_sems.at[number])

    def head_loads(head):
        slot = head % 2
        return [
            pltpu.make_async_copy(source.at[head], target.at[slot], head_sems.at[slot, number])
            for number, (source, target) in enumerate(
                (
                    (slope_h, slope), (full_a_h, full_a), (full_b_h, full_b), (full_c_h, full_c),
                    (score_weight_h, score_weight),
                )
            )
        ]

    def hidden_load(turn):
        slot = turn % 2
        return pltpu.make_async_copy(
            hidden_h.at[turn % HEADS], hidden.at[slot], hidden_sems.at[slot]
        )

    def weight_load(head):
        slot = head % 2
        return pltpu.make_async_copy(
            hidden_weight_h.at[head], arena.at[6 + slot, 0:768], weight_sems.at[slot]
        )

    for load in loads:
        load.start()
    for load in head_loads(0):
        load.start()
    for number in (0, 1):
        hidden_load(number).start()

    barrier = pltpu.get_barrier_semaphore()
    for device in (to_x, to_y, to_mate):
        pl.semaphore_signal(barrier, inc=1, device_id=device, device_id_type=MESH_ID)

    @pl.when(z < 3)
    def _():
        pl.semaphore_signal(barrier, inc=1, device_id=to_up, device_id_type=MESH_ID)

    @pl.when(z > 0)
    def _():
        pl.semaphore_signal(barrier, inc=1, device_id=to_down, device_id_type=MESH_ID)

    inner = (z > 0) & (z < 3)

    @pl.when(inner)
    def _():
        pl.semaphore_wait(barrier, 5)

    @pl.when(jnp.logical_not(inner))
    def _():
        pl.semaphore_wait(barrier, 4)

    def remote(source, target, sems, slot, device):
        return pltpu.make_async_remote_copy(
            src_ref=source,
            dst_ref=target,
            send_sem=sems.at[0, slot],
            recv_sem=sems.at[1, slot],
            device_id=device,
            device_id_type=MESH_ID,
        )

    def span(at, rows):
        return pl.ds(pl.multiple_of(at * rows, 16), rows)

    def repeat(first, last, body):
        def turn(at, carry):
            body(at)
            return carry

        lax.fori_loop(first, last, turn, 0)

    def pair_copy(at):
        rows = span(at, PAIR_ROWS)
        return remote(pair_out.at[rows], pair_in.at[rows], pair_sems, at, to_mate)

    def pair_ready(chunk):
        for at in range(4):

            @pl.when(chunk == (0, 1, 3, 5)[at])
            def _():
                pair_copy(at).wait_recv()

    def pair_done(spare):
        repeat(0, 4, lambda at: pair_copy(at).wait_send())
        if spare:
            pl.semaphore_signal(pair_free, inc=1, device_id=to_mate, device_id_type=MESH_ID)

    def live_of(chunk):
        count = jnp.where(chunk == 0, live_a[0], jnp.where(chunk < 3, live_b[0], live_c[0]))
        return jnp.where(count > 0, 1.0, 0.0).astype(f32)

    def add_line(row, line):
        for tile in range(line.shape[1] // 128):
            small[pl.ds(row + tile, 1)] += line[:, 128 * tile : 128 * tile + 128]

    def column_sum(block):
        return jnp.sum(block.astype(f32), axis=0, keepdims=True)

    def put(slot, dest, row, block):
        z_at, y_at, x_at = dest // 4, (dest // 2) % 2, dest % 2
        rows = block.shape[0]
        own[slot, row // ROWS, z_at, y_at, x_at, row % ROWS : row % ROWS + rows, :] = block

    def produce(item, third):
        slot = item % 3

        def feed_forward(left, right, column):
            column = pl.multiple_of(column, 128)

            def part(half):
                block = dot_rows(arena[left + half], right[:, pl.ds(column, 128)])
                for at in range(8):
                    own[slot, third, 2 * half + at // 4, at // 2 % 2, at % 2] = block[
                        96 * at : 96 * at + 96
                    ]

            repeat(0, 2, part)

        @pl.when(item < 2)
        def _():
            feed_forward(0, branch, 384 * item + 128 * third)

        @pl.when((item >= 2) & (item < 4))
        def _():
            feed_forward(6, second, 384 * (item - 2) + 128 * third)

        def heads(block_of):
            def part(head):
                block = block_of(head)
                for piece in range(8):
                    unit = 8 * head + piece
                    own[slot, unit % 3, unit // 12, unit // 6 % 2, unit // 3 % 2] = block[
                        96 * piece : 96 * piece + 96
                    ]

            repeat(2 * third, 2 * third + 2, part)

        def score_heads(block_of):
            def part(head):
                turn = HEADS * (item - 4) + head
                hidden_load(turn).wait()
                return block_of(head, hidden.at[turn % 2])

            heads(part)

            for turn in (0, 1):
                after = HEADS * (item - 4) + 2 * third + 2 + turn

                @pl.when(after < 4 * HEADS)
                def _():
                    hidden_load(after).start()

        @pl.when(item == 4)
        def _():
            score_heads(
                lambda head, rows: dot_rows(rows[0:128], score_a[head])
                + dot_rows(rows[128:384], score_b[head, :, 0:128])
                + dot_rows(rows[384:896], score_c[head, :, 0:128])
            )

        @pl.when(item == 5)
        def _():
            score_heads(
                lambda head, rows: dot_rows(rows[128:384], score_b[head, :, 128:256])
                + dot_rows(rows[384:896], score_c[head, :, 128:256])
            )

        @pl.when((item == 6) | (item == 7))
        def _():
            column = pl.multiple_of(128 * (item - 4), 128)
            score_heads(
                lambda head, rows: dot_rows(rows[384:896], score_c[head, :, pl.ds(column, 128)])
            )

        @pl.when((item == 8) & (third == 0))
        def _():
            normed_load.wait()
            flipped[...] = second[...].T

        @pl.when((item >= 8) & (item < 14))
        def _():
            column = pl.multiple_of(128 * (item - 8), 128)
            heads(lambda head: dot_plain(flipped[...], arena[head, :, pl.ds(column, 128)]))

        for part, (left, right) in enumerate(((value, second), (mixing, attended))):

            @pl.when((item == 14) & (third == part))
            def _():
                block = dot_rows(left[...], right[...])
                for dest in range(16):
                    for piece in range(6):
                        put(
                            slot, dest, 144 * part + 24 * piece,
                            block[24 * dest : 24 * dest + 24, 128 * piece : 128 * piece + 128],
                        )

    def deliver(item):
        def spread(target, tiles, first):
            for part in range(PARTS):
                target[pl.ds(first + tiles * ROWS * part, ROWS, stride=tiles), :] = done[part]

        def stack(target, first):
            for part in range(PARTS):
                target[pl.ds(first + part, ROWS, stride=6), :] = done[part]

        @pl.when(item < 2)
        def _():
            stack(out_reduce, 3 * item)

        @pl.when((item >= 2) & (item < 4))
        def _():
            stack(out_expand, 3 * (item - 2))

        @pl.when((item >= 4) & (item < 8))
        def _():
            spread(out_score, 4, item - 4)

        @pl.when((item >= 8) & (item < 14))
        def _():
            spread(out_hidden, 6, item - 8)

        @pl.when(item == 14)
        def _():
            for start, target in ((0, out_value), (144, out_output)):
                for piece in range(6):
                    row = start + 24 * piece
                    target[pl.ds(piece, 24, stride=6), :] = done[
                        row // ROWS, row % ROWS : row % ROWS + 24
                    ]

    def home(i):
        return own.at[(i // PARTS) % 3, i % PARTS], i % SLOTS

    def first_copies(i):
        held, slot = home(i)[0], i % AHEAD
        return (
            remote(held.at[:, :, 1 - x, 0:FIRST], first_x.at[slot], first_sems.at[0], slot, to_x),
            remote(held.at[:, 1 - y, :, FIRST:ROWS], first_y.at[slot], first_sems.at[1], slot, to_y),
        )

    def next_copies(i):
        held, slot = home(i)
        return (
            remote(held.at[:, y, 1 - x, FIRST : FIRST + EDGE], next_x.at[slot], next_sems.at[0], slot, to_x),
            remote(held.at[:, 1 - y, x, 0:EDGE], next_y.at[slot], next_sems.at[1], slot, to_y),
        )

    def last_copies(i):
        slot = i % SLOTS
        return (
            remote(middle.at[slot, z, 3 - x], last_x.at[slot], last_sems.at[0], slot, to_x),
            remote(middle.at[slot, z, 1 - y], last_y.at[slot], last_sems.at[1], slot, to_y),
        )

    def line_up(kept, landing, sems, slot, place):
        return remote(kept.at[slot, place + 1 : 4], landing.at[slot, place:3], sems.at[0], slot, to_up)

    def line_down(kept, landing, sems, slot, place):
        return remote(kept.at[slot, 0:place], landing.at[slot, 0:place], sems.at[1], slot, to_down)

    def line_hop(kept, landing_up, landing_down, sems, i, hop):
        slot = i % SLOTS
        for place in range(4):
            if place == hop:

                @pl.when(z == place)
                def _():
                    if place > 0:
                        line_up(kept, landing_up, sems, slot, place - 1).wait_recv()
                        kept[slot, place:4] += landing_up[slot, place - 1 : 3]
                    if place < 3:
                        line_up(kept, landing_up, sems, slot, place).start()

            if 3 - place == hop:

                @pl.when(z == place)
                def _():
                    if place < 3:
                        line_down(kept, landing_down, sems, slot, place + 1).wait_recv()
                        kept[slot, 0 : place + 1] += landing_down[slot, 0 : place + 1]
                    if place > 0:
                        line_down(kept, landing_down, sems, slot, place).start()

    def line_sent(kept, landing_up, landing_down, sems, i):
        slot = i % SLOTS
        for place in range(4):

            @pl.when(z == place)
            def _():
                if place < 3:
                    line_up(kept, landing_up, sems, slot, place).wait_send()
                if place > 0:
                    line_down(kept, landing_down, sems, slot, place).wait_send()

    middle_line = (middle, middle_up, middle_down, middle_sems)
    edge_line = (edge, edge_up, edge_down, edge_sems)

    def small_steps(t):
        def copy(number, source, target, device):
            return pltpu.make_async_remote_copy(
                src_ref=source, dst_ref=target, send_sem=small_sems.at[0, number],
                recv_sem=small_sems.at[1, number], device_id=device, device_id_type=MESH_ID,
            )

        over_x = copy(0, small, small_x, to_x)
        over_y = copy(1, small_sum, small_y, to_y)

        def up(place):
            part = small_z.at[0 : place + 1]
            return copy(2, part, part, to_up)

        def down(place):
            part = small_z.at[place:4]
            return copy(3, part, part, to_down)

        @pl.when(t == 0)
        def _():
            over_x.start()

        @pl.when(t == 1)
        def _():
            over_x.wait()
            small_sum[...] = small[...] + small_x[...]
            over_y.start()

        @pl.when(t == 2)
        def _():
            over_y.wait()
            small_z[z] = small_sum[...] + small_y[...]

        for place in range(4):

            @pl.when((z == place) & (t == 2 + place))
            def _():
                if place > 0:
                    up(place - 1).wait_recv()
                if place < 3:
                    up(place).start()

            @pl.when((z == place) & (t == 5 - place))
            def _():
                if place < 3:
                    down(place + 1).wait_recv()
                if place > 0:
                    down(place).start()

        @pl.when(t == 6)
        def _():
            small_sum[...] = ((small_z[0] + small_z[1]) + small_z[2]) + small_z[3]
            for (row, rows), target in zip(SMALL_PLACES, small_out):
                columns = target.shape[1] // 128
                for at in range(rows):
                    line, tile = at // columns, at % columns
                    target[line : line + 1, 128 * tile : 128 * tile + 128] = small_sum[
                        row + at : row + at + 1
                    ]
            for place in range(4):

                @pl.when(z == place)
                def _():
                    if place < 3:
                        up(place).wait_send()
                    if place > 0:
                        down(place).wait_send()

    def expand_of(quarter, rows):
        column = pl.multiple_of(quarter % 2 * 384, 128)
        bias = [expand_bias[pl.ds(3 * quarter + at, 1)] for at in range(3)]
        return dot_plain(
            second[rows], arena[4 + quarter // 2, 0:768, pl.ds(column, 384)]
        ) + jnp.concatenate(bias, axis=1)

    def activate(quarter, half):
        rows = span(half, 448)
        gelu, _ = gelu_pair(expand_of(quarter, rows))
        column = pl.multiple_of(quarter % 2 * 384, 128)
        arena[quarter // 2, rows, pl.ds(column, 384)] = gelu.astype(bf16)

    def expand_gradient(turn):
        quarter, rows = turn // 2, span(turn % 2, 448)
        column = pl.multiple_of(quarter % 2 * 384, 128)
        _, steep = gelu_pair(expand_of(quarter, rows))
        spread = dot_last(branch[rows], arena[2 + quarter // 2, pl.ds(column, 384)])
        grown = (steep * spread).astype(bf16)
        arena[6 + quarter // 2, rows, pl.ds(column, 384)] = grown
        add_line(EXPAND_BIAS + 3 * quarter, column_sum(grown))

    def second_gradient(at):
        rows = span(at, PAIR_ROWS)
        pair_out[rows] = dot_last(arena[6, rows], arena[4, 0:768]) + dot_last(
            arena[7, rows], arena[5, 0:768]
        )
        pair_copy(at).start()

    def branch_away(at):
        return remote(
            stage.at[at % 2], branch_far_h.at[span(at, PAIR_ROWS)], far_sems, at, to_mate
        )

    def branch_save(at):
        return pltpu.make_async_copy(
            stage.at[at % 2], branch_own_h.at[span(at, PAIR_ROWS)], near_sems.at[at]
        )

    def branch_sent(at):
        branch_away(at).wait_send()
        branch_save(at).wait()

    def branch_part(at):
        rows = span(at, PAIR_ROWS)

        @pl.when(at >= 2)
        def _():
            branch_sent(at - 2)

        stage[at % 2] = dot_plain(arena[0, rows], arena[2, 0:768]) + dot_plain(
            arena[1, rows], arena[3, 0:768]
        )
        branch_away(at).start()
        branch_save(at).start()

    def middle_gradient(chunk):
        rows = span(chunk, 128)
        pair_ready(chunk)
        total = pair_out[rows] + pair_in[rows]
        unit, scale = normalise(residual[rows])
        add_line(SECOND_GAIN, column_sum(total * unit))
        add_line(SECOND_SHIFT, column_sum(total))
        scaled = total * wide(second_gain)
        mean = jnp.mean(scaled, axis=-1, keepdims=True)
        inner = jnp.mean(scaled * unit, axis=-1, keepdims=True)
        result = branch[rows].astype(f32) + (scaled - mean - unit * inner) * scale
        residual[rows] = result
        rounded = result.astype(bf16)
        attended[rows] = rounded
        add_line(OUTPUT_BIAS, column_sum(rounded))

    def head_gradient(head):
        slot, left = head % 2, head % 2 == 0
        both = pl.ds(pl.multiple_of(128 * (head // 2), 128), 128)

        @pl.when(head + 1 < HEADS)
        def _():
            for load in head_loads(head + 1):
                load.start()

        for load in head_loads(head):
            load.wait()
        for (start, length), full, score in zip(
            BUCKETS, (full_a, full_b, full_c), (score_a, score_b, score_c)
        ):
            rows = slice(start, start + length)

            def columns(member):
                pair = member[rows, both]
                return jnp.where(left, pair[:, 0:WIDTH], pair[:, WIDTH : 2 * WIDTH])

            attention = full[slot]
            softmax = attention.astype(f32)
            upstream = columns(mixed)
            attention_gradient = dot_last(upstream, columns(values))
            own_value = dot_rows(attention, upstream).astype(bf16)
            other = jnp.where(left, own_value, value[rows, both][:, 0:WIDTH])
            value[rows, both] = jnp.concatenate([other, own_value], axis=1)
            inner = jnp.sum(attention_gradient * softmax, axis=-1, keepdims=True)
            gradient = (softmax * (attention_gradient - inner)).astype(bf16)
            score[head] = gradient
            add_line(SCORE_BIAS + 4 * head, column_sum(gradient))
            spread = dot_last(gradient, score_weight[slot, :, 0:length])
            grown = (slope[slot, rows].astype(f32) * spread).astype(bf16)
            arena[head, rows] = grown
            add_line(HIDDEN_BIAS + 6 * head, column_sum(grown))

    def piece_loads(chunk):
        rows = span(chunk, 128)
        return [
            pltpu.make_async_copy(source.at[rows], pieces.at[at], piece_sems.at[at])
            for at, source in enumerate((middle_h, branch_own_h, branch_far_h))
        ]

    def finish(chunk, block, targets):
        def copy(number):
            bucket = (0, 1, 1, 2, 2, 2, 2)[number]
            row = 128 * (number - (0, 1, 3)[bucket])
            return pltpu.make_async_copy(
                finished.at[number % 2], targets[bucket].at[0, row : row + 128],
                finished_sems.at[number % 2],
            )

        for number in range(2, 7):

            @pl.when(chunk == number)
            def _():
                copy(number - 2).wait()

        finished[chunk % 2] = block.astype(bf16)
        for number in range(7):

            @pl.when(chunk == number)
            def _():
                copy(number).start()
                if number == 6:
                    copy(5).wait()
                    copy(6).wait()

    def result_rows(chunk):
        for load in piece_loads(chunk):
            load.wait()
        total = live_of(chunk) * (pieces[0] + ((pieces[1] + pieces[2]) + wide(reduce_bias)))
        finish(chunk, total, (result_a, result_b, result_c))

        @pl.when(chunk < 6)
        def _():
            for load in piece_loads(chunk + 1):
                load.start()

    def normed_gradient(head):
        weight_load(head).wait()

        def part(half):
            rows = span(half, 448)
            block = dot_last(arena[head, rows], arena[6 + head % 2, 0:768])
            pair_out[rows] = jnp.where(head == 0, 0.0, pair_out[rows]) + block

        repeat(0, 2, part)

        @pl.when(head + 2 < HEADS)
        def _():
            weight_load(head + 2).start()

    def input_gradient(chunk):
        rows = span(chunk, 128)
        pair_ready(chunk)
        total = pair_out[rows] + pair_in[rows]
        unit, scale = normalise(tokens[rows].astype(f32))
        add_line(FIRST_GAIN, column_sum(total * unit))
        add_line(FIRST_SHIFT, column_sum(total))
        scaled = total * wide(first_gain)
        mean = jnp.mean(scaled, axis=-1, keepdims=True)
        inner = jnp.mean(scaled * unit, axis=-1, keepdims=True)
        result = residual[rows] + (scaled - mean - unit * inner) * scale
        finish(chunk, result, (gradient_a, gradient_b, gradient_c))

    def layer_steps(t):
        def between(first, count):
            return (t >= first) & (t < first + count)

        @pl.when(t == 0)
        def _():
            loads[10].wait()
            loads[11].wait()

        @pl.when(between(0, 2))
        def _():
            repeat(4 * t, 4 * t + 4, expand_gradient)

        @pl.when(t == 2)
        def _():
            pl.semaphore_wait(pair_free, 1)
            repeat(0, 4, second_gradient)

        @pl.when(between(BRANCH_AT, 2))
        def _():
            late = t - BRANCH_AT
            repeat(2 * late, 2 * late + 2, branch_part)

        @pl.when(t == BRANCH_AT + 1)
        def _():
            middle_save.wait()

        @pl.when(between(BRANCH_AT + 1, 2))
        def _():
            late = t - BRANCH_AT - 1
            repeat(4 * late, 4 + 3 * late, middle_gradient)

        @pl.when(t == BRANCH_AT + 2)
        def _():
            pair_done(True)
            mixed[...] = dot_last(attended[...], output_weight[...]).astype(bf16)
            repeat(2, 4, branch_sent)
            loads[12].wait()

        @pl.when(between(HEADS_AT, HEADS))
        def _():
            head_gradient(t - HEADS_AT)

        @pl.when(t == HEADS_AT + HEADS)
        def _():
            add_line(VALUE_BIAS, column_sum(value[...]))

        @pl.when(t == RESULT_AT - 1)
        def _():
            normed_load.start()
            weight_load(0).start()
            weight_load(1).start()
            repeat(0, 4, lambda at: branch_away(at).wait_recv())
            for load in piece_loads(0):
                load.start()

        @pl.when(between(RESULT_AT, 7))
        def _():
            result_rows(t - RESULT_AT)

        @pl.when(between(NORMED_AT, 12) & ((t - NORMED_AT) % 2 == 0))
        def _():
            normed_gradient((t - NORMED_AT) // 2)

        @pl.when(t == PAIR_AT)
        def _():
            loads[13].wait()
            pair_out[...] += dot_last(value[...], value_weight[...])
            pl.semaphore_wait(pair_free, 1)
            repeat(0, 4, lambda at: pair_copy(at).start())

        @pl.when(between(INPUT_AT, 7))
        def _():
            input_gradient(t - INPUT_AT)

        @pl.when(t == INPUT_AT + 7)
        def _():
            pair_done(False)

    small[...] = jnp.zeros_like(small)
    loads[0].wait()
    loads[1].wait()

    def attend(at):
        rows = span(at, PAIR_ROWS)
        pair_out[rows] = dot_plain(mixing[rows], output_weight[...])
        pair_copy(at).start()

    repeat(0, 4, attend)
    for number in range(2, 5):
        loads[number].wait()
    for number in range(7, 10):
        loads[number].wait()

    def mask(chunk):
        rows = span(chunk, 128)
        upstream = (live_of(chunk) * branch[rows].astype(f32)).astype(bf16)
        branch[rows] = upstream
        add_line(REDUCE_BIAS, column_sum(upstream))

    def second_norm(chunk):
        rows = span(chunk, 112)

        @pl.when(chunk % 2 == 0)
        def _():
            pair_copy(chunk // 2).wait_recv()

        total = tokens[rows].astype(f32) + ((pair_out[rows] + pair_in[rows]) + wide(output_bias))
        residual[rows] = total
        unit, _ = normalise(total)
        second[rows] = (unit * wide(second_gain) + wide(second_shift)).astype(bf16)

    def half_rows(half):
        repeat(4 * half, 4 * half + 4, second_norm)
        repeat(0, 4, lambda quarter: activate(quarter, half))

    for number in range(14, 17):
        loads[number].wait()
    repeat(0, 7, mask)
    loads[5].wait()
    loads[6].wait()
    repeat(0, 2, half_rows)
    pair_done(True)
    middle_save.start()

    def step(turn, carry):
        t = turn - 4

        def at_lag(lag):
            i = t - lag
            return i, (i >= 0) & (i < STEPS)

        @pl.when((turn >= 3) & (turn < STEPS + 3))
        def _():
            for copy in first_copies(turn - 3):
                copy.start()

        small_steps(t - SMALL_AT)

        i, alive = at_lag(5)

        @pl.when(alive)
        def _():
            slot = i % SLOTS
            for copy in last_copies(i):
                copy.wait()
            line_hop(*edge_line, i, 3)
            line_sent(*middle_line, i)
            line_sent(*edge_line, i)
            part = done.at[i % PARTS]
            part[0:EDGE] = edge[slot, z, 0]
            part[EDGE:FIRST] = middle[slot, z, y] + last_y[slot]
            part[FIRST : FIRST + EDGE] = edge[slot, z, 1]
            part[FIRST + EDGE : ROWS] = middle[slot, z, 2 + x] + last_x[slot]

            @pl.when(i % PARTS == PARTS - 1)
            def _():
                deliver(i // PARTS)
                for number, last in enumerate((1, 3, 7, 13, 14, 14)):

                    @pl.when(i // PARTS == last)
                    def _():
                        share_save(number).start()

        i, alive = at_lag(4)

        @pl.when(alive)
        def _():
            line_hop(*middle_line, i, 3)
            for copy in last_copies(i):
                copy.start()
            line_hop(*edge_line, i, 2)

        i, alive = at_lag(3)

        @pl.when(alive)
        def _():
            line_hop(*middle_line, i, 2)
            line_hop(*edge_line, i, 1)

        i, alive = at_lag(2)

        @pl.when(alive)
        def _():
            held, slot = home(i)
            line_hop(*middle_line, i, 1)
            for copy in next_copies(i):
                copy.wait()
            edge[slot, :, 0] = held[:, y, x, 0:EDGE] + next_y[slot]
            edge[slot, :, 1] = held[:, y, x, FIRST : FIRST + EDGE] + next_x[slot]
            line_hop(*edge_line, i, 0)

        i, alive = at_lag(1)

        @pl.when(alive)
        def _():
            held, slot = home(i)
            came = i % AHEAD
            for copy in first_copies(i):
                copy.wait()
            middle[slot, :, 0:2] = held[:, :, x, EDGE:FIRST] + first_x[came, :, :, EDGE:FIRST]
            middle[slot, :, 2:4] = (
                held[:, y, :, FIRST + EDGE : ROWS] + first_y[came, :, :, EDGE:FIRST]
            )
            line_hop(*middle_line, i, 0)
            held[:, :, x, 0:EDGE] += first_x[came, :, :, 0:EDGE]
            held[:, y, :, FIRST : FIRST + EDGE] += first_y[came, :, :, 0:EDGE]
            for copy in next_copies(i):
                copy.start()

        item, third = turn // PARTS, turn % PARTS

        whole = item == 4
        first = jnp.where(whole & (third < PARTS - 1), PARTS, jnp.where(whole, 0, third))

        @pl.when(item < ITEMS)
        def _():
            repeat(first, jnp.where(whole, PARTS, third + 1), lambda at: produce(item, at))

        layer_steps(t)
        return carry

    lax.fori_loop(0, STEPS + LAGS + 4, step, 0)
    for number in range(6):
        share_save(number).wait()


def layer_call(kept, pieces, cotangents, weights, lives, vectors):
    f32, bf16 = jnp.float32, jnp.bfloat16
    rows, features = 896, 768
    far, near = pl.BlockSpec(memory_space=pl.ANY), pl.BlockSpec(memory_space=pltpu.VMEM)
    narrow = HEADS * WIDTH
    pair, signal = pltpu.SemaphoreType.DMA((2, 2, SLOTS)), pltpu.SemaphoreType.DMA
    block = pltpu.VMEM((rows, features), bf16)
    slim = pltpu.VMEM((rows, narrow), bf16)
    tall = pltpu.VMEM((rows, features), f32)
    squares = [length for _, length in BUCKETS]
    shares = [jax.ShapeDtypeStruct((lines, 128), f32) for lines in (1728, 1152, 144, 144, 576, 576)]
    scratch = [
        *(pltpu.VMEM(member.shape, f32) for member in shares),
        *([pltpu.SMEM((1,), jnp.int32)] * 3),
        pltpu.VMEM((8, rows, features), bf16),
        block, block, block, block,
        pltpu.VMEM((features, rows), bf16),
        slim, slim, slim, slim,
        pltpu.VMEM((narrow, features), bf16),
        pltpu.VMEM((features, narrow), bf16),
        pltpu.VMEM((2, features, 512), bf16),
        pltpu.VMEM((2, rows, features), bf16),
        *(pltpu.VMEM((2, length, length), bf16) for length in squares),
        *(pltpu.VMEM((HEADS, length, length), bf16) for length in squares),
        pltpu.VMEM((2, rows, features), bf16),
        tall, tall, tall,
        pltpu.VMEM((2, PAIR_ROWS, features), f32),
        pltpu.VMEM((3, 128, features), f32),
        pltpu.VMEM((2, 128, features), bf16),
        pltpu.VMEM((3, PARTS, 4, 2, 2, ROWS, 128), f32),
        pltpu.VMEM((AHEAD, 4, 2, FIRST, 128), f32),
        pltpu.VMEM((AHEAD, 4, 2, FIRST, 128), f32),
        pltpu.VMEM((SLOTS, 4, EDGE, 128), f32),
        pltpu.VMEM((SLOTS, 4, EDGE, 128), f32),
        pltpu.VMEM((SLOTS, 4, 4, WIDE, 128), f32),
        pltpu.VMEM((SLOTS, 3, 4, WIDE, 128), f32),
        pltpu.VMEM((SLOTS, 3, 4, WIDE, 128), f32),
        pltpu.VMEM((SLOTS, 4, 2, EDGE, 128), f32),
        pltpu.VMEM((SLOTS, 3, 2, EDGE, 128), f32),
        pltpu.VMEM((SLOTS, 3, 2, EDGE, 128), f32),
        pltpu.VMEM((SLOTS, WIDE, 128), f32),
        pltpu.VMEM((SLOTS, WIDE, 128), f32),
        pltpu.VMEM((PARTS, ROWS, 128), f32),
        *([pltpu.VMEM((SMALL_ROWS, 128), f32)] * 4),
        pltpu.VMEM((4, SMALL_ROWS, 128), f32),
        signal((22,)), signal((2, 5)), signal((2,)), signal((2,)), signal((2, 4)), signal((2, 4)),
        signal((4,)), signal((3,)), signal((2,)),
        pltpu.SemaphoreType.DMA((2, 2, AHEAD)), pair, pair, pair, pair,
        signal((2, 4)), signal((6,)),
        pltpu.SemaphoreType.REGULAR,
    ]
    results = [jax.ShapeDtypeStruct(member.shape, bf16) for member in pieces] * 2
    sums = [
        jax.ShapeDtypeStruct(member, f32)
        for member in (
            (6, 128), (6, 128), (HEADS, features), (HEADS, 512), (3, 128),
            (6, 128), (6, 128), (6, 128), (12, 128), (6, 128),
        )
    ]
    spare = [jax.ShapeDtypeStruct((rows, features), f32)] * 3
    outs = pl.pallas_call(
        layer_kernel,
        out_shape=(*results, *shares, *sums, *spare),
        in_specs=[far] * 23 + [near] * 6,
        out_specs=(far,) * 12 + (near,) * 10 + (far,) * 3,
        scratch_shapes=scratch,
        compiler_params=pltpu.CompilerParams(
            collective_id=1, has_side_effects=True, vmem_limit_bytes=63 * 2**20
        ),
        name="layer_and_gradient_scatter",
    )(*kept, *pieces, *cotangents, *weights, *lives, *vectors)
    return outs[:22]


def copy_kernel(*refs):
    count = (len(refs) - 1) // 3
    sources, targets, rooms, sems = refs[:count], refs[count:2*count], refs[2*count:-1], refs[-1]
    loads = [
        pltpu.make_async_copy(source, room, sems.at[0, at])
        for at, (source, room) in enumerate(zip(sources, rooms))
    ]
    saves = [
        pltpu.make_async_copy(room, target, sems.at[1, at])
        for at, (room, target) in enumerate(zip(rooms, targets))
    ]
    for load in loads:
        load.start()
    for load, save in zip(loads, saves):
        load.wait()
        save.start()
    for save in saves:
        save.wait()


def copy_call(members):
    far = pl.BlockSpec(memory_space=pl.ANY)
    return pl.pallas_call(
        copy_kernel,
        out_shape=tuple(jax.ShapeDtypeStruct(member.shape, member.dtype) for member in members),
        in_specs=[far] * len(members),
        out_specs=(far,) * len(members),
        scratch_shapes=[
            *(pltpu.VMEM(member.shape, member.dtype) for member in members),
            pltpu.SemaphoreType.DMA((2, len(members))),
        ],
        name="copy_out",
    )(*members)


def lines(vector):
    return vector.reshape(-1, 128)


def grid_body(
    tokens_short,
    tokens_middle,
    tokens_long,
    live_short,
    live_middle,
    live_long,
    first_gain,
    first_shift,
    hidden_weight,
    hidden_bias,
    score_weight,
    score_bias,
    value_weight,
    value_bias,
    output_weight,
    output_bias,
    second_gain,
    second_shift,
    expand_weight,
    expand_bias,
    reduce_weight,
    reduce_bias,
    cotangent_short,
    cotangent_middle,
    cotangent_long,
):
    pieces = (tokens_short, tokens_middle, tokens_long)
    normed, hidden, slope, full_a, full_b, full_c, values, mixing = attention_forward_call(
        pieces, first_gain, first_shift, hidden_weight, hidden_bias, score_weight, score_bias,
        value_weight, value_bias,
    )
    outs = layer_call(
        (mixing, normed, values, hidden, slope, full_a, full_b, full_c),
        pieces,
        (cotangent_short, cotangent_middle, cotangent_long),
        (hidden_weight, score_weight, value_weight, output_weight, expand_weight, reduce_weight),
        (live_short, live_middle, live_long),
        (
            lines(first_gain), lines(output_bias), lines(second_gain), lines(second_shift),
            lines(expand_bias), lines(reduce_bias),
        ),
    )
    outs = copy_call(outs)
    hidden_share, score_share, value_share, output_share, expand_share, reduce_share = (
        member.reshape(-1) for member in outs[6:12]
    )
    sums = [
        member if member.shape[1] > 128 else member.reshape(-1) for member in outs[12:]
    ]
    return (
        *outs[:6],
        sums[0],
        sums[1],
        hidden_share,
        sums[2],
        score_share,
        sums[3],
        value_share,
        sums[4],
        output_share,
        *sums[5:8],
        expand_share,
        sums[8],
        reduce_share,
        sums[9],
    )


def plain_body(
    tokens_short,
    tokens_middle,
    tokens_long,
    live_short,
    live_middle,
    live_long,
    first_gain,
    first_shift,
    hidden_weight,
    hidden_bias,
    score_weight,
    score_bias,
    value_weight,
    value_bias,
    output_weight,
    output_bias,
    second_gain,
    second_shift,
    expand_weight,
    expand_bias,
    reduce_weight,
    reduce_bias,
    cotangent_short,
    cotangent_middle,
    cotangent_long,
):
    pieces = (tokens_short, tokens_middle, tokens_long)
    cotangents = (cotangent_short, cotangent_middle, cotangent_long)
    live_counts = (live_short, live_middle, live_long)
    features = tokens_short.shape[2]
    head_count = hidden_weight.shape[0]
    head_width = value_weight.shape[1] // head_count
    full_length = score_weight.shape[2]
    lengths = [piece.shape[1] for piece in pieces]
    slot_counts = [piece.shape[0] for piece in pieces]
    row_counts = [slot_counts[bucket] * lengths[bucket] for bucket in range(3)]
    row_starts = [0, row_counts[0], row_counts[0] + row_counts[1]]
    tokens = jnp.concatenate([piece.reshape(-1, features) for piece in pieces], axis=0)
    token_values = tokens.astype(jnp.float32)
    live_rows = jnp.concatenate(
        [
            live_flags(live_counts[bucket], slot_counts[bucket], lengths[bucket])
            for bucket in range(3)
        ]
    )[:, None]
    upstream = (
        jnp.concatenate([piece.reshape(-1, features) for piece in cotangents], axis=0).astype(
            jnp.float32
        )
        * live_rows
    )
    normed = layer_norm(token_values, first_gain, first_shift).astype(jnp.bfloat16)
    hidden_input = product("td,hde->hte", normed, hidden_weight) + hidden_bias[:, None, :]
    hidden_input, hidden = (hidden_input, jax.nn.gelu(hidden_input).astype(jnp.bfloat16))
    values = (product("td,dc->tc", normed, value_weight) + value_bias).astype(jnp.bfloat16)
    mixing_parts = []
    log_totals = []
    for bucket in range(3):
        length = lengths[bucket]
        row_start = row_starts[bucket]
        row_count = row_counts[bucket]
        slot_count = slot_counts[bucket]
        block_hidden = hidden[:, row_start : row_start + row_count]
        scores = (
            product("hnd,hdk->hnk", block_hidden, score_weight[:, :, :length])
            + score_bias[:, None, :length]
        )
        log_total = jax.nn.logsumexp(scores, axis=-1, keepdims=True)
        attention = (
            jnp.exp(scores - log_total)
            .astype(jnp.bfloat16)
            .reshape(head_count, slot_count, length, length)
        )
        block_values = values[row_start : row_start + row_count].reshape(
            slot_count, length, head_count, head_width
        )
        mixing = product("hsqk,skhe->sqhe", attention, block_values)
        mixing_parts.append(mixing.reshape(row_count, head_count * head_width).astype(jnp.bfloat16))
        log_totals.append(log_total)
    mixing = jnp.concatenate(mixing_parts, axis=0)
    attended = lax.psum(product("tc,cd->td", mixing, output_weight), "mp") + output_bias
    middle = token_values + attended
    second = layer_norm(middle, second_gain, second_shift).astype(jnp.bfloat16)
    expand_input = product("td,df->tf", second, expand_weight) + expand_bias
    activated = jax.nn.gelu(expand_input).astype(jnp.bfloat16)
    branch = lax.psum(product("tf,fd->td", activated, reduce_weight), "mp") + reduce_bias
    result = live_rows * (middle + branch)
    branch_gradient = upstream.astype(jnp.bfloat16)
    reduce_bias_gradient = jnp.sum(branch_gradient.astype(jnp.float32), axis=0)
    reduce_weight_gradient = product("tf,td->fd", activated, branch_gradient).reshape(-1)
    expand_gradient = gelu_backward(
        expand_input, product("td,fd->tf", branch_gradient, reduce_weight)
    ).astype(jnp.bfloat16)
    expand_bias_gradient = jnp.sum(expand_gradient.astype(jnp.float32), axis=0)
    expand_weight_gradient = product("tf,td->fd", expand_gradient, second).reshape(-1)
    second_gradient = lax.psum(product("tf,df->td", expand_gradient, expand_weight), "mp")
    middle_norm, second_gain_gradient, second_shift_gradient = jax.vjp(
        layer_norm, middle, second_gain, second_shift
    )[1](second_gradient)
    middle_gradient = upstream + middle_norm
    attended_gradient = middle_gradient.astype(jnp.bfloat16)
    output_bias_gradient = jnp.sum(attended_gradient.astype(jnp.float32), axis=0)
    output_weight_gradient = product("tc,td->cd", mixing, attended_gradient).reshape(-1)
    mixing_gradient = product("td,cd->tc", attended_gradient, output_weight).astype(jnp.bfloat16)
    score_weight_gradient = jnp.zeros(score_weight.shape, jnp.float32)
    score_bias_gradient = jnp.zeros(score_bias.shape, jnp.float32)
    hidden_parts = []
    value_parts = []
    for bucket in range(3):
        length = lengths[bucket]
        row_start = row_starts[bucket]
        row_count = row_counts[bucket]
        slot_count = slot_counts[bucket]
        block_hidden = hidden[:, row_start : row_start + row_count]
        block_weight = score_weight[:, :, :length]
        scores = product("hnd,hdk->hnk", block_hidden, block_weight) + score_bias[:, None, :length]
        softmax_full = jnp.exp(scores - log_totals[bucket])
        attention = softmax_full.astype(jnp.bfloat16).reshape(
            head_count, slot_count, length, length
        )
        block_values = values[row_start : row_start + row_count].reshape(
            slot_count, length, head_count, head_width
        )
        block_gradient = mixing_gradient[row_start : row_start + row_count].reshape(
            slot_count, length, head_count, head_width
        )
        attention_gradient = product("sqhe,skhe->hsqk", block_gradient, block_values).reshape(
            head_count, row_count, length
        )
        value_parts.append(
            product("hsqk,sqhe->skhe", attention, block_gradient).reshape(
                row_count, head_count * head_width
            )
        )
        score_gradient = softmax_full * (
            attention_gradient - jnp.sum(attention_gradient * softmax_full, axis=-1, keepdims=True)
        )
        score_gradient = score_gradient.astype(jnp.bfloat16)
        padding = full_length - length
        score_bias_gradient = score_bias_gradient + jnp.pad(
            jnp.sum(score_gradient.astype(jnp.float32), axis=1), ((0, 0), (0, padding))
        )
        score_weight_gradient = score_weight_gradient + jnp.pad(
            product("hnd,hnk->hdk", block_hidden, score_gradient), ((0, 0), (0, 0), (0, padding))
        )
        hidden_parts.append(product("hnk,hdk->hnd", score_gradient, block_weight))
    hidden_gradient = jnp.concatenate(hidden_parts, axis=1)
    value_gradient = jnp.concatenate(value_parts, axis=0).astype(jnp.bfloat16)
    value_bias_gradient = jnp.sum(value_gradient.astype(jnp.float32), axis=0)
    value_weight_gradient = product("tc,td->cd", value_gradient, normed).reshape(-1)
    input_gradient_hidden = gelu_backward(hidden_input, hidden_gradient).astype(jnp.bfloat16)
    hidden_bias_gradient = jnp.sum(input_gradient_hidden.astype(jnp.float32), axis=1)
    hidden_weight_gradient = product("td,hte->hde", normed, input_gradient_hidden).reshape(-1)
    score_weight_gradient = score_weight_gradient.reshape(-1)
    normed_part = product("hte,hde->td", input_gradient_hidden, hidden_weight) + product(
        "tc,dc->td", value_gradient, value_weight
    )
    normed_gradient = lax.psum(normed_part, "mp")
    input_norm, first_gain_gradient, first_shift_gradient = jax.vjp(
        layer_norm, token_values, first_gain, first_shift
    )[1](normed_gradient)
    input_gradient = middle_gradient + input_norm
    (
        hidden_weight_gradient,
        score_weight_gradient,
        value_weight_gradient,
        output_weight_gradient,
        expand_weight_gradient,
        reduce_weight_gradient,
    ) = (
        lax.psum_scatter(hidden_weight_gradient, "dp", scatter_dimension=0, tiled=True),
        lax.psum_scatter(score_weight_gradient, "dp", scatter_dimension=0, tiled=True),
        lax.psum_scatter(value_weight_gradient, "dp", scatter_dimension=0, tiled=True),
        lax.psum_scatter(output_weight_gradient, "dp", scatter_dimension=0, tiled=True),
        lax.psum_scatter(expand_weight_gradient, "dp", scatter_dimension=0, tiled=True),
        lax.psum_scatter(reduce_weight_gradient, "dp", scatter_dimension=0, tiled=True),
    )
    (
        first_gain_gradient,
        first_shift_gradient,
        hidden_bias_gradient,
        score_bias_gradient,
        value_bias_gradient,
        output_bias_gradient,
        second_gain_gradient,
        second_shift_gradient,
        expand_bias_gradient,
        reduce_bias_gradient,
    ) = lax.psum(
        (
            first_gain_gradient,
            first_shift_gradient,
            hidden_bias_gradient,
            score_bias_gradient,
            value_bias_gradient,
            output_bias_gradient,
            second_gain_gradient,
            second_shift_gradient,
            expand_bias_gradient,
            reduce_bias_gradient,
        ),
        "dp",
    )
    outputs = []
    gradients = []
    for bucket in range(3):
        row_start = row_starts[bucket]
        row_count = row_counts[bucket]
        outputs.append(
            result[row_start : row_start + row_count]
            .reshape(slot_counts[bucket], lengths[bucket], features)
            .astype(jnp.bfloat16)
        )
        gradients.append(
            input_gradient[row_start : row_start + row_count]
            .reshape(slot_counts[bucket], lengths[bucket], features)
            .astype(jnp.bfloat16)
        )
    return (
        outputs[0],
        outputs[1],
        outputs[2],
        gradients[0],
        gradients[1],
        gradients[2],
        first_gain_gradient,
        first_shift_gradient,
        hidden_weight_gradient,
        hidden_bias_gradient,
        score_weight_gradient,
        score_bias_gradient,
        value_weight_gradient,
        value_bias_gradient,
        output_weight_gradient,
        output_bias_gradient,
        second_gain_gradient,
        second_shift_gradient,
        expand_weight_gradient,
        expand_bias_gradient,
        reduce_weight_gradient,
        reduce_bias_gradient,
    )


def solution(mesh):
    placed = (
        P("dp", None, None),
        P("dp", None, None),
        P("dp", None, None),
        P("dp"),
        P("dp"),
        P("dp"),
        P(),
        P(),
        P("mp", None, None),
        P("mp", None),
        P("mp", None, None),
        P("mp", None),
        P(None, "mp"),
        P("mp"),
        P("mp", None),
        P(),
        P(),
        P(),
        P(None, "mp"),
        P("mp"),
        P("mp", None),
        P(),
        P("dp", None, None),
        P("dp", None, None),
        P("dp", None, None),
    )
    fits = mesh.shape["dp"] == 16 and mesh.shape["mp"] == 2
    return jax.shard_map(
        grid_body if fits else plain_body,
        mesh=mesh,
        in_specs=placed,
        out_specs=(
            P("dp", None, None),
            P("dp", None, None),
            P("dp", None, None),
            P("dp", None, None),
            P("dp", None, None),
            P("dp", None, None),
            P(),
            P(),
            P(("mp", "dp")),
            P("mp", None),
            P(("mp", "dp")),
            P("mp", None),
            P(("mp", "dp")),
            P("mp"),
            P(("mp", "dp")),
            P(),
            P(),
            P(),
            P(("mp", "dp")),
            P("mp"),
            P(("mp", "dp")),
            P(),
        ),
        check_vma=False,
    )
```

```python
import jax
import jax.numpy as jnp
from jax import lax
from jax.experimental import pallas as pl
from jax.experimental.pallas import tpu as pltpu
from jax.sharding import PartitionSpec as P

epsilon = 1e-05


def layer_norm(values, gains, offset):
    centred = values - jnp.mean(values, axis=-1, keepdims=True)
    variance = jnp.mean(centred * centred, axis=-1, keepdims=True)
    return centred * lax.rsqrt(variance + epsilon) * gains + offset


def product(form, left, right):
    return jnp.einsum(form, left, right, preferred_element_type=jnp.float32)


def gelu_backward(inputs, upstream):
    return jax.vjp(jax.nn.gelu, inputs)[1](upstream)[0]


def live_flags(count_array, slot_count, length):
    flags = (jnp.arange(slot_count) < count_array[0]).astype(jnp.float32)
    return jnp.repeat(flags, length)


BUCKETS = ((0, 128), (128, 256), (384, 512))
HEADS = 6
WIDTH = 64
ROOT = 0.7978845608028654
CUBE = 0.044715


def dot_rows(left, right):
    return lax.dot_general(
        left, right, (((0,), (0,)), ((), ())), preferred_element_type=jnp.float32
    )


def dot_last(left, right):
    return lax.dot_general(
        left, right, (((1,), (1,)), ((), ())), preferred_element_type=jnp.float32
    )


def dot_plain(left, right):
    return jnp.dot(left, right, preferred_element_type=jnp.float32)


def wide(lines):
    return jnp.concatenate([lines[at : at + 1] for at in range(lines.shape[0])], axis=1)


def normalise(rows):
    centred = rows - jnp.mean(rows, axis=-1, keepdims=True)
    scale = lax.rsqrt(jnp.mean(centred * centred, axis=-1, keepdims=True) + epsilon)
    return centred * scale, scale


def gelu_pair(inputs):
    square = inputs * inputs
    curve = jnp.tanh(inputs * (ROOT + ROOT * CUBE * square))
    half = 0.5 + 0.5 * curve
    gelu = inputs * half
    slope = half + (gelu * (1.0 - half)) * (2.0 * ROOT + 6.0 * ROOT * CUBE * square)
    return gelu, slope


SLOTS = 4
AHEAD = 8
ITEMS = 15
LAGS = 5
PARTS = 3
ROWS = 96
EDGE = 16
WIDE = 32
FIRST = EDGE + WIDE
STEPS = PARTS * ITEMS
PAIR_ROWS = 224
SMALL_ROWS = 112
FIRST_GAIN, FIRST_SHIFT, HIDDEN_BIAS, SCORE_BIAS, VALUE_BIAS = 0, 6, 12, 48, 72
OUTPUT_BIAS, SECOND_GAIN, SECOND_SHIFT, EXPAND_BIAS, REDUCE_BIAS = 75, 81, 87, 93, 105
SMALL_PLACES = (
    (FIRST_GAIN, 6), (FIRST_SHIFT, 6), (HIDDEN_BIAS, 36), (SCORE_BIAS, 24), (VALUE_BIAS, 3),
    (OUTPUT_BIAS, 6), (SECOND_GAIN, 6), (SECOND_SHIFT, 6), (EXPAND_BIAS, 12), (REDUCE_BIAS, 6),
)
BRANCH_AT, HEADS_AT, RESULT_AT, NORMED_AT, PAIR_AT, INPUT_AT, SMALL_AT = 2, 4, 11, 12, 24, 26, 34
MESH_ID = pl.DeviceIdType.MESH


def layer_kernel(
    tokens_a_h, tokens_b_h, tokens_c_h, branch_a_h, branch_b_h, branch_c_h,
    hidden_weight_h, score_weight_h, value_weight_h, output_weight_h, expand_weight_h,
    reduce_weight_h, live_a_h, live_b_h, live_c_h,
    first_gain, first_shift, hidden_bias, score_bias, value_bias, output_bias, second_gain,
    second_shift, expand_bias, reduce_bias,
    result_a, result_b, result_c, gradient_a, gradient_b, gradient_c,
    hidden_out_h, score_out_h, value_out_h, output_out_h, expand_out_h, reduce_out_h, *rest,
):
    small_out, rest = rest[:10], rest[10:]
    middle_h, branch_own_h, branch_far_h, hidden_h, slope_h, full_a_h, full_b_h, full_c_h = rest[:8]
    rest = rest[8:]
    (
        out_hidden, out_value, out_output, live_a, live_b, live_c,
        arena, normed, branch, second, attended, tokens, flipped, mixing, values, mixed, value,
        output_weight, value_weight, score_weight, slope, full_a, full_b, full_c,
        score_a, score_b, score_c, hidden, residual, pair_out, pair_in, stage, finished,
        own, first_x, first_y, next_x, next_y, middle, middle_up, middle_down,
        edge, edge_up, edge_down, last_x, last_y, done,
        small, small_x, small_sum, small_y, small_z,
        load_sems, front_sems, score_sems, keep_sems, head_sems, hidden_sems, weight_sems, pair_sems, far_sems, near_sems, piece_sems,
        finished_sems, first_sems, next_sems, middle_sems, edge_sems, last_sems, small_sems,
        share_sems, pair_free,
    ) = rest
    out_reduce, out_expand = out_hidden.at[0:576], out_hidden.at[576:1152]
    out_score = out_hidden.at[0:1152]
    f32, bf16 = jnp.float32, jnp.bfloat16
    spot = lax.axis_index("dp")
    x, y, z = spot % 2, (spot // 2) % 2, spot // 4
    to_x = {"dp": spot + 1 - 2 * x}
    to_y = {"dp": spot + 2 - 4 * y}
    to_up = {"dp": spot + 4}
    to_down = {"dp": spot - 4}
    to_mate = {"mp": 1 - lax.axis_index("mp")}

    loads = []
    for number, (source, target) in enumerate(
        (
            (tokens_a_h.at[0], tokens.at[0:128]), (tokens_b_h.at[0], tokens.at[128:384]),
            (tokens_c_h.at[0], tokens.at[384:896]), (value_weight_h, value_weight),
            (output_weight_h, output_weight),
            (expand_weight_h.at[:, 0:768], arena.at[6, 0:768]),
            (expand_weight_h.at[:, 768:1536], arena.at[7, 0:768]),
            (branch_a_h.at[0], branch.at[0:128]), (branch_b_h.at[0], branch.at[128:384]),
            (branch_c_h.at[0], branch.at[384:896]),
            (reduce_weight_h.at[0:768], arena.at[2, 0:768]),
            (reduce_weight_h.at[768:1536], arena.at[3, 0:768]),
            (live_a_h, live_a), (live_b_h, live_b), (live_c_h, live_c),
        )
    ):
        loads.append(pltpu.make_async_copy(source, target, load_sems.at[number]))
    middle_save = pltpu.make_async_copy(residual, middle_h, load_sems.at[15])

    def front_load(head):
        return pltpu.make_async_copy(
            hidden_weight_h.at[head], arena.at[head, 0:768], front_sems.at[head]
        )

    def score_load(turn):
        return pltpu.make_async_copy(
            score_weight_h.at[turn % HEADS], score_weight.at[turn % 2], score_sems.at[turn % 2]
        )

    def share_save(number):
        source, target = (
            (out_reduce, reduce_out_h), (out_expand, expand_out_h), (out_score, score_out_h),
            (out_hidden, hidden_out_h), (out_value, value_out_h), (out_output, output_out_h),
        )[number]
        return pltpu.make_async_copy(source, target, share_sems.at[number])

    def head_loads(head):
        slot = head % 2
        return [
            pltpu.make_async_copy(source.at[head], target.at[slot], head_sems.at[slot, number])
            for number, (source, target) in enumerate(
                (
                    (slope_h, slope), (full_a_h, full_a), (full_b_h, full_b), (full_c_h, full_c),
                    (score_weight_h, score_weight),
                )
            )
        ]

    def hidden_load(turn):
        slot = turn % 2
        return pltpu.make_async_copy(
            hidden_h.at[turn % HEADS], hidden.at[slot], hidden_sems.at[slot]
        )

    def weight_load(head):
        slot = head % 2
        return pltpu.make_async_copy(
            hidden_weight_h.at[head], arena.at[6 + slot, 0:768], weight_sems.at[slot]
        )

    for load in loads[0:4]:
        load.start()
    for number in (0, 1):
        front_load(number).start()
        score_load(number).start()
    for load in loads[4:10] + loads[12:15]:
        load.start()

    barrier = pltpu.get_barrier_semaphore()
    for device in (to_x, to_y, to_mate):
        pl.semaphore_signal(barrier, inc=1, device_id=device, device_id_type=MESH_ID)

    @pl.when(z < 3)
    def _():
        pl.semaphore_signal(barrier, inc=1, device_id=to_up, device_id_type=MESH_ID)

    @pl.when(z > 0)
    def _():
        pl.semaphore_signal(barrier, inc=1, device_id=to_down, device_id_type=MESH_ID)

    inner = (z > 0) & (z < 3)

    @pl.when(inner)
    def _():
        pl.semaphore_wait(barrier, 5)

    @pl.when(jnp.logical_not(inner))
    def _():
        pl.semaphore_wait(barrier, 4)

    def remote(source, target, sems, slot, device):
        return pltpu.make_async_remote_copy(
            src_ref=source,
            dst_ref=target,
            send_sem=sems.at[0, slot],
            recv_sem=sems.at[1, slot],
            device_id=device,
            device_id_type=MESH_ID,
        )

    def span(at, rows):
        return pl.ds(pl.multiple_of(at * rows, 16), rows)

    def repeat(first, last, body):
        def turn(at, carry):
            body(at)
            return carry

        lax.fori_loop(first, last, turn, 0)

    def pair_copy(at):
        rows = span(at, PAIR_ROWS)
        return remote(pair_out.at[rows], pair_in.at[rows], pair_sems, at, to_mate)

    def pair_ready(chunk):
        for at in range(4):

            @pl.when(chunk == (0, 1, 3, 5)[at])
            def _():
                pair_copy(at).wait_recv()

    def pair_done(spare):
        repeat(0, 4, lambda at: pair_copy(at).wait_send())
        if spare:
            pl.semaphore_signal(pair_free, inc=1, device_id=to_mate, device_id_type=MESH_ID)

    def live_of(chunk):
        count = jnp.where(chunk == 0, live_a[0], jnp.where(chunk < 3, live_b[0], live_c[0]))
        return jnp.where(count > 0, 1.0, 0.0).astype(f32)

    def add_line(row, line):
        for tile in range(line.shape[1] // 128):
            small[pl.ds(row + tile, 1)] += line[:, 128 * tile : 128 * tile + 128]

    def column_sum(block):
        return jnp.sum(block.astype(f32), axis=0, keepdims=True)

    def put(slot, dest, row, block):
        z_at, y_at, x_at = dest // 4, (dest // 2) % 2, dest % 2
        rows = block.shape[0]
        own[slot, row // ROWS, z_at, y_at, x_at, row % ROWS : row % ROWS + rows, :] = block

    def produce(item, third):
        slot = item % 3

        def feed_forward(left, right, column):
            columns = pl.ds(pl.multiple_of(column, 128), 384)

            def part(half):
                block = dot_rows(arena[left + half], right[:, columns])
                for piece in range(3):
                    for at in range(8):
                        own[slot, piece, 2 * half + at // 4, at // 2 % 2, at % 2] = block[
                            96 * at : 96 * at + 96, 128 * piece : 128 * piece + 128
                        ]

            repeat(0, 2, part)

        @pl.when(item < 2)
        def _():
            feed_forward(0, branch, 384 * item)

        @pl.when((item >= 2) & (item < 4))
        def _():
            feed_forward(4, second, 384 * (item - 2))

        def heads(block_of):
            def part(head):
                block = block_of(head)
                for piece in range(8):
                    unit = 8 * head + piece
                    own[slot, unit % 3, unit // 12, unit // 6 % 2, unit // 3 % 2] = block[
                        96 * piece : 96 * piece + 96
                    ]

            repeat(2 * third, 2 * third + 2, part)

        def score_heads(block_of):
            def part(head):
                turn = HEADS * (item - 4) + head
                hidden_load(turn).wait()
                return block_of(head, hidden.at[turn % 2])

            heads(part)

            for turn in (0, 1):
                after = HEADS * (item - 4) + 2 * third + 2 + turn

                @pl.when(after < 4 * HEADS)
                def _():
                    hidden_load(after).start()

        @pl.when(item == 4)
        def _():
            score_heads(
                lambda head, rows: dot_rows(rows[0:128], score_a[head])
                + dot_rows(rows[128:384], score_b[head, :, 0:128])
                + dot_rows(rows[384:896], score_c[head, :, 0:128])
            )

        @pl.when(item == 5)
        def _():
            score_heads(
                lambda head, rows: dot_rows(rows[128:384], score_b[head, :, 128:256])
                + dot_rows(rows[384:896], score_c[head, :, 128:256])
            )

        @pl.when((item == 6) | (item == 7))
        def _():
            column = pl.multiple_of(128 * (item - 4), 128)
            score_heads(
                lambda head, rows: dot_rows(rows[384:896], score_c[head, :, pl.ds(column, 128)])
            )

        @pl.when((item == 8) & (third == 0))
        def _():
            flipped[...] = normed[...].T

        @pl.when((item >= 8) & (item < 14))
        def _():
            column = pl.multiple_of(128 * (item - 8), 128)
            heads(lambda head: dot_plain(flipped[...], arena[head, :, pl.ds(column, 128)]))

        for part, (left, right) in enumerate(((value, normed), (mixing, attended))):

            @pl.when((item == 14) & (third == part))
            def _():
                block = dot_rows(left[...], right[...])
                for dest in range(16):
                    for piece in range(6):
                        put(
                            slot, dest, 144 * part + 24 * piece,
                            block[24 * dest : 24 * dest + 24, 128 * piece : 128 * piece + 128],
                        )

    def deliver(item):
        def spread(target, tiles, first):
            for part in range(PARTS):
                target[pl.ds(first + tiles * ROWS * part, ROWS, stride=tiles), :] = done[part]

        def stack(target, first):
            for part in range(PARTS):
                target[pl.ds(first + part, ROWS, stride=6), :] = done[part]

        for number, item_at in ((0, 4), (1, 4), (2, 8)):

            @pl.when(item == item_at)
            def _():
                share_save(number).wait()

        @pl.when(item < 2)
        def _():
            stack(out_reduce, 3 * item)

        @pl.when((item >= 2) & (item < 4))
        def _():
            stack(out_expand, 3 * (item - 2))

        @pl.when((item >= 4) & (item < 8))
        def _():
            spread(out_score, 4, item - 4)

        @pl.when((item >= 8) & (item < 14))
        def _():
            spread(out_hidden, 6, item - 8)

        @pl.when(item == 14)
        def _():
            for start, target in ((0, out_value), (144, out_output)):
                for piece in range(6):
                    row = start + 24 * piece
                    target[pl.ds(piece, 24, stride=6), :] = done[
                        row // ROWS, row % ROWS : row % ROWS + 24
                    ]

    def home(i):
        return own.at[(i // PARTS) % 3, i % PARTS], i % SLOTS

    def first_copies(i):
        held, slot = home(i)[0], i % AHEAD
        return (
            remote(held.at[:, :, 1 - x, 0:FIRST], first_x.at[slot], first_sems.at[0], slot, to_x),
            remote(held.at[:, 1 - y, :, FIRST:ROWS], first_y.at[slot], first_sems.at[1], slot, to_y),
        )

    def next_copies(i):
        held, slot = home(i)
        return (
            remote(held.at[:, y, 1 - x, FIRST : FIRST + EDGE], next_x.at[slot], next_sems.at[0], slot, to_x),
            remote(held.at[:, 1 - y, x, 0:EDGE], next_y.at[slot], next_sems.at[1], slot, to_y),
        )

    def last_copies(i):
        slot = i % SLOTS
        return (
            remote(middle.at[slot, z, 3 - x], last_x.at[slot], last_sems.at[0], slot, to_x),
            remote(middle.at[slot, z, 1 - y], last_y.at[slot], last_sems.at[1], slot, to_y),
        )

    def line_up(kept, landing, sems, slot, place):
        return remote(kept.at[slot, place + 1 : 4], landing.at[slot, place:3], sems.at[0], slot, to_up)

    def line_down(kept, landing, sems, slot, place):
        return remote(kept.at[slot, 0:place], landing.at[slot, 0:place], sems.at[1], slot, to_down)

    def line_hop(kept, landing_up, landing_down, sems, i, hop):
        slot = i % SLOTS
        for place in range(4):
            if place == hop:

                @pl.when(z == place)
                def _():
                    if place > 0:
                        line_up(kept, landing_up, sems, slot, place - 1).wait_recv()
                        kept[slot, place:4] += landing_up[slot, place - 1 : 3]
                    if place < 3:
                        line_up(kept, landing_up, sems, slot, place).start()

            if 3 - place == hop:

                @pl.when(z == place)
                def _():
                    if place < 3:
                        line_down(kept, landing_down, sems, slot, place + 1).wait_recv()
                        kept[slot, 0 : place + 1] += landing_down[slot, 0 : place + 1]
                    if place > 0:
                        line_down(kept, landing_down, sems, slot, place).start()

    def line_sent(kept, landing_up, landing_down, sems, i):
        slot = i % SLOTS
        for place in range(4):

            @pl.when(z == place)
            def _():
                if place < 3:
                    line_up(kept, landing_up, sems, slot, place).wait_send()
                if place > 0:
                    line_down(kept, landing_down, sems, slot, place).wait_send()

    middle_line = (middle, middle_up, middle_down, middle_sems)
    edge_line = (edge, edge_up, edge_down, edge_sems)

    def small_steps(t):
        def copy(number, source, target, device):
            return pltpu.make_async_remote_copy(
                src_ref=source, dst_ref=target, send_sem=small_sems.at[0, number],
                recv_sem=small_sems.at[1, number], device_id=device, device_id_type=MESH_ID,
            )

        over_x = copy(0, small, small_x, to_x)
        over_y = copy(1, small_sum, small_y, to_y)

        def up(place):
            part = small_z.at[0 : place + 1]
            return copy(2, part, part, to_up)

        def down(place):
            part = small_z.at[place:4]
            return copy(3, part, part, to_down)

        @pl.when(t == 0)
        def _():
            over_x.start()

        @pl.when(t == 1)
        def _():
            over_x.wait()
            small_sum[...] = small[...] + small_x[...]
            over_y.start()

        @pl.when(t == 2)
        def _():
            over_y.wait()
            small_z[z] = small_sum[...] + small_y[...]

        for place in range(4):

            @pl.when((z == place) & (t == 2 + place))
            def _():
                if place > 0:
                    up(place - 1).wait_recv()
                if place < 3:
                    up(place).start()

            @pl.when((z == place) & (t == 5 - place))
            def _():
                if place < 3:
                    down(place + 1).wait_recv()
                if place > 0:
                    down(place).start()

        @pl.when(t == 6)
        def _():
            small_sum[...] = ((small_z[0] + small_z[1]) + small_z[2]) + small_z[3]
            for (row, rows), target in zip(SMALL_PLACES, small_out):
                columns = target.shape[1] // 128
                for at in range(rows):
                    line, tile = at // columns, at % columns
                    target[line : line + 1, 128 * tile : 128 * tile + 128] = small_sum[
                        row + at : row + at + 1
                    ]
            for place in range(4):

                @pl.when(z == place)
                def _():
                    if place < 3:
                        up(place).wait_send()
                    if place > 0:
                        down(place).wait_send()

    def expand_of(quarter, rows):
        column = pl.multiple_of(quarter % 2 * 384, 128)
        bias = [expand_bias[pl.ds(3 * quarter + at, 1)] for at in range(3)]
        return dot_plain(
            second[rows], arena[6 + quarter // 2, 0:768, pl.ds(column, 384)]
        ) + jnp.concatenate(bias, axis=1)

    def activate(quarter, rows):
        gelu, _ = gelu_pair(expand_of(quarter, rows))
        column = pl.multiple_of(quarter % 2 * 384, 128)
        arena[quarter // 2, rows, pl.ds(column, 384)] = gelu.astype(bf16)

    def expand_gradient(turn):
        quarter, rows = turn // 2, span(turn % 2, 448)
        column = pl.multiple_of(quarter % 2 * 384, 128)
        _, steep = gelu_pair(expand_of(quarter, rows))
        spread = dot_last(branch[rows], arena[2 + quarter // 2, pl.ds(column, 384)])
        grown = (steep * spread).astype(bf16)
        arena[4 + quarter // 2, rows, pl.ds(column, 384)] = grown
        add_line(EXPAND_BIAS + 3 * quarter, column_sum(grown))

    def second_gradient(at):
        rows = span(at, PAIR_ROWS)
        pair_out[rows] = dot_last(arena[4, rows], arena[6, 0:768]) + dot_last(
            arena[5, rows], arena[7, 0:768]
        )
        pair_copy(at).start()

    def branch_away(at):
        return remote(
            stage.at[span(at % 2, PAIR_ROWS)], branch_far_h.at[span(at, PAIR_ROWS)], far_sems, at,
            to_mate,
        )

    def branch_save(at):
        return pltpu.make_async_copy(
            stage.at[span(at % 2, PAIR_ROWS)], branch_own_h.at[span(at, PAIR_ROWS)], near_sems.at[at]
        )

    def branch_sent(at):
        branch_away(at).wait_send()
        branch_save(at).wait()

    def branch_part(at):
        rows = span(at, PAIR_ROWS)

        @pl.when(at >= 2)
        def _():
            branch_sent(at - 2)

        stage[span(at % 2, PAIR_ROWS)] = dot_plain(arena[0, rows], arena[2, 0:768]) + dot_plain(
            arena[1, rows], arena[3, 0:768]
        )
        branch_away(at).start()
        branch_save(at).start()

    def middle_gradient(chunk):
        rows = span(chunk, 128)
        pair_ready(chunk)
        total = pair_out[rows] + pair_in[rows]
        unit, scale = normalise(residual[rows])
        add_line(SECOND_GAIN, column_sum(total * unit))
        add_line(SECOND_SHIFT, column_sum(total))
        scaled = total * wide(second_gain)
        mean = jnp.mean(scaled, axis=-1, keepdims=True)
        inner = jnp.mean(scaled * unit, axis=-1, keepdims=True)
        result = branch[rows].astype(f32) + (scaled - mean - unit * inner) * scale
        residual[rows] = result
        rounded = result.astype(bf16)
        attended[rows] = rounded
        add_line(OUTPUT_BIAS, column_sum(rounded))

    def head_gradient(head):
        slot, left = head % 2, head % 2 == 0
        both = pl.ds(pl.multiple_of(128 * (head // 2), 128), 128)

        @pl.when(head + 1 < HEADS)
        def _():
            for load in head_loads(head + 1):
                load.start()

        for load in head_loads(head):
            load.wait()
        for (start, length), full, score in zip(
            BUCKETS, (full_a, full_b, full_c), (score_a, score_b, score_c)
        ):
            rows = slice(start, start + length)

            def columns(member):
                pair = member[rows, both]
                return jnp.where(left, pair[:, 0:WIDTH], pair[:, WIDTH : 2 * WIDTH])

            attention = full[slot]
            softmax = attention.astype(f32)
            upstream = columns(mixed)
            attention_gradient = dot_last(upstream, columns(values))
            own_value = dot_rows(attention, upstream).astype(bf16)
            other = jnp.where(left, own_value, value[rows, both][:, 0:WIDTH])
            value[rows, both] = jnp.concatenate([other, own_value], axis=1)
            inner = jnp.sum(attention_gradient * softmax, axis=-1, keepdims=True)
            gradient = (softmax * (attention_gradient - inner)).astype(bf16)
            score[head] = gradient
            add_line(SCORE_BIAS + 4 * head, column_sum(gradient))
            spread = dot_last(gradient, score_weight[slot, :, 0:length])
            grown = (slope[slot, rows].astype(f32) * spread).astype(bf16)
            arena[head, rows] = grown
            add_line(HIDDEN_BIAS + 6 * head, column_sum(grown))

    def piece_loads(chunk):
        rows = span(chunk, 128)
        return [
            pltpu.make_async_copy(
                source.at[rows], stage.at[128 * at : 128 * at + 128], piece_sems.at[at]
            )
            for at, source in enumerate((middle_h, branch_own_h, branch_far_h))
        ]

    def finish(chunk, block, targets):
        def copy(number):
            bucket = (0, 1, 1, 2, 2, 2, 2)[number]
            row = 128 * (number - (0, 1, 3)[bucket])
            return pltpu.make_async_copy(
                finished.at[number % 2], targets[bucket].at[0, row : row + 128],
                finished_sems.at[number % 2],
            )

        for number in range(2, 7):

            @pl.when(chunk == number)
            def _():
                copy(number - 2).wait()

        finished[chunk % 2] = block.astype(bf16)
        for number in range(7):

            @pl.when(chunk == number)
            def _():
                copy(number).start()
                if number == 6:
                    copy(5).wait()
                    copy(6).wait()

    def result_rows(chunk):
        for load in piece_loads(chunk):
            load.wait()
        total = live_of(chunk) * (
            stage[0:128] + ((stage[128:256] + stage[256:384]) + wide(reduce_bias))
        )
        finish(chunk, total, (result_a, result_b, result_c))

        @pl.when(chunk < 6)
        def _():
            for load in piece_loads(chunk + 1):
                load.start()

    def normed_gradient(head):
        weight_load(head).wait()

        def part(half):
            rows = span(half, 448)
            block = dot_last(arena[head, rows], arena[6 + head % 2, 0:768])
            pair_out[rows] = jnp.where(head == 0, 0.0, pair_out[rows]) + block

        repeat(0, 2, part)

        @pl.when(head + 2 < HEADS)
        def _():
            weight_load(head + 2).start()

    def input_gradient(chunk):
        rows = span(chunk, 128)
        pair_ready(chunk)
        total = pair_out[rows] + pair_in[rows]
        unit, scale = normalise(tokens[rows].astype(f32))
        add_line(FIRST_GAIN, column_sum(total * unit))
        add_line(FIRST_SHIFT, column_sum(total))
        scaled = total * wide(first_gain)
        mean = jnp.mean(scaled, axis=-1, keepdims=True)
        inner = jnp.mean(scaled * unit, axis=-1, keepdims=True)
        result = residual[rows] + (scaled - mean - unit * inner) * scale
        finish(chunk, result, (gradient_a, gradient_b, gradient_c))

    def layer_steps(t):
        def between(first, count):
            return (t >= first) & (t < first + count)

        @pl.when(t == 0)
        def _():
            loads[10].wait()
            loads[11].wait()

        @pl.when(between(0, 2))
        def _():
            repeat(4 * t, 4 * t + 4, expand_gradient)

        @pl.when(t == 2)
        def _():
            pl.semaphore_wait(pair_free, 1)
            repeat(0, 4, second_gradient)

        @pl.when(between(BRANCH_AT, 2))
        def _():
            late = t - BRANCH_AT
            repeat(2 * late, 2 * late + 2, branch_part)

        @pl.when(t == BRANCH_AT + 1)
        def _():
            middle_save.wait()

        @pl.when(between(BRANCH_AT + 1, 2))
        def _():
            late = t - BRANCH_AT - 1
            repeat(4 * late, 4 + 3 * late, middle_gradient)

        @pl.when(t == BRANCH_AT + 2)
        def _():
            pair_done(True)
            mixed[...] = dot_last(attended[...], output_weight[...]).astype(bf16)
            repeat(2, 4, branch_sent)

        @pl.when(between(HEADS_AT, HEADS))
        def _():
            head_gradient(t - HEADS_AT)

        @pl.when(t == HEADS_AT + HEADS)
        def _():
            add_line(VALUE_BIAS, column_sum(value[...]))

        @pl.when(t == RESULT_AT - 1)
        def _():
            weight_load(0).start()
            weight_load(1).start()
            repeat(0, 4, lambda at: branch_away(at).wait_recv())
            for load in piece_loads(0):
                load.start()

        @pl.when(between(RESULT_AT, 7))
        def _():
            result_rows(t - RESULT_AT)

        @pl.when(between(NORMED_AT, 12) & ((t - NORMED_AT) % 2 == 0))
        def _():
            normed_gradient((t - NORMED_AT) // 2)

        @pl.when(t == PAIR_AT)
        def _():
            pair_out[...] += dot_last(value[...], value_weight[...])
            pl.semaphore_wait(pair_free, 1)
            repeat(0, 4, lambda at: pair_copy(at).start())

        @pl.when(between(INPUT_AT, 7))
        def _():
            input_gradient(t - INPUT_AT)

        @pl.when(t == INPUT_AT + 7)
        def _():
            pair_done(False)

    def first_norm(chunk):
        rows = span(chunk, 128)
        unit, _ = normalise(tokens[rows].astype(f32))
        normed[rows] = (unit * wide(first_gain) + wide(first_shift)).astype(bf16)

    def keep(turn, short, kind=""):
        head, slot = turn % HEADS, turn % 2
        rows = slice(0, 384) if short else slice(384, 896)
        pairs = [
            (hidden.at[slot, rows], hidden_h.at[head, rows]),
            (slope.at[slot, rows], slope_h.at[head, rows]),
        ]
        if short:
            pairs += [(full_a.at[slot], full_a_h.at[head]), (full_b.at[slot], full_b_h.at[head])]
        else:
            pairs += [(full_c.at[slot], full_c_h.at[head])]
        return [
            pltpu.make_async_copy(source, target, keep_sems.at[number, slot])
            for number, (source, target) in enumerate(pairs)
            if kind in ("", "rows" if number < 2 else "full")
        ]

    def front_head(turn, short):
        head, slot, left = turn % HEADS, turn % 2, turn % 2 == 0
        both = slice(128 * (head // 2), 128 * (head // 2) + 128)

        @pl.when(turn >= (HEADS + 2 if short else 2))
        def _():
            for copy in keep(turn - 2, short):
                copy.wait()

        if short:

            @pl.when(turn < HEADS + 2)
            def _():
                for copy in keep(turn - 2, False):
                    copy.wait()

        else:
            front_load(head).wait()

            @pl.when(head + 2 < HEADS)
            def _():
                front_load(head + 2).start()

        bias = hidden_bias[head : head + 1]
        for row in range(0, 384, 128) if short else range(384, 896, 128):
            rows = slice(row, row + 128)
            gelu, steep = gelu_pair(dot_plain(normed[rows], arena[head, 0:768]) + bias)
            hidden[slot, rows] = gelu.astype(bf16)
            slope[slot, rows] = steep.astype(bf16)
        for copy in keep(turn, short, "rows"):
            copy.start()
        score_load(turn).wait()
        fulls = (full_a, full_b, full_c)
        for bucket in (0, 1) if short else (2,):
            start, length = BUCKETS[bucket]
            rows = slice(start, start + length)
            scores = dot_plain(hidden[slot, rows], score_weight[slot, :, 0:length])
            scores = scores + score_bias[head : head + 1, 0:length]
            powers = jnp.exp(scores - jnp.max(scores, axis=-1, keepdims=True))
            softmax = powers * (1.0 / jnp.sum(powers, axis=-1, keepdims=True))
            attention = softmax.astype(bf16)
            fulls[bucket][slot] = attention
            pair = values[rows, both]
            own_values = pair[:, 0:WIDTH] if left else pair[:, WIDTH : 2 * WIDTH]
            mixture = dot_plain(attention, own_values).astype(bf16)
            mixing[rows, WIDTH * head : WIDTH * head + WIDTH] = mixture
        for copy in keep(turn, short, "full"):
            copy.start()

        @pl.when(turn + 2 < 2 * HEADS)
        def _():
            score_load(turn + 2).start()

    front_rows = (slice(384, 640), slice(640, 896), slice(0, 192), slice(192, 384))

    def front_copy(at):
        rows = front_rows[at]
        return remote(pair_out.at[rows], pair_in.at[rows], pair_sems, at, to_mate)

    def attend(at):
        rows = front_rows[at]
        pair_out[rows] = dot_plain(mixing[rows], output_weight[...])
        front_copy(at).start()

    def mask(chunk):
        rows = span(chunk, 128)
        upstream = (live_of(chunk) * branch[rows].astype(f32)).astype(bf16)
        branch[rows] = upstream
        add_line(REDUCE_BIAS, column_sum(upstream))

    def second_norm(chunk):
        rows = span(chunk, 128)
        for at in range(4):

            @pl.when(chunk == (3, 5, 0, 1)[at])
            def _():
                front_copy(at).wait_recv()

        total = tokens[rows].astype(f32) + ((pair_out[rows] + pair_in[rows]) + wide(output_bias))
        residual[rows] = total
        unit, _ = normalise(total)
        second[rows] = (unit * wide(second_gain) + wide(second_shift)).astype(bf16)

    small[...] = jnp.zeros_like(small)
    for load in loads[0:3]:
        load.wait()
    repeat(0, 7, first_norm)
    loads[3].wait()
    values[...] = (dot_plain(normed[...], value_weight[...]) + wide(value_bias)).astype(bf16)
    for turn in range(HEADS):
        front_head(turn, False)
    loads[4].wait()
    attend(0)
    attend(1)
    for turn in range(HEADS, 2 * HEADS):
        front_head(turn, True)
    attend(2)
    attend(3)
    for load in loads[10:12]:
        load.start()
    for load in loads[5:10] + loads[12:15]:
        load.wait()
    repeat(0, 7, mask)
    repeat(3, 7, second_norm)
    repeat(0, 4, lambda quarter: activate(quarter, slice(384, 896)))
    repeat(0, 3, second_norm)
    repeat(0, 4, lambda quarter: activate(quarter, slice(0, 384)))
    for at in range(4):
        front_copy(at).wait_send()
    pl.semaphore_signal(pair_free, inc=1, device_id=to_mate, device_id_type=MESH_ID)
    middle_save.start()
    for turn in (2 * HEADS - 2, 2 * HEADS - 1):
        for copy in keep(turn, True):
            copy.wait()
    for load in head_loads(0):
        load.start()
    for number in (0, 1):
        hidden_load(number).start()

    def step(turn, carry):
        t = turn - 5

        def at_lag(lag):
            i = t - lag
            return i, (i >= 0) & (i < STEPS)

        @pl.when((turn >= 3) & (turn < STEPS + 3))
        def _():
            for copy in first_copies(turn - 3):
                copy.start()

        small_steps(turn - 4 - SMALL_AT)

        i, alive = at_lag(5)

        @pl.when(alive)
        def _():
            slot = i % SLOTS
            for copy in last_copies(i):
                copy.wait()
            line_hop(*edge_line, i, 3)
            line_sent(*middle_line, i)
            line_sent(*edge_line, i)
            part = done.at[i % PARTS]
            part[0:EDGE] = edge[slot, z, 0]
            part[EDGE:FIRST] = middle[slot, z, y] + last_y[slot]
            part[FIRST : FIRST + EDGE] = edge[slot, z, 1]
            part[FIRST + EDGE : ROWS] = middle[slot, z, 2 + x] + last_x[slot]

            @pl.when(i % PARTS == PARTS - 1)
            def _():
                deliver(i // PARTS)
                for number, last in enumerate((1, 3, 7, 13, 14, 14)):

                    @pl.when(i // PARTS == last)
                    def _():
                        share_save(number).start()

        i, alive = at_lag(4)

        @pl.when(alive)
        def _():
            line_hop(*middle_line, i, 3)
            for copy in last_copies(i):
                copy.start()
            line_hop(*edge_line, i, 2)

        i, alive = at_lag(3)

        @pl.when(alive)
        def _():
            line_hop(*middle_line, i, 2)
            line_hop(*edge_line, i, 1)

        i, alive = at_lag(2)

        @pl.when(alive)
        def _():
            held, slot = home(i)
            line_hop(*middle_line, i, 1)
            for copy in next_copies(i):
                copy.wait()
            edge[slot, :, 0] = held[:, y, x, 0:EDGE] + next_y[slot]
            edge[slot, :, 1] = held[:, y, x, FIRST : FIRST + EDGE] + next_x[slot]
            line_hop(*edge_line, i, 0)

        i, alive = at_lag(1)

        @pl.when(alive)
        def _():
            held, slot = home(i)
            came = i % AHEAD
            for copy in first_copies(i):
                copy.wait()
            middle[slot, :, 0:2] = held[:, :, x, EDGE:FIRST] + first_x[came, :, :, EDGE:FIRST]
            middle[slot, :, 2:4] = (
                held[:, y, :, FIRST + EDGE : ROWS] + first_y[came, :, :, EDGE:FIRST]
            )
            line_hop(*middle_line, i, 0)
            held[:, :, x, 0:EDGE] += first_x[came, :, :, 0:EDGE]
            held[:, y, :, FIRST : FIRST + EDGE] += first_y[came, :, :, 0:EDGE]
            for copy in next_copies(i):
                copy.start()

        item, third = turn // PARTS, turn % PARTS

        once, late = item < 4, item == 4
        first = jnp.where(late & (third < PARTS - 1), PARTS, jnp.where(late, 0, third))
        last = jnp.where(late, PARTS, jnp.where(once & (third > 0), third, third + 1))

        @pl.when(item < ITEMS)
        def _():
            repeat(first, last, lambda at: produce(item, at))

        layer_steps(turn - 4)
        return carry

    lax.fori_loop(0, STEPS + LAGS + 5, step, 0)
    for number in range(3, 6):
        share_save(number).wait()


def layer_call(pieces, cotangents, weights, lives, vectors):
    f32, bf16 = jnp.float32, jnp.bfloat16
    rows, features = 896, 768
    far, near = pl.BlockSpec(memory_space=pl.ANY), pl.BlockSpec(memory_space=pltpu.VMEM)
    narrow = HEADS * WIDTH
    pair, signal = pltpu.SemaphoreType.DMA((2, 2, SLOTS)), pltpu.SemaphoreType.DMA
    block = pltpu.VMEM((rows, features), bf16)
    slim = pltpu.VMEM((rows, narrow), bf16)
    tall = pltpu.VMEM((rows, features), f32)
    squares = [length for _, length in BUCKETS]
    shares = [jax.ShapeDtypeStruct((lines, 128), f32) for lines in (1728, 1152, 144, 144, 576, 576)]
    scratch = [
        *(pltpu.VMEM((lines, 128), f32) for lines in (1728, 144, 144)),
        *([pltpu.SMEM((1,), jnp.int32)] * 3),
        pltpu.VMEM((8, rows, features), bf16),
        block, block, block, block, block,
        pltpu.VMEM((features, rows), bf16),
        slim, slim, slim, slim,
        pltpu.VMEM((narrow, features), bf16),
        pltpu.VMEM((features, narrow), bf16),
        pltpu.VMEM((2, features, 512), bf16),
        pltpu.VMEM((2, rows, features), bf16),
        *(pltpu.VMEM((2, length, length), bf16) for length in squares),
        *(pltpu.VMEM((HEADS, length, length), bf16) for length in squares),
        pltpu.VMEM((2, rows, features), bf16),
        tall, tall, tall,
        pltpu.VMEM((2 * PAIR_ROWS, features), f32),
        pltpu.VMEM((2, 128, features), bf16),
        pltpu.VMEM((3, PARTS, 4, 2, 2, ROWS, 128), f32),
        pltpu.VMEM((AHEAD, 4, 2, FIRST, 128), f32),
        pltpu.VMEM((AHEAD, 4, 2, FIRST, 128), f32),
        pltpu.VMEM((SLOTS, 4, EDGE, 128), f32),
        pltpu.VMEM((SLOTS, 4, EDGE, 128), f32),
        pltpu.VMEM((SLOTS, 4, 4, WIDE, 128), f32),
        pltpu.VMEM((SLOTS, 3, 4, WIDE, 128), f32),
        pltpu.VMEM((SLOTS, 3, 4, WIDE, 128), f32),
        pltpu.VMEM((SLOTS, 4, 2, EDGE, 128), f32),
        pltpu.VMEM((SLOTS, 3, 2, EDGE, 128), f32),
        pltpu.VMEM((SLOTS, 3, 2, EDGE, 128), f32),
        pltpu.VMEM((SLOTS, WIDE, 128), f32),
        pltpu.VMEM((SLOTS, WIDE, 128), f32),
        pltpu.VMEM((PARTS, ROWS, 128), f32),
        *([pltpu.VMEM((SMALL_ROWS, 128), f32)] * 4),
        pltpu.VMEM((4, SMALL_ROWS, 128), f32),
        signal((16,)), signal((HEADS,)), signal((2,)), signal((4, 2)), signal((2, 5)), signal((2,)), signal((2,)), signal((2, 4)), signal((2, 4)),
        signal((4,)), signal((3,)), signal((2,)),
        pltpu.SemaphoreType.DMA((2, 2, AHEAD)), pair, pair, pair, pair,
        signal((2, 4)), signal((6,)),
        pltpu.SemaphoreType.REGULAR,
    ]
    results = [jax.ShapeDtypeStruct(member.shape, bf16) for member in pieces] * 2
    sums = [
        jax.ShapeDtypeStruct(member, f32)
        for member in (
            (6, 128), (6, 128), (HEADS, features), (HEADS, 512), (3, 128),
            (6, 128), (6, 128), (6, 128), (12, 128), (6, 128),
        )
    ]
    spare = [jax.ShapeDtypeStruct((rows, features), f32)] * 3
    spare += [jax.ShapeDtypeStruct((HEADS, rows, features), bf16)] * 2
    spare += [jax.ShapeDtypeStruct((HEADS, length, length), bf16) for length in squares]
    outs = pl.pallas_call(
        layer_kernel,
        out_shape=(*results, *shares, *sums, *spare),
        in_specs=[far] * 15 + [near] * 10,
        out_specs=(far,) * 12 + (near,) * 10 + (far,) * 8,
        scratch_shapes=scratch,
        compiler_params=pltpu.CompilerParams(
            collective_id=1, has_side_effects=True, vmem_limit_bytes=63 * 2**20
        ),
        name="layer_and_gradient_scatter",
    )(*pieces, *cotangents, *weights, *lives, *vectors)
    return outs[:22]


def copy_kernel(*refs):
    count = (len(refs) - 1) // 3
    sources, targets, rooms, sems = refs[:count], refs[count:2*count], refs[2*count:-1], refs[-1]
    loads = [
        pltpu.make_async_copy(source, room, sems.at[0, at])
        for at, (source, room) in enumerate(zip(sources, rooms))
    ]
    saves = [
        pltpu.make_async_copy(room, target, sems.at[1, at])
        for at, (room, target) in enumerate(zip(rooms, targets))
    ]
    for load in loads:
        load.start()
    for load, save in zip(loads, saves):
        load.wait()
        save.start()
    for save in saves:
        save.wait()


def copy_call(members):
    far = pl.BlockSpec(memory_space=pl.ANY)
    return pl.pallas_call(
        copy_kernel,
        out_shape=tuple(jax.ShapeDtypeStruct(member.shape, member.dtype) for member in members),
        in_specs=[far] * len(members),
        out_specs=(far,) * len(members),
        scratch_shapes=[
            *(pltpu.VMEM(member.shape, member.dtype) for member in members),
            pltpu.SemaphoreType.DMA((2, len(members))),
        ],
        name="copy_out",
    )(*members)


def lines(vector):
    return vector.reshape(-1, 128)


def grid_body(
    tokens_short,
    tokens_middle,
    tokens_long,
    live_short,
    live_middle,
    live_long,
    first_gain,
    first_shift,
    hidden_weight,
    hidden_bias,
    score_weight,
    score_bias,
    value_weight,
    value_bias,
    output_weight,
    output_bias,
    second_gain,
    second_shift,
    expand_weight,
    expand_bias,
    reduce_weight,
    reduce_bias,
    cotangent_short,
    cotangent_middle,
    cotangent_long,
):
    pieces = (tokens_short, tokens_middle, tokens_long)
    outs = layer_call(
        pieces,
        (cotangent_short, cotangent_middle, cotangent_long),
        (hidden_weight, score_weight, value_weight, output_weight, expand_weight, reduce_weight),
        (live_short, live_middle, live_long),
        (
            lines(first_gain), lines(first_shift), hidden_bias, score_bias, lines(value_bias),
            lines(output_bias), lines(second_gain), lines(second_shift), lines(expand_bias),
            lines(reduce_bias),
        ),
    )
    outs = copy_call(outs)
    hidden_share, score_share, value_share, output_share, expand_share, reduce_share = (
        member.reshape(-1) for member in outs[6:12]
    )
    sums = [
        member if member.shape[1] > 128 else member.reshape(-1) for member in outs[12:]
    ]
    return (
        *outs[:6],
        sums[0],
        sums[1],
        hidden_share,
        sums[2],
        score_share,
        sums[3],
        value_share,
        sums[4],
        output_share,
        *sums[5:8],
        expand_share,
        sums[8],
        reduce_share,
        sums[9],
    )


def plain_body(
    tokens_short,
    tokens_middle,
    tokens_long,
    live_short,
    live_middle,
    live_long,
    first_gain,
    first_shift,
    hidden_weight,
    hidden_bias,
    score_weight,
    score_bias,
    value_weight,
    value_bias,
    output_weight,
    output_bias,
    second_gain,
    second_shift,
    expand_weight,
    expand_bias,
    reduce_weight,
    reduce_bias,
    cotangent_short,
    cotangent_middle,
    cotangent_long,
):
    pieces = (tokens_short, tokens_middle, tokens_long)
    cotangents = (cotangent_short, cotangent_middle, cotangent_long)
    live_counts = (live_short, live_middle, live_long)
    features = tokens_short.shape[2]
    head_count = hidden_weight.shape[0]
    head_width = value_weight.shape[1] // head_count
    full_length = score_weight.shape[2]
    lengths = [piece.shape[1] for piece in pieces]
    slot_counts = [piece.shape[0] for piece in pieces]
    row_counts = [slot_counts[bucket] * lengths[bucket] for bucket in range(3)]
    row_starts = [0, row_counts[0], row_counts[0] + row_counts[1]]
    tokens = jnp.concatenate([piece.reshape(-1, features) for piece in pieces], axis=0)
    token_values = tokens.astype(jnp.float32)
    live_rows = jnp.concatenate(
        [
            live_flags(live_counts[bucket], slot_counts[bucket], lengths[bucket])
            for bucket in range(3)
        ]
    )[:, None]
    upstream = (
        jnp.concatenate([piece.reshape(-1, features) for piece in cotangents], axis=0).astype(
            jnp.float32
        )
        * live_rows
    )
    normed = layer_norm(token_values, first_gain, first_shift).astype(jnp.bfloat16)
    hidden_input = product("td,hde->hte", normed, hidden_weight) + hidden_bias[:, None, :]
    hidden_input, hidden = (hidden_input, jax.nn.gelu(hidden_input).astype(jnp.bfloat16))
    values = (product("td,dc->tc", normed, value_weight) + value_bias).astype(jnp.bfloat16)
    mixing_parts = []
    log_totals = []
    for bucket in range(3):
        length = lengths[bucket]
        row_start = row_starts[bucket]
        row_count = row_counts[bucket]
        slot_count = slot_counts[bucket]
        block_hidden = hidden[:, row_start : row_start + row_count]
        scores = (
            product("hnd,hdk->hnk", block_hidden, score_weight[:, :, :length])
            + score_bias[:, None, :length]
        )
        log_total = jax.nn.logsumexp(scores, axis=-1, keepdims=True)
        attention = (
            jnp.exp(scores - log_total)
            .astype(jnp.bfloat16)
            .reshape(head_count, slot_count, length, length)
        )
        block_values = values[row_start : row_start + row_count].reshape(
            slot_count, length, head_count, head_width
        )
        mixing = product("hsqk,skhe->sqhe", attention, block_values)
        mixing_parts.append(mixing.reshape(row_count, head_count * head_width).astype(jnp.bfloat16))
        log_totals.append(log_total)
    mixing = jnp.concatenate(mixing_parts, axis=0)
    attended = lax.psum(product("tc,cd->td", mixing, output_weight), "mp") + output_bias
    middle = token_values + attended
    second = layer_norm(middle, second_gain, second_shift).astype(jnp.bfloat16)
    expand_input = product("td,df->tf", second, expand_weight) + expand_bias
    activated = jax.nn.gelu(expand_input).astype(jnp.bfloat16)
    branch = lax.psum(product("tf,fd->td", activated, reduce_weight), "mp") + reduce_bias
    result = live_rows * (middle + branch)
    branch_gradient = upstream.astype(jnp.bfloat16)
    reduce_bias_gradient = jnp.sum(branch_gradient.astype(jnp.float32), axis=0)
    reduce_weight_gradient = product("tf,td->fd", activated, branch_gradient).reshape(-1)
    expand_gradient = gelu_backward(
        expand_input, product("td,fd->tf", branch_gradient, reduce_weight)
    ).astype(jnp.bfloat16)
    expand_bias_gradient = jnp.sum(expand_gradient.astype(jnp.float32), axis=0)
    expand_weight_gradient = product("tf,td->fd", expand_gradient, second).reshape(-1)
    second_gradient = lax.psum(product("tf,df->td", expand_gradient, expand_weight), "mp")
    middle_norm, second_gain_gradient, second_shift_gradient = jax.vjp(
        layer_norm, middle, second_gain, second_shift
    )[1](second_gradient)
    middle_gradient = upstream + middle_norm
    attended_gradient = middle_gradient.astype(jnp.bfloat16)
    output_bias_gradient = jnp.sum(attended_gradient.astype(jnp.float32), axis=0)
    output_weight_gradient = product("tc,td->cd", mixing, attended_gradient).reshape(-1)
    mixing_gradient = product("td,cd->tc", attended_gradient, output_weight).astype(jnp.bfloat16)
    score_weight_gradient = jnp.zeros(score_weight.shape, jnp.float32)
    score_bias_gradient = jnp.zeros(score_bias.shape, jnp.float32)
    hidden_parts = []
    value_parts = []
    for bucket in range(3):
        length = lengths[bucket]
        row_start = row_starts[bucket]
        row_count = row_counts[bucket]
        slot_count = slot_counts[bucket]
        block_hidden = hidden[:, row_start : row_start + row_count]
        block_weight = score_weight[:, :, :length]
        scores = product("hnd,hdk->hnk", block_hidden, block_weight) + score_bias[:, None, :length]
        softmax_full = jnp.exp(scores - log_totals[bucket])
        attention = softmax_full.astype(jnp.bfloat16).reshape(
            head_count, slot_count, length, length
        )
        block_values = values[row_start : row_start + row_count].reshape(
            slot_count, length, head_count, head_width
        )
        block_gradient = mixing_gradient[row_start : row_start + row_count].reshape(
            slot_count, length, head_count, head_width
        )
        attention_gradient = product("sqhe,skhe->hsqk", block_gradient, block_values).reshape(
            head_count, row_count, length
        )
        value_parts.append(
            product("hsqk,sqhe->skhe", attention, block_gradient).reshape(
                row_count, head_count * head_width
            )
        )
        score_gradient = softmax_full * (
            attention_gradient - jnp.sum(attention_gradient * softmax_full, axis=-1, keepdims=True)
        )
        score_gradient = score_gradient.astype(jnp.bfloat16)
        padding = full_length - length
        score_bias_gradient = score_bias_gradient + jnp.pad(
            jnp.sum(score_gradient.astype(jnp.float32), axis=1), ((0, 0), (0, padding))
        )
        score_weight_gradient = score_weight_gradient + jnp.pad(
            product("hnd,hnk->hdk", block_hidden, score_gradient), ((0, 0), (0, 0), (0, padding))
        )
        hidden_parts.append(product("hnk,hdk->hnd", score_gradient, block_weight))
    hidden_gradient = jnp.concatenate(hidden_parts, axis=1)
    value_gradient = jnp.concatenate(value_parts, axis=0).astype(jnp.bfloat16)
    value_bias_gradient = jnp.sum(value_gradient.astype(jnp.float32), axis=0)
    value_weight_gradient = product("tc,td->cd", value_gradient, normed).reshape(-1)
    input_gradient_hidden = gelu_backward(hidden_input, hidden_gradient).astype(jnp.bfloat16)
    hidden_bias_gradient = jnp.sum(input_gradient_hidden.astype(jnp.float32), axis=1)
    hidden_weight_gradient = product("td,hte->hde", normed, input_gradient_hidden).reshape(-1)
    score_weight_gradient = score_weight_gradient.reshape(-1)
    normed_part = product("hte,hde->td", input_gradient_hidden, hidden_weight) + product(
        "tc,dc->td", value_gradient, value_weight
    )
    normed_gradient = lax.psum(normed_part, "mp")
    input_norm, first_gain_gradient, first_shift_gradient = jax.vjp(
        layer_norm, token_values, first_gain, first_shift
    )[1](normed_gradient)
    input_gradient = middle_gradient + input_norm
    (
        hidden_weight_gradient,
        score_weight_gradient,
        value_weight_gradient,
        output_weight_gradient,
        expand_weight_gradient,
        reduce_weight_gradient,
    ) = (
        lax.psum_scatter(hidden_weight_gradient, "dp", scatter_dimension=0, tiled=True),
        lax.psum_scatter(score_weight_gradient, "dp", scatter_dimension=0, tiled=True),
        lax.psum_scatter(value_weight_gradient, "dp", scatter_dimension=0, tiled=True),
        lax.psum_scatter(output_weight_gradient, "dp", scatter_dimension=0, tiled=True),
        lax.psum_scatter(expand_weight_gradient, "dp", scatter_dimension=0, tiled=True),
        lax.psum_scatter(reduce_weight_gradient, "dp", scatter_dimension=0, tiled=True),
    )
    (
        first_gain_gradient,
        first_shift_gradient,
        hidden_bias_gradient,
        score_bias_gradient,
        value_bias_gradient,
        output_bias_gradient,
        second_gain_gradient,
        second_shift_gradient,
        expand_bias_gradient,
        reduce_bias_gradient,
    ) = lax.psum(
        (
            first_gain_gradient,
            first_shift_gradient,
            hidden_bias_gradient,
            score_bias_gradient,
            value_bias_gradient,
            output_bias_gradient,
            second_gain_gradient,
            second_shift_gradient,
            expand_bias_gradient,
            reduce_bias_gradient,
        ),
        "dp",
    )
    outputs = []
    gradients = []
    for bucket in range(3):
        row_start = row_starts[bucket]
        row_count = row_counts[bucket]
        outputs.append(
            result[row_start : row_start + row_count]
            .reshape(slot_counts[bucket], lengths[bucket], features)
            .astype(jnp.bfloat16)
        )
        gradients.append(
            input_gradient[row_start : row_start + row_count]
            .reshape(slot_counts[bucket], lengths[bucket], features)
            .astype(jnp.bfloat16)
        )
    return (
        outputs[0],
        outputs[1],
        outputs[2],
        gradients[0],
        gradients[1],
        gradients[2],
        first_gain_gradient,
        first_shift_gradient,
        hidden_weight_gradient,
        hidden_bias_gradient,
        score_weight_gradient,
        score_bias_gradient,
        value_weight_gradient,
        value_bias_gradient,
        output_weight_gradient,
        output_bias_gradient,
        second_gain_gradient,
        second_shift_gradient,
        expand_weight_gradient,
        expand_bias_gradient,
        reduce_weight_gradient,
        reduce_bias_gradient,
    )


def solution(mesh):
    placed = (
        P("dp", None, None),
        P("dp", None, None),
        P("dp", None, None),
        P("dp"),
        P("dp"),
        P("dp"),
        P(),
        P(),
        P("mp", None, None),
        P("mp", None),
        P("mp", None, None),
        P("mp", None),
        P(None, "mp"),
        P("mp"),
        P("mp", None),
        P(),
        P(),
        P(),
        P(None, "mp"),
        P("mp"),
        P("mp", None),
        P(),
        P("dp", None, None),
        P("dp", None, None),
        P("dp", None, None),
    )
    fits = mesh.shape["dp"] == 16 and mesh.shape["mp"] == 2
    return jax.shard_map(
        grid_body if fits else plain_body,
        mesh=mesh,
        in_specs=placed,
        out_specs=(
            P("dp", None, None),
            P("dp", None, None),
            P("dp", None, None),
            P("dp", None, None),
            P("dp", None, None),
            P("dp", None, None),
            P(),
            P(),
            P(("mp", "dp")),
            P("mp", None),
            P(("mp", "dp")),
            P("mp", None),
            P(("mp", "dp")),
            P("mp"),
            P(("mp", "dp")),
            P(),
            P(),
            P(),
            P(("mp", "dp")),
            P("mp"),
            P(("mp", "dp")),
            P(),
        ),
        check_vma=False,
    )
```

```python
import jax
import jax.numpy as jnp
from jax import lax
from jax.experimental import pallas as pl
from jax.experimental.pallas import tpu as pltpu
from jax.sharding import PartitionSpec as P

epsilon = 1e-05


def layer_norm(values, gains, offset):
    centred = values - jnp.mean(values, axis=-1, keepdims=True)
    variance = jnp.mean(centred * centred, axis=-1, keepdims=True)
    return centred * lax.rsqrt(variance + epsilon) * gains + offset


def product(form, left, right):
    return jnp.einsum(form, left, right, preferred_element_type=jnp.float32)


def gelu_backward(inputs, upstream):
    return jax.vjp(jax.nn.gelu, inputs)[1](upstream)[0]


def live_flags(count_array, slot_count, length):
    flags = (jnp.arange(slot_count) < count_array[0]).astype(jnp.float32)
    return jnp.repeat(flags, length)


BUCKETS = ((0, 128), (128, 256), (384, 512))
HEADS = 6
WIDTH = 64
ROOT = 0.7978845608028654
CUBE = 0.044715


def dot_rows(left, right):
    return lax.dot_general(
        left, right, (((0,), (0,)), ((), ())), preferred_element_type=jnp.float32
    )


def dot_last(left, right):
    return lax.dot_general(
        left, right, (((1,), (1,)), ((), ())), preferred_element_type=jnp.float32
    )


def dot_plain(left, right):
    return jnp.dot(left, right, preferred_element_type=jnp.float32)


def wide(lines):
    return jnp.concatenate([lines[at : at + 1] for at in range(lines.shape[0])], axis=1)


def normalise(rows):
    centred = rows - jnp.mean(rows, axis=-1, keepdims=True)
    scale = lax.rsqrt(jnp.mean(centred * centred, axis=-1, keepdims=True) + epsilon)
    return centred * scale, scale


def gelu_pair(inputs):
    square = inputs * inputs
    curve = jnp.tanh(inputs * (ROOT + ROOT * CUBE * square))
    half = 0.5 + 0.5 * curve
    gelu = inputs * half
    slope = half + (gelu * (1.0 - half)) * (2.0 * ROOT + 6.0 * ROOT * CUBE * square)
    return gelu, slope


SLOTS = 4
AHEAD = 8
ITEMS = 15
LAGS = 5
PARTS = 3
ROWS = 96
EDGE = 16
WIDE = 32
FIRST = EDGE + WIDE
STEPS = PARTS * ITEMS
PAIR_ROWS = 224
SMALL_ROWS = 112
FIRST_GAIN, FIRST_SHIFT, HIDDEN_BIAS, SCORE_BIAS, VALUE_BIAS = 0, 6, 12, 48, 72
OUTPUT_BIAS, SECOND_GAIN, SECOND_SHIFT, EXPAND_BIAS, REDUCE_BIAS = 75, 81, 87, 93, 105
SMALL_PLACES = (
    (FIRST_GAIN, 6), (FIRST_SHIFT, 6), (HIDDEN_BIAS, 36), (SCORE_BIAS, 24), (VALUE_BIAS, 3),
    (OUTPUT_BIAS, 6), (SECOND_GAIN, 6), (SECOND_SHIFT, 6), (EXPAND_BIAS, 12), (REDUCE_BIAS, 6),
)
BRANCH_AT, HEADS_AT, RESULT_AT, NORMED_AT, PAIR_AT, INPUT_AT, SMALL_AT = 2, 4, 11, 12, 24, 26, 34
MESH_ID = pl.DeviceIdType.MESH


def layer_kernel(
    tokens_a_h, tokens_b_h, tokens_c_h, branch_a_h, branch_b_h, branch_c_h,
    hidden_weight_h, score_weight_h, value_weight_h, output_weight_h, expand_weight_h,
    reduce_weight_h, live_a_h, live_b_h, live_c_h,
    first_gain, first_shift, hidden_bias, score_bias, value_bias, output_bias, second_gain,
    second_shift, expand_bias, reduce_bias,
    result_a, result_b, result_c, gradient_a, gradient_b, gradient_c,
    hidden_out_h, score_out_h, value_out_h, output_out_h, expand_out_h, reduce_out_h, *rest,
):
    small_out, rest = rest[:10], rest[10:]
    middle_h, branch_own_h, branch_far_h, hidden_h, slope_h, full_a_h, full_b_h, full_c_h = rest[:8]
    rest = rest[8:]
    (
        out_hidden, out_value, out_output, live_a, live_b, live_c,
        arena, normed, branch, second, attended, tokens, flipped, mixing, values, mixed, value,
        output_weight, value_weight, score_weight, slope, full_a, full_b, full_c,
        score_a, score_b, score_c, hidden, residual, pair_out, pair_in, stage, finished,
        own, first_x, first_y, next_x, next_y, middle, middle_up, middle_down,
        edge, edge_up, edge_down, last_x, last_y, done,
        small, small_x, small_sum, small_y, small_z,
        load_sems, front_sems, score_sems, keep_sems, head_sems, hidden_sems, weight_sems, pair_sems, far_sems, near_sems, piece_sems,
        finished_sems, first_sems, next_sems, middle_sems, edge_sems, last_sems, small_sems,
        share_sems, tail_sems, pair_free,
    ) = rest
    out_reduce, out_expand = out_hidden.at[0:576], out_hidden.at[576:1152]
    out_score = out_hidden.at[0:1152]
    f32, bf16 = jnp.float32, jnp.bfloat16
    spot = lax.axis_index("dp")
    x, y, z = spot % 2, (spot // 2) % 2, spot // 4
    to_x = {"dp": spot + 1 - 2 * x}
    to_y = {"dp": spot + 2 - 4 * y}
    to_up = {"dp": spot + 4}
    to_down = {"dp": spot - 4}
    to_mate = {"mp": 1 - lax.axis_index("mp")}

    loads = []
    for number, (source, target) in enumerate(
        (
            (tokens_a_h.at[0], tokens.at[0:128]), (tokens_b_h.at[0], tokens.at[128:384]),
            (tokens_c_h.at[0], tokens.at[384:896]), (value_weight_h, value_weight),
            (output_weight_h, output_weight),
            (expand_weight_h.at[:, 0:768], arena.at[6, 0:768]),
            (expand_weight_h.at[:, 768:1536], arena.at[7, 0:768]),
            (branch_a_h.at[0], branch.at[0:128]), (branch_b_h.at[0], branch.at[128:384]),
            (branch_c_h.at[0], branch.at[384:896]),
            (reduce_weight_h.at[0:768], arena.at[2, 0:768]),
            (reduce_weight_h.at[768:1536], arena.at[3, 0:768]),
            (live_a_h, live_a), (live_b_h, live_b), (live_c_h, live_c),
        )
    ):
        loads.append(pltpu.make_async_copy(source, target, load_sems.at[number]))
    middle_save = pltpu.make_async_copy(residual, middle_h, load_sems.at[15])

    def front_load(head):
        return pltpu.make_async_copy(
            hidden_weight_h.at[head], arena.at[head, 0:768], front_sems.at[head]
        )

    def score_load(turn):
        return pltpu.make_async_copy(
            score_weight_h.at[turn % HEADS], score_weight.at[turn % 2], score_sems.at[turn % 2]
        )

    def share_save(number):
        source, target = (
            (out_reduce, reduce_out_h), (out_expand, expand_out_h), (out_score, score_out_h),
            (out_hidden, hidden_out_h), (out_value, value_out_h), (out_output, output_out_h),
        )[number]
        return pltpu.make_async_copy(source, target, share_sems.at[number])

    def head_loads(head):
        slot = head % 2
        return [
            pltpu.make_async_copy(source.at[head], target.at[slot], head_sems.at[slot, number])
            for number, (source, target) in enumerate(
                (
                    (slope_h, slope), (full_a_h, full_a), (full_b_h, full_b), (full_c_h, full_c),
                    (score_weight_h, score_weight),
                )
            )
        ]

    def hidden_load(turn, first):
        slot, rows = turn % 2, slice(first, 896)
        return pltpu.make_async_copy(
            hidden_h.at[turn % HEADS, rows], hidden.at[slot, rows], hidden_sems.at[slot]
        )

    def weight_load(head):
        slot = head % 2
        return pltpu.make_async_copy(
            hidden_weight_h.at[head], arena.at[6 + slot, 0:768], weight_sems.at[slot]
        )

    for load in loads[0:4]:
        load.start()
    for number in (0, 1):
        front_load(number).start()
        score_load(number).start()
    for load in loads[4:10] + loads[12:15]:
        load.start()

    barrier = pltpu.get_barrier_semaphore()
    for device in (to_x, to_y, to_mate):
        pl.semaphore_signal(barrier, inc=1, device_id=device, device_id_type=MESH_ID)

    @pl.when(z < 3)
    def _():
        pl.semaphore_signal(barrier, inc=1, device_id=to_up, device_id_type=MESH_ID)

    @pl.when(z > 0)
    def _():
        pl.semaphore_signal(barrier, inc=1, device_id=to_down, device_id_type=MESH_ID)

    inner = (z > 0) & (z < 3)

    @pl.when(inner)
    def _():
        pl.semaphore_wait(barrier, 5)

    @pl.when(jnp.logical_not(inner))
    def _():
        pl.semaphore_wait(barrier, 4)

    def remote(source, target, sems, slot, device):
        return pltpu.make_async_remote_copy(
            src_ref=source,
            dst_ref=target,
            send_sem=sems.at[0, slot],
            recv_sem=sems.at[1, slot],
            device_id=device,
            device_id_type=MESH_ID,
        )

    def span(at, rows):
        return pl.ds(pl.multiple_of(at * rows, 16), rows)

    def repeat(first, last, body):
        def turn(at, carry):
            body(at)
            return carry

        lax.fori_loop(first, last, turn, 0)

    def pair_copy(at):
        rows = span(at, PAIR_ROWS)
        return remote(pair_out.at[rows], pair_in.at[rows], pair_sems, at, to_mate)

    def pair_ready(chunk):
        for at in range(4):

            @pl.when(chunk == (0, 1, 3, 5)[at])
            def _():
                pair_copy(at).wait_recv()

    def pair_done(spare):
        repeat(0, 4, lambda at: pair_copy(at).wait_send())
        if spare:
            pl.semaphore_signal(pair_free, inc=1, device_id=to_mate, device_id_type=MESH_ID)

    def live_of(chunk):
        count = jnp.where(chunk == 0, live_a[0], jnp.where(chunk < 3, live_b[0], live_c[0]))
        return jnp.where(count > 0, 1.0, 0.0).astype(f32)

    def add_line(row, line):
        for tile in range(line.shape[1] // 128):
            small[pl.ds(row + tile, 1)] += line[:, 128 * tile : 128 * tile + 128]

    def column_sum(block):
        return jnp.sum(block.astype(f32), axis=0, keepdims=True)

    def put(slot, dest, row, block):
        z_at, y_at, x_at = dest // 4, (dest // 2) % 2, dest % 2
        rows = block.shape[0]
        own[slot, row // ROWS, z_at, y_at, x_at, row % ROWS : row % ROWS + rows, :] = block

    def produce(item, third):
        slot = item % 3

        def feed_forward(left, right, column):
            columns = pl.ds(pl.multiple_of(column, 128), 384)

            def part(half):
                block = dot_rows(arena[left + half], right[:, columns])
                for piece in range(3):
                    for at in range(8):
                        own[slot, piece, 2 * half + at // 4, at // 2 % 2, at % 2] = block[
                            96 * at : 96 * at + 96, 128 * piece : 128 * piece + 128
                        ]

            repeat(0, 2, part)

        @pl.when(item < 2)
        def _():
            feed_forward(0, branch, 384 * item)

        @pl.when((item >= 2) & (item < 4))
        def _():
            feed_forward(4, second, 384 * (item - 2))

        def heads(block_of):
            def part(head):
                block = block_of(head)
                for piece in range(8):
                    unit = 8 * head + piece
                    own[slot, unit % 3, unit // 12, unit // 6 % 2, unit // 3 % 2] = block[
                        96 * piece : 96 * piece + 96
                    ]

            repeat(2 * third, 2 * third + 2, part)

        def score_heads(start, block_of):
            def part(head):
                turn = HEADS * (item - 4) + head
                hidden_load(turn, start).wait()
                return block_of(head, hidden.at[turn % 2])

            heads(part)

            for turn in (0, 1):
                after = HEADS * (item - 4) + 2 * third + 2 + turn

                for low, high, rows in ((0, 1, 0), (1, 2, 128), (2, 4, 384)):

                    @pl.when((after >= HEADS * low) & (after < HEADS * high))
                    def _():
                        hidden_load(after, rows).start()

        @pl.when(item == 4)
        def _():
            score_heads(
                0,
                lambda head, rows: dot_rows(rows[0:128], score_a[head])
                + dot_rows(rows[128:384], score_b[head, :, 0:128])
                + dot_rows(rows[384:896], score_c[head, :, 0:128])
            )

        @pl.when(item == 5)
        def _():
            score_heads(
                128,
                lambda head, rows: dot_rows(rows[128:384], score_b[head, :, 128:256])
                + dot_rows(rows[384:896], score_c[head, :, 128:256])
            )

        @pl.when((item == 6) | (item == 7))
        def _():
            column = pl.multiple_of(128 * (item - 4), 128)
            score_heads(
                384,
                lambda head, rows: dot_rows(rows[384:896], score_c[head, :, pl.ds(column, 128)]),
            )

        @pl.when((item == 8) & (third == 0))
        def _():
            flipped[...] = normed[...].T

        @pl.when((item >= 8) & (item < 14))
        def _():
            column = pl.multiple_of(128 * (item - 8), 128)
            heads(lambda head: dot_plain(flipped[...], arena[head, :, pl.ds(column, 128)]))

        for part, (left, right) in enumerate(((value, normed), (mixing, attended))):

            @pl.when((item == 14) & (third == part))
            def _():
                block = dot_rows(left[...], right[...])
                for dest in range(16):
                    for piece in range(6):
                        put(
                            slot, dest, 144 * part + 24 * piece,
                            block[24 * dest : 24 * dest + 24, 128 * piece : 128 * piece + 128],
                        )

    def deliver(item):
        def spread(target, tiles, first):
            for part in range(PARTS):
                target[pl.ds(first + tiles * ROWS * part, ROWS, stride=tiles), :] = done[part]

        def stack(target, first):
            for part in range(PARTS):
                target[pl.ds(first + part, ROWS, stride=6), :] = done[part]

        for number, item_at in ((0, 4), (1, 4), (2, 8)):

            @pl.when(item == item_at)
            def _():
                share_save(number).wait()

        @pl.when(item < 2)
        def _():
            stack(out_reduce, 3 * item)

        @pl.when((item >= 2) & (item < 4))
        def _():
            stack(out_expand, 3 * (item - 2))

        @pl.when((item >= 4) & (item < 8))
        def _():
            spread(out_score, 4, item - 4)

        @pl.when((item >= 8) & (item < 14))
        def _():
            spread(out_hidden, 6, item - 8)

        @pl.when(item == 14)
        def _():
            for start, target in ((0, out_value), (144, out_output)):
                for piece in range(6):
                    row = start + 24 * piece
                    target[pl.ds(piece, 24, stride=6), :] = done[
                        row // ROWS, row % ROWS : row % ROWS + 24
                    ]

    def home(i):
        return own.at[(i // PARTS) % 3, i % PARTS], i % SLOTS

    def first_copies(i):
        held, slot = home(i)[0], i % AHEAD
        return (
            remote(held.at[:, :, 1 - x, 0:FIRST], first_x.at[slot], first_sems.at[0], slot, to_x),
            remote(held.at[:, 1 - y, :, FIRST:ROWS], first_y.at[slot], first_sems.at[1], slot, to_y),
        )

    def next_copies(i):
        held, slot = home(i)
        return (
            remote(held.at[:, y, 1 - x, FIRST : FIRST + EDGE], next_x.at[slot], next_sems.at[0], slot, to_x),
            remote(held.at[:, 1 - y, x, 0:EDGE], next_y.at[slot], next_sems.at[1], slot, to_y),
        )

    def last_copies(i):
        slot = i % SLOTS
        return (
            remote(middle.at[slot, z, 3 - x], last_x.at[slot], last_sems.at[0], slot, to_x),
            remote(middle.at[slot, z, 1 - y], last_y.at[slot], last_sems.at[1], slot, to_y),
        )

    def line_up(kept, landing, sems, slot, place):
        return remote(kept.at[slot, place + 1 : 4], landing.at[slot, place:3], sems.at[0], slot, to_up)

    def line_down(kept, landing, sems, slot, place):
        return remote(kept.at[slot, 0:place], landing.at[slot, 0:place], sems.at[1], slot, to_down)

    def line_hop(kept, landing_up, landing_down, sems, i, hop):
        slot = i % SLOTS
        for place in range(4):
            if place == hop:

                @pl.when(z == place)
                def _():
                    if place > 0:
                        line_up(kept, landing_up, sems, slot, place - 1).wait_recv()
                        kept[slot, place:4] += landing_up[slot, place - 1 : 3]
                    if place < 3:
                        line_up(kept, landing_up, sems, slot, place).start()

            if 3 - place == hop:

                @pl.when(z == place)
                def _():
                    if place < 3:
                        line_down(kept, landing_down, sems, slot, place + 1).wait_recv()
                        kept[slot, 0 : place + 1] += landing_down[slot, 0 : place + 1]
                    if place > 0:
                        line_down(kept, landing_down, sems, slot, place).start()

    def line_sent(kept, landing_up, landing_down, sems, i):
        slot = i % SLOTS
        for place in range(4):

            @pl.when(z == place)
            def _():
                if place < 3:
                    line_up(kept, landing_up, sems, slot, place).wait_send()
                if place > 0:
                    line_down(kept, landing_down, sems, slot, place).wait_send()

    def tail_up(slot, dest):
        return remote(middle.at[slot, dest], middle_up.at[slot, dest - 1], tail_sems.at[0], dest, to_up)

    def tail_down(slot, dest):
        return remote(middle.at[slot, dest], middle_down.at[slot, dest], tail_sems.at[1], dest, to_down)

    def tail_hop(i, hop):
        slot = i % SLOTS
        for place in range(4):
            if place == hop:

                @pl.when(z == place)
                def _():
                    for dest in range(3, place - 1, -1):
                        if place > 0:
                            tail_up(slot, dest).wait_recv()
                            middle[slot, dest] += middle_up[slot, dest - 1]
                        if dest > place:
                            tail_up(slot, dest).start()

            if 3 - place == hop:

                @pl.when(z == place)
                def _():
                    for dest in range(0, place + 1):
                        if place < 3:
                            tail_down(slot, dest).wait_recv()
                            middle[slot, dest] += middle_down[slot, dest]
                        if dest < place:
                            tail_down(slot, dest).start()

    def tail_sent(i):
        slot = i % SLOTS
        for place in range(4):

            @pl.when(z == place)
            def _():
                for dest in range(place + 1, 4):
                    tail_up(slot, dest).wait_send()
                for dest in range(0, place):
                    tail_down(slot, dest).wait_send()

    def middle_hop(i, hop):
        @pl.when(i < STEPS - 1)
        def _():
            line_hop(*middle_line, i, hop)

        @pl.when(i == STEPS - 1)
        def _():
            tail_hop(i, hop)

    def middle_sent(i):
        @pl.when(i < STEPS - 1)
        def _():
            line_sent(*middle_line, i)

        @pl.when(i == STEPS - 1)
        def _():
            tail_sent(i)

    middle_line = (middle, middle_up, middle_down, middle_sems)
    edge_line = (edge, edge_up, edge_down, edge_sems)

    def small_steps(t):
        def copy(number, source, target, device):
            return pltpu.make_async_remote_copy(
                src_ref=source, dst_ref=target, send_sem=small_sems.at[0, number],
                recv_sem=small_sems.at[1, number], device_id=device, device_id_type=MESH_ID,
            )

        over_x = copy(0, small, small_x, to_x)
        over_y = copy(1, small_sum, small_y, to_y)

        def up(place):
            part = small_z.at[0 : place + 1]
            return copy(2, part, part, to_up)

        def down(place):
            part = small_z.at[place:4]
            return copy(3, part, part, to_down)

        @pl.when(t == 0)
        def _():
            over_x.start()

        @pl.when(t == 1)
        def _():
            over_x.wait()
            small_sum[...] = small[...] + small_x[...]
            over_y.start()

        @pl.when(t == 2)
        def _():
            over_y.wait()
            small_z[z] = small_sum[...] + small_y[...]

        for place in range(4):

            @pl.when((z == place) & (t == 2 + place))
            def _():
                if place > 0:
                    up(place - 1).wait_recv()
                if place < 3:
                    up(place).start()

            @pl.when((z == place) & (t == 5 - place))
            def _():
                if place < 3:
                    down(place + 1).wait_recv()
                if place > 0:
                    down(place).start()

        @pl.when(t == 6)
        def _():
            small_sum[...] = ((small_z[0] + small_z[1]) + small_z[2]) + small_z[3]
            for (row, rows), target in zip(SMALL_PLACES, small_out):
                columns = target.shape[1] // 128
                for at in range(rows):
                    line, tile = at // columns, at % columns
                    target[line : line + 1, 128 * tile : 128 * tile + 128] = small_sum[
                        row + at : row + at + 1
                    ]
            for place in range(4):

                @pl.when(z == place)
                def _():
                    if place < 3:
                        up(place).wait_send()
                    if place > 0:
                        down(place).wait_send()

    def expand_of(quarter, rows):
        column = pl.multiple_of(quarter % 2 * 384, 128)
        bias = [expand_bias[pl.ds(3 * quarter + at, 1)] for at in range(3)]
        return dot_plain(
            second[rows], arena[6 + quarter // 2, 0:768, pl.ds(column, 384)]
        ) + jnp.concatenate(bias, axis=1)

    def activate(quarter, rows):
        gelu, _ = gelu_pair(expand_of(quarter, rows))
        column = pl.multiple_of(quarter % 2 * 384, 128)
        arena[quarter // 2, rows, pl.ds(column, 384)] = gelu.astype(bf16)

    def expand_gradient(turn):
        quarter, rows = turn // 2, span(turn % 2, 448)
        column = pl.multiple_of(quarter % 2 * 384, 128)
        _, steep = gelu_pair(expand_of(quarter, rows))
        spread = dot_last(branch[rows], arena[2 + quarter // 2, pl.ds(column, 384)])
        grown = (steep * spread).astype(bf16)
        arena[4 + quarter // 2, rows, pl.ds(column, 384)] = grown
        add_line(EXPAND_BIAS + 3 * quarter, column_sum(grown))

    def second_gradient(at):
        rows = span(at, PAIR_ROWS)
        pair_out[rows] = dot_last(arena[4, rows], arena[6, 0:768]) + dot_last(
            arena[5, rows], arena[7, 0:768]
        )
        pair_copy(at).start()

    def branch_away(at):
        return remote(
            stage.at[span(at % 2, PAIR_ROWS)], branch_far_h.at[span(at, PAIR_ROWS)], far_sems, at,
            to_mate,
        )

    def branch_save(at):
        return pltpu.make_async_copy(
            stage.at[span(at % 2, PAIR_ROWS)], branch_own_h.at[span(at, PAIR_ROWS)], near_sems.at[at]
        )

    def branch_sent(at):
        branch_away(at).wait_send()
        branch_save(at).wait()

    def branch_part(at):
        rows = span(at, PAIR_ROWS)

        @pl.when(at >= 2)
        def _():
            branch_sent(at - 2)

        stage[span(at % 2, PAIR_ROWS)] = dot_plain(arena[0, rows], arena[2, 0:768]) + dot_plain(
            arena[1, rows], arena[3, 0:768]
        )
        branch_away(at).start()
        branch_save(at).start()

    def middle_gradient(chunk):
        rows = span(chunk, 128)
        pair_ready(chunk)
        total = pair_out[rows] + pair_in[rows]
        unit, scale = normalise(residual[rows])
        add_line(SECOND_GAIN, column_sum(total * unit))
        add_line(SECOND_SHIFT, column_sum(total))
        scaled = total * wide(second_gain)
        mean = jnp.mean(scaled, axis=-1, keepdims=True)
        inner = jnp.mean(scaled * unit, axis=-1, keepdims=True)
        result = branch[rows].astype(f32) + (scaled - mean - unit * inner) * scale
        residual[rows] = result
        rounded = result.astype(bf16)
        attended[rows] = rounded
        add_line(OUTPUT_BIAS, column_sum(rounded))

    def head_gradient(head):
        slot, left = head % 2, head % 2 == 0
        both = pl.ds(pl.multiple_of(128 * (head // 2), 128), 128)

        @pl.when(head + 1 < HEADS)
        def _():
            for load in head_loads(head + 1):
                load.start()

        for load in head_loads(head):
            load.wait()
        for (start, length), full, score in zip(
            BUCKETS, (full_a, full_b, full_c), (score_a, score_b, score_c)
        ):
            rows = slice(start, start + length)

            def columns(member):
                pair = member[rows, both]
                return jnp.where(left, pair[:, 0:WIDTH], pair[:, WIDTH : 2 * WIDTH])

            attention = full[slot]
            softmax = attention.astype(f32)
            upstream = columns(mixed)
            attention_gradient = dot_last(upstream, columns(values))
            own_value = dot_rows(attention, upstream).astype(bf16)
            other = jnp.where(left, own_value, value[rows, both][:, 0:WIDTH])
            value[rows, both] = jnp.concatenate([other, own_value], axis=1)
            inner = jnp.sum(attention_gradient * softmax, axis=-1, keepdims=True)
            gradient = (softmax * (attention_gradient - inner)).astype(bf16)
            score[head] = gradient
            add_line(SCORE_BIAS + 4 * head, column_sum(gradient))
            spread = dot_last(gradient, score_weight[slot, :, 0:length])
            grown = (slope[slot, rows].astype(f32) * spread).astype(bf16)
            arena[head, rows] = grown
            add_line(HIDDEN_BIAS + 6 * head, column_sum(grown))

    def piece_loads(chunk):
        rows = span(chunk, 128)
        return [
            pltpu.make_async_copy(
                source.at[rows], stage.at[128 * at : 128 * at + 128], piece_sems.at[at]
            )
            for at, source in enumerate((middle_h, branch_own_h, branch_far_h))
        ]

    def finish(chunk, block, targets):
        def copy(number):
            bucket = (0, 1, 1, 2, 2, 2, 2)[number]
            row = 128 * (number - (0, 1, 3)[bucket])
            return pltpu.make_async_copy(
                finished.at[number % 2], targets[bucket].at[0, row : row + 128],
                finished_sems.at[number % 2],
            )

        for number in range(2, 7):

            @pl.when(chunk == number)
            def _():
                copy(number - 2).wait()

        finished[chunk % 2] = block.astype(bf16)
        for number in range(7):

            @pl.when(chunk == number)
            def _():
                copy(number).start()
                if number == 6:
                    copy(5).wait()
                    copy(6).wait()

    def result_rows(chunk):
        for load in piece_loads(chunk):
            load.wait()
        total = live_of(chunk) * (
            stage[0:128] + ((stage[128:256] + stage[256:384]) + wide(reduce_bias))
        )
        finish(chunk, total, (result_a, result_b, result_c))

        @pl.when(chunk < 6)
        def _():
            for load in piece_loads(chunk + 1):
                load.start()

    def normed_gradient(head):
        weight_load(head).wait()

        def part(half):
            rows = span(half, 448)
            block = dot_last(arena[head, rows], arena[6 + head % 2, 0:768])
            pair_out[rows] = jnp.where(head == 0, 0.0, pair_out[rows]) + block

        repeat(0, 2, part)

        @pl.when(head + 2 < HEADS)
        def _():
            weight_load(head + 2).start()

    def input_gradient(chunk):
        rows = span(chunk, 128)
        pair_ready(chunk)
        total = pair_out[rows] + pair_in[rows]
        unit, scale = normalise(tokens[rows].astype(f32))
        add_line(FIRST_GAIN, column_sum(total * unit))
        add_line(FIRST_SHIFT, column_sum(total))
        scaled = total * wide(first_gain)
        mean = jnp.mean(scaled, axis=-1, keepdims=True)
        inner = jnp.mean(scaled * unit, axis=-1, keepdims=True)
        result = residual[rows] + (scaled - mean - unit * inner) * scale
        finish(chunk, result, (gradient_a, gradient_b, gradient_c))

    def layer_steps(t):
        def between(first, count):
            return (t >= first) & (t < first + count)

        @pl.when(t == 0)
        def _():
            loads[10].wait()
            loads[11].wait()

        @pl.when(between(0, 2))
        def _():
            repeat(4 * t, 4 * t + 4, expand_gradient)

        @pl.when(t == 2)
        def _():
            pl.semaphore_wait(pair_free, 1)
            repeat(0, 4, second_gradient)

        @pl.when(between(BRANCH_AT, 2))
        def _():
            late = t - BRANCH_AT
            repeat(2 * late, 2 * late + 2, branch_part)

        @pl.when(t == BRANCH_AT + 1)
        def _():
            middle_save.wait()

        @pl.when(between(BRANCH_AT + 1, 2))
        def _():
            late = t - BRANCH_AT - 1
            repeat(4 * late, 4 + 3 * late, middle_gradient)

        @pl.when(t == BRANCH_AT + 2)
        def _():
            pair_done(True)
            mixed[...] = dot_last(attended[...], output_weight[...]).astype(bf16)
            repeat(2, 4, branch_sent)

        @pl.when(between(HEADS_AT, HEADS))
        def _():
            head_gradient(t - HEADS_AT)

        @pl.when(t == HEADS_AT + HEADS)
        def _():
            add_line(VALUE_BIAS, column_sum(value[...]))

        @pl.when(t == RESULT_AT - 1)
        def _():
            weight_load(0).start()
            weight_load(1).start()
            repeat(0, 4, lambda at: branch_away(at).wait_recv())
            for load in piece_loads(0):
                load.start()

        @pl.when(between(RESULT_AT, 7))
        def _():
            result_rows(t - RESULT_AT)

        @pl.when(between(NORMED_AT, 12) & ((t - NORMED_AT) % 2 == 0))
        def _():
            normed_gradient((t - NORMED_AT) // 2)

        @pl.when(t == PAIR_AT)
        def _():
            pair_out[...] += dot_last(value[...], value_weight[...])
            pl.semaphore_wait(pair_free, 1)
            repeat(0, 4, lambda at: pair_copy(at).start())

        @pl.when(between(INPUT_AT, 7))
        def _():
            input_gradient(t - INPUT_AT)

        @pl.when(t == INPUT_AT + 7)
        def _():
            pair_done(False)

    def first_norm(chunk):
        rows = span(chunk, 128)
        unit, _ = normalise(tokens[rows].astype(f32))
        normed[rows] = (unit * wide(first_gain) + wide(first_shift)).astype(bf16)

    def keep(turn, short, kind=""):
        head, slot = turn % HEADS, turn % 2
        rows = slice(0, 384) if short else slice(384, 896)
        pairs = [
            (hidden.at[slot, rows], hidden_h.at[head, rows]),
            (slope.at[slot, rows], slope_h.at[head, rows]),
        ]
        if short:
            pairs += [(full_a.at[slot], full_a_h.at[head]), (full_b.at[slot], full_b_h.at[head])]
        else:
            pairs += [(full_c.at[slot], full_c_h.at[head])]
        return [
            pltpu.make_async_copy(source, target, keep_sems.at[number, slot])
            for number, (source, target) in enumerate(pairs)
            if kind in ("", "rows" if number < 2 else "full")
        ]

    def front_head(turn, short):
        head, slot, left = turn % HEADS, turn % 2, turn % 2 == 0
        both = slice(128 * (head // 2), 128 * (head // 2) + 128)

        @pl.when(turn >= (HEADS + 2 if short else 2))
        def _():
            for copy in keep(turn - 2, short):
                copy.wait()

        if short:

            @pl.when(turn < HEADS + 2)
            def _():
                for copy in keep(turn - 2, False):
                    copy.wait()

        else:
            front_load(head).wait()

            @pl.when(head + 2 < HEADS)
            def _():
                front_load(head + 2).start()

        bias = hidden_bias[head : head + 1]
        for row in range(0, 384, 128) if short else range(384, 896, 128):
            rows = slice(row, row + 128)
            gelu, steep = gelu_pair(dot_plain(normed[rows], arena[head, 0:768]) + bias)
            hidden[slot, rows] = gelu.astype(bf16)
            slope[slot, rows] = steep.astype(bf16)
        for copy in keep(turn, short, "rows"):
            copy.start()
        score_load(turn).wait()
        fulls = (full_a, full_b, full_c)
        for bucket in (0, 1) if short else (2,):
            start, length = BUCKETS[bucket]
            rows = slice(start, start + length)
            scores = dot_plain(hidden[slot, rows], score_weight[slot, :, 0:length])
            scores = scores + score_bias[head : head + 1, 0:length]
            powers = jnp.exp(scores - jnp.max(scores, axis=-1, keepdims=True))
            softmax = powers * (1.0 / jnp.sum(powers, axis=-1, keepdims=True))
            attention = softmax.astype(bf16)
            fulls[bucket][slot] = attention
            pair = values[rows, both]
            own_values = pair[:, 0:WIDTH] if left else pair[:, WIDTH : 2 * WIDTH]
            mixture = dot_plain(attention, own_values).astype(bf16)
            mixing[rows, WIDTH * head : WIDTH * head + WIDTH] = mixture
        for copy in keep(turn, short, "full"):
            copy.start()

        @pl.when(turn + 2 < 2 * HEADS)
        def _():
            score_load(turn + 2).start()

    front_rows = (slice(384, 640), slice(640, 896), slice(0, 192), slice(192, 384))

    def front_copy(at):
        rows = front_rows[at]
        return remote(pair_out.at[rows], pair_in.at[rows], pair_sems, at, to_mate)

    def attend(at):
        rows = front_rows[at]
        pair_out[rows] = dot_plain(mixing[rows], output_weight[...])
        front_copy(at).start()

    def mask(chunk):
        rows = span(chunk, 128)
        upstream = (live_of(chunk) * branch[rows].astype(f32)).astype(bf16)
        branch[rows] = upstream
        add_line(REDUCE_BIAS, column_sum(upstream))

    def second_norm(chunk):
        rows = span(chunk, 128)
        for at in range(4):

            @pl.when(chunk == (3, 5, 0, 1)[at])
            def _():
                front_copy(at).wait_recv()

        total = tokens[rows].astype(f32) + ((pair_out[rows] + pair_in[rows]) + wide(output_bias))
        residual[rows] = total
        unit, _ = normalise(total)
        second[rows] = (unit * wide(second_gain) + wide(second_shift)).astype(bf16)

    small[...] = jnp.zeros_like(small)
    for load in loads[0:3]:
        load.wait()
    repeat(0, 7, first_norm)
    loads[3].wait()
    values[...] = (dot_plain(normed[...], value_weight[...]) + wide(value_bias)).astype(bf16)
    for turn in range(HEADS):
        front_head(turn, False)
    loads[4].wait()
    attend(0)
    attend(1)
    for turn in range(HEADS, 2 * HEADS):
        front_head(turn, True)
    attend(2)
    attend(3)
    for load in loads[10:12]:
        load.start()
    for load in loads[5:10] + loads[12:15]:
        load.wait()
    repeat(0, 7, mask)
    repeat(3, 7, second_norm)
    repeat(0, 4, lambda quarter: activate(quarter, slice(384, 896)))
    repeat(0, 3, second_norm)
    repeat(0, 4, lambda quarter: activate(quarter, slice(0, 384)))
    for at in range(4):
        front_copy(at).wait_send()
    pl.semaphore_signal(pair_free, inc=1, device_id=to_mate, device_id_type=MESH_ID)
    middle_save.start()
    for turn in (2 * HEADS - 2, 2 * HEADS - 1):
        for copy in keep(turn, True):
            copy.wait()
    for load in head_loads(0):
        load.start()
    for number in (0, 1):
        hidden_load(number, 0).start()

    def step(turn, carry):
        t = turn - 5

        def at_lag(lag):
            i = t - lag
            return i, (i >= 0) & (i < STEPS)

        @pl.when((turn >= 3) & (turn < STEPS + 3))
        def _():
            for copy in first_copies(turn - 3):
                copy.start()

        small_steps(turn - 4 - SMALL_AT)

        i, alive = at_lag(5)

        @pl.when(alive)
        def _():
            slot = i % SLOTS
            for copy in last_copies(i):
                copy.wait()
            line_hop(*edge_line, i, 3)
            middle_sent(i)
            line_sent(*edge_line, i)
            part = done.at[i % PARTS]
            part[0:EDGE] = edge[slot, z, 0]
            part[EDGE:FIRST] = middle[slot, z, y] + last_y[slot]
            part[FIRST : FIRST + EDGE] = edge[slot, z, 1]
            part[FIRST + EDGE : ROWS] = middle[slot, z, 2 + x] + last_x[slot]

            @pl.when(i % PARTS == PARTS - 1)
            def _():
                deliver(i // PARTS)
                for number, last in enumerate((1, 3, 7, 13, 14, 14)):

                    @pl.when(i // PARTS == last)
                    def _():
                        share_save(number).start()

        i, alive = at_lag(4)

        @pl.when(alive)
        def _():
            middle_hop(i, 3)
            for copy in last_copies(i):
                copy.start()
            line_hop(*edge_line, i, 2)

        i, alive = at_lag(3)

        @pl.when(alive)
        def _():
            middle_hop(i, 2)
            line_hop(*edge_line, i, 1)

        i, alive = at_lag(2)

        @pl.when(alive)
        def _():
            held, slot = home(i)
            middle_hop(i, 1)
            for copy in next_copies(i):
                copy.wait()
            edge[slot, :, 0] = held[:, y, x, 0:EDGE] + next_y[slot]
            edge[slot, :, 1] = held[:, y, x, FIRST : FIRST + EDGE] + next_x[slot]
            line_hop(*edge_line, i, 0)

        i, alive = at_lag(1)

        @pl.when(alive)
        def _():
            held, slot = home(i)
            came = i % AHEAD
            for copy in first_copies(i):
                copy.wait()
            middle[slot, :, 0:2] = held[:, :, x, EDGE:FIRST] + first_x[came, :, :, EDGE:FIRST]
            middle[slot, :, 2:4] = (
                held[:, y, :, FIRST + EDGE : ROWS] + first_y[came, :, :, EDGE:FIRST]
            )
            middle_hop(i, 0)
            held[:, :, x, 0:EDGE] += first_x[came, :, :, 0:EDGE]
            held[:, y, :, FIRST : FIRST + EDGE] += first_y[came, :, :, 0:EDGE]
            for copy in next_copies(i):
                copy.start()

        item, third = turn // PARTS, turn % PARTS

        once, late = item < 4, item == 4
        first = jnp.where(late & (third < PARTS - 1), PARTS, jnp.where(late, 0, third))
        last = jnp.where(late, PARTS, jnp.where(once & (third > 0), third, third + 1))

        @pl.when(item < ITEMS)
        def _():
            repeat(first, last, lambda at: produce(item, at))

        layer_steps(turn - 4)
        return carry

    lax.fori_loop(0, STEPS + LAGS + 5, step, 0)
    for number in range(3, 6):
        share_save(number).wait()


def layer_call(pieces, cotangents, weights, lives, vectors):
    f32, bf16 = jnp.float32, jnp.bfloat16
    rows, features = 896, 768
    far, near = pl.BlockSpec(memory_space=pl.ANY), pl.BlockSpec(memory_space=pltpu.VMEM)
    narrow = HEADS * WIDTH
    pair, signal = pltpu.SemaphoreType.DMA((2, 2, SLOTS)), pltpu.SemaphoreType.DMA
    block = pltpu.VMEM((rows, features), bf16)
    slim = pltpu.VMEM((rows, narrow), bf16)
    tall = pltpu.VMEM((rows, features), f32)
    squares = [length for _, length in BUCKETS]
    shares = [jax.ShapeDtypeStruct((lines, 128), f32) for lines in (1728, 1152, 144, 144, 576, 576)]
    scratch = [
        *(pltpu.VMEM((lines, 128), f32) for lines in (1728, 144, 144)),
        *([pltpu.SMEM((1,), jnp.int32)] * 3),
        pltpu.VMEM((8, rows, features), bf16),
        block, block, block, block, block,
        pltpu.VMEM((features, rows), bf16),
        slim, slim, slim, slim,
        pltpu.VMEM((narrow, features), bf16),
        pltpu.VMEM((features, narrow), bf16),
        pltpu.VMEM((2, features, 512), bf16),
        pltpu.VMEM((2, rows, features), bf16),
        *(pltpu.VMEM((2, length, length), bf16) for length in squares),
        *(pltpu.VMEM((HEADS, length, length), bf16) for length in squares),
        pltpu.VMEM((2, rows, features), bf16),
        tall, tall, tall,
        pltpu.VMEM((2 * PAIR_ROWS, features), f32),
        pltpu.VMEM((2, 128, features), bf16),
        pltpu.VMEM((3, PARTS, 4, 2, 2, ROWS, 128), f32),
        pltpu.VMEM((AHEAD, 4, 2, FIRST, 128), f32),
        pltpu.VMEM((AHEAD, 4, 2, FIRST, 128), f32),
        pltpu.VMEM((SLOTS, 4, EDGE, 128), f32),
        pltpu.VMEM((SLOTS, 4, EDGE, 128), f32),
        pltpu.VMEM((SLOTS, 4, 4, WIDE, 128), f32),
        pltpu.VMEM((SLOTS, 3, 4, WIDE, 128), f32),
        pltpu.VMEM((SLOTS, 3, 4, WIDE, 128), f32),
        pltpu.VMEM((SLOTS, 4, 2, EDGE, 128), f32),
        pltpu.VMEM((SLOTS, 3, 2, EDGE, 128), f32),
        pltpu.VMEM((SLOTS, 3, 2, EDGE, 128), f32),
        pltpu.VMEM((SLOTS, WIDE, 128), f32),
        pltpu.VMEM((SLOTS, WIDE, 128), f32),
        pltpu.VMEM((PARTS, ROWS, 128), f32),
        *([pltpu.VMEM((SMALL_ROWS, 128), f32)] * 4),
        pltpu.VMEM((4, SMALL_ROWS, 128), f32),
        signal((16,)), signal((HEADS,)), signal((2,)), signal((4, 2)), signal((2, 5)), signal((2,)), signal((2,)), signal((2, 4)), signal((2, 4)),
        signal((4,)), signal((3,)), signal((2,)),
        pltpu.SemaphoreType.DMA((2, 2, AHEAD)), pair, pair, pair, pair,
        signal((2, 4)), signal((6,)), pltpu.SemaphoreType.DMA((2, 2, 4)),
        pltpu.SemaphoreType.REGULAR,
    ]
    results = [jax.ShapeDtypeStruct(member.shape, bf16) for member in pieces] * 2
    sums = [
        jax.ShapeDtypeStruct(member, f32)
        for member in (
            (6, 128), (6, 128), (HEADS, features), (HEADS, 512), (3, 128),
            (6, 128), (6, 128), (6, 128), (12, 128), (6, 128),
        )
    ]
    spare = [jax.ShapeDtypeStruct((rows, features), f32)] * 3
    spare += [jax.ShapeDtypeStruct((HEADS, rows, features), bf16)] * 2
    spare += [jax.ShapeDtypeStruct((HEADS, length, length), bf16) for length in squares]
    outs = pl.pallas_call(
        layer_kernel,
        out_shape=(*results, *shares, *sums, *spare),
        in_specs=[far] * 15 + [near] * 10,
        out_specs=(far,) * 12 + (near,) * 10 + (far,) * 8,
        scratch_shapes=scratch,
        compiler_params=pltpu.CompilerParams(
            collective_id=1, has_side_effects=True, vmem_limit_bytes=63 * 2**20
        ),
        name="layer_and_gradient_scatter",
    )(*pieces, *cotangents, *weights, *lives, *vectors)
    return outs[:22]


def copy_kernel(*refs):
    count = (len(refs) - 1) // 3
    sources, targets, rooms, sems = refs[:count], refs[count:2*count], refs[2*count:-1], refs[-1]
    loads = [
        pltpu.make_async_copy(source, room, sems.at[0, at])
        for at, (source, room) in enumerate(zip(sources, rooms))
    ]
    saves = [
        pltpu.make_async_copy(room, target, sems.at[1, at])
        for at, (room, target) in enumerate(zip(rooms, targets))
    ]
    for load in loads:
        load.start()
    for load, save in zip(loads, saves):
        load.wait()
        save.start()
    for save in saves:
        save.wait()


def copy_call(members):
    far = pl.BlockSpec(memory_space=pl.ANY)
    return pl.pallas_call(
        copy_kernel,
        out_shape=tuple(jax.ShapeDtypeStruct(member.shape, member.dtype) for member in members),
        in_specs=[far] * len(members),
        out_specs=(far,) * len(members),
        scratch_shapes=[
            *(pltpu.VMEM(member.shape, member.dtype) for member in members),
            pltpu.SemaphoreType.DMA((2, len(members))),
        ],
        name="copy_out",
    )(*members)


def lines(vector):
    return vector.reshape(-1, 128)


def grid_body(
    tokens_short,
    tokens_middle,
    tokens_long,
    live_short,
    live_middle,
    live_long,
    first_gain,
    first_shift,
    hidden_weight,
    hidden_bias,
    score_weight,
    score_bias,
    value_weight,
    value_bias,
    output_weight,
    output_bias,
    second_gain,
    second_shift,
    expand_weight,
    expand_bias,
    reduce_weight,
    reduce_bias,
    cotangent_short,
    cotangent_middle,
    cotangent_long,
):
    pieces = (tokens_short, tokens_middle, tokens_long)
    outs = layer_call(
        pieces,
        (cotangent_short, cotangent_middle, cotangent_long),
        (hidden_weight, score_weight, value_weight, output_weight, expand_weight, reduce_weight),
        (live_short, live_middle, live_long),
        (
            lines(first_gain), lines(first_shift), hidden_bias, score_bias, lines(value_bias),
            lines(output_bias), lines(second_gain), lines(second_shift), lines(expand_bias),
            lines(reduce_bias),
        ),
    )
    outs = copy_call(outs)
    hidden_share, score_share, value_share, output_share, expand_share, reduce_share = (
        member.reshape(-1) for member in outs[6:12]
    )
    sums = [
        member if member.shape[1] > 128 else member.reshape(-1) for member in outs[12:]
    ]
    return (
        *outs[:6],
        sums[0],
        sums[1],
        hidden_share,
        sums[2],
        score_share,
        sums[3],
        value_share,
        sums[4],
        output_share,
        *sums[5:8],
        expand_share,
        sums[8],
        reduce_share,
        sums[9],
    )


def plain_body(
    tokens_short,
    tokens_middle,
    tokens_long,
    live_short,
    live_middle,
    live_long,
    first_gain,
    first_shift,
    hidden_weight,
    hidden_bias,
    score_weight,
    score_bias,
    value_weight,
    value_bias,
    output_weight,
    output_bias,
    second_gain,
    second_shift,
    expand_weight,
    expand_bias,
    reduce_weight,
    reduce_bias,
    cotangent_short,
    cotangent_middle,
    cotangent_long,
):
    pieces = (tokens_short, tokens_middle, tokens_long)
    cotangents = (cotangent_short, cotangent_middle, cotangent_long)
    live_counts = (live_short, live_middle, live_long)
    features = tokens_short.shape[2]
    head_count = hidden_weight.shape[0]
    head_width = value_weight.shape[1] // head_count
    full_length = score_weight.shape[2]
    lengths = [piece.shape[1] for piece in pieces]
    slot_counts = [piece.shape[0] for piece in pieces]
    row_counts = [slot_counts[bucket] * lengths[bucket] for bucket in range(3)]
    row_starts = [0, row_counts[0], row_counts[0] + row_counts[1]]
    tokens = jnp.concatenate([piece.reshape(-1, features) for piece in pieces], axis=0)
    token_values = tokens.astype(jnp.float32)
    live_rows = jnp.concatenate(
        [
            live_flags(live_counts[bucket], slot_counts[bucket], lengths[bucket])
            for bucket in range(3)
        ]
    )[:, None]
    upstream = (
        jnp.concatenate([piece.reshape(-1, features) for piece in cotangents], axis=0).astype(
            jnp.float32
        )
        * live_rows
    )
    normed = layer_norm(token_values, first_gain, first_shift).astype(jnp.bfloat16)
    hidden_input = product("td,hde->hte", normed, hidden_weight) + hidden_bias[:, None, :]
    hidden_input, hidden = (hidden_input, jax.nn.gelu(hidden_input).astype(jnp.bfloat16))
    values = (product("td,dc->tc", normed, value_weight) + value_bias).astype(jnp.bfloat16)
    mixing_parts = []
    log_totals = []
    for bucket in range(3):
        length = lengths[bucket]
        row_start = row_starts[bucket]
        row_count = row_counts[bucket]
        slot_count = slot_counts[bucket]
        block_hidden = hidden[:, row_start : row_start + row_count]
        scores = (
            product("hnd,hdk->hnk", block_hidden, score_weight[:, :, :length])
            + score_bias[:, None, :length]
        )
        log_total = jax.nn.logsumexp(scores, axis=-1, keepdims=True)
        attention = (
            jnp.exp(scores - log_total)
            .astype(jnp.bfloat16)
            .reshape(head_count, slot_count, length, length)
        )
        block_values = values[row_start : row_start + row_count].reshape(
            slot_count, length, head_count, head_width
        )
        mixing = product("hsqk,skhe->sqhe", attention, block_values)
        mixing_parts.append(mixing.reshape(row_count, head_count * head_width).astype(jnp.bfloat16))
        log_totals.append(log_total)
    mixing = jnp.concatenate(mixing_parts, axis=0)
    attended = lax.psum(product("tc,cd->td", mixing, output_weight), "mp") + output_bias
    middle = token_values + attended
    second = layer_norm(middle, second_gain, second_shift).astype(jnp.bfloat16)
    expand_input = product("td,df->tf", second, expand_weight) + expand_bias
    activated = jax.nn.gelu(expand_input).astype(jnp.bfloat16)
    branch = lax.psum(product("tf,fd->td", activated, reduce_weight), "mp") + reduce_bias
    result = live_rows * (middle + branch)
    branch_gradient = upstream.astype(jnp.bfloat16)
    reduce_bias_gradient = jnp.sum(branch_gradient.astype(jnp.float32), axis=0)
    reduce_weight_gradient = product("tf,td->fd", activated, branch_gradient).reshape(-1)
    expand_gradient = gelu_backward(
        expand_input, product("td,fd->tf", branch_gradient, reduce_weight)
    ).astype(jnp.bfloat16)
    expand_bias_gradient = jnp.sum(expand_gradient.astype(jnp.float32), axis=0)
    expand_weight_gradient = product("tf,td->fd", expand_gradient, second).reshape(-1)
    second_gradient = lax.psum(product("tf,df->td", expand_gradient, expand_weight), "mp")
    middle_norm, second_gain_gradient, second_shift_gradient = jax.vjp(
        layer_norm, middle, second_gain, second_shift
    )[1](second_gradient)
    middle_gradient = upstream + middle_norm
    attended_gradient = middle_gradient.astype(jnp.bfloat16)
    output_bias_gradient = jnp.sum(attended_gradient.astype(jnp.float32), axis=0)
    output_weight_gradient = product("tc,td->cd", mixing, attended_gradient).reshape(-1)
    mixing_gradient = product("td,cd->tc", attended_gradient, output_weight).astype(jnp.bfloat16)
    score_weight_gradient = jnp.zeros(score_weight.shape, jnp.float32)
    score_bias_gradient = jnp.zeros(score_bias.shape, jnp.float32)
    hidden_parts = []
    value_parts = []
    for bucket in range(3):
        length = lengths[bucket]
        row_start = row_starts[bucket]
        row_count = row_counts[bucket]
        slot_count = slot_counts[bucket]
        block_hidden = hidden[:, row_start : row_start + row_count]
        block_weight = score_weight[:, :, :length]
        scores = product("hnd,hdk->hnk", block_hidden, block_weight) + score_bias[:, None, :length]
        softmax_full = jnp.exp(scores - log_totals[bucket])
        attention = softmax_full.astype(jnp.bfloat16).reshape(
            head_count, slot_count, length, length
        )
        block_values = values[row_start : row_start + row_count].reshape(
            slot_count, length, head_count, head_width
        )
        block_gradient = mixing_gradient[row_start : row_start + row_count].reshape(
            slot_count, length, head_count, head_width
        )
        attention_gradient = product("sqhe,skhe->hsqk", block_gradient, block_values).reshape(
            head_count, row_count, length
        )
        value_parts.append(
            product("hsqk,sqhe->skhe", attention, block_gradient).reshape(
                row_count, head_count * head_width
            )
        )
        score_gradient = softmax_full * (
            attention_gradient - jnp.sum(attention_gradient * softmax_full, axis=-1, keepdims=True)
        )
        score_gradient = score_gradient.astype(jnp.bfloat16)
        padding = full_length - length
        score_bias_gradient = score_bias_gradient + jnp.pad(
            jnp.sum(score_gradient.astype(jnp.float32), axis=1), ((0, 0), (0, padding))
        )
        score_weight_gradient = score_weight_gradient + jnp.pad(
            product("hnd,hnk->hdk", block_hidden, score_gradient), ((0, 0), (0, 0), (0, padding))
        )
        hidden_parts.append(product("hnk,hdk->hnd", score_gradient, block_weight))
    hidden_gradient = jnp.concatenate(hidden_parts, axis=1)
    value_gradient = jnp.concatenate(value_parts, axis=0).astype(jnp.bfloat16)
    value_bias_gradient = jnp.sum(value_gradient.astype(jnp.float32), axis=0)
    value_weight_gradient = product("tc,td->cd", value_gradient, normed).reshape(-1)
    input_gradient_hidden = gelu_backward(hidden_input, hidden_gradient).astype(jnp.bfloat16)
    hidden_bias_gradient = jnp.sum(input_gradient_hidden.astype(jnp.float32), axis=1)
    hidden_weight_gradient = product("td,hte->hde", normed, input_gradient_hidden).reshape(-1)
    score_weight_gradient = score_weight_gradient.reshape(-1)
    normed_part = product("hte,hde->td", input_gradient_hidden, hidden_weight) + product(
        "tc,dc->td", value_gradient, value_weight
    )
    normed_gradient = lax.psum(normed_part, "mp")
    input_norm, first_gain_gradient, first_shift_gradient = jax.vjp(
        layer_norm, token_values, first_gain, first_shift
    )[1](normed_gradient)
    input_gradient = middle_gradient + input_norm
    (
        hidden_weight_gradient,
        score_weight_gradient,
        value_weight_gradient,
        output_weight_gradient,
        expand_weight_gradient,
        reduce_weight_gradient,
    ) = (
        lax.psum_scatter(hidden_weight_gradient, "dp", scatter_dimension=0, tiled=True),
        lax.psum_scatter(score_weight_gradient, "dp", scatter_dimension=0, tiled=True),
        lax.psum_scatter(value_weight_gradient, "dp", scatter_dimension=0, tiled=True),
        lax.psum_scatter(output_weight_gradient, "dp", scatter_dimension=0, tiled=True),
        lax.psum_scatter(expand_weight_gradient, "dp", scatter_dimension=0, tiled=True),
        lax.psum_scatter(reduce_weight_gradient, "dp", scatter_dimension=0, tiled=True),
    )
    (
        first_gain_gradient,
        first_shift_gradient,
        hidden_bias_gradient,
        score_bias_gradient,
        value_bias_gradient,
        output_bias_gradient,
        second_gain_gradient,
        second_shift_gradient,
        expand_bias_gradient,
        reduce_bias_gradient,
    ) = lax.psum(
        (
            first_gain_gradient,
            first_shift_gradient,
            hidden_bias_gradient,
            score_bias_gradient,
            value_bias_gradient,
            output_bias_gradient,
            second_gain_gradient,
            second_shift_gradient,
            expand_bias_gradient,
            reduce_bias_gradient,
        ),
        "dp",
    )
    outputs = []
    gradients = []
    for bucket in range(3):
        row_start = row_starts[bucket]
        row_count = row_counts[bucket]
        outputs.append(
            result[row_start : row_start + row_count]
            .reshape(slot_counts[bucket], lengths[bucket], features)
            .astype(jnp.bfloat16)
        )
        gradients.append(
            input_gradient[row_start : row_start + row_count]
            .reshape(slot_counts[bucket], lengths[bucket], features)
            .astype(jnp.bfloat16)
        )
    return (
        outputs[0],
        outputs[1],
        outputs[2],
        gradients[0],
        gradients[1],
        gradients[2],
        first_gain_gradient,
        first_shift_gradient,
        hidden_weight_gradient,
        hidden_bias_gradient,
        score_weight_gradient,
        score_bias_gradient,
        value_weight_gradient,
        value_bias_gradient,
        output_weight_gradient,
        output_bias_gradient,
        second_gain_gradient,
        second_shift_gradient,
        expand_weight_gradient,
        expand_bias_gradient,
        reduce_weight_gradient,
        reduce_bias_gradient,
    )


def solution(mesh):
    placed = (
        P("dp", None, None),
        P("dp", None, None),
        P("dp", None, None),
        P("dp"),
        P("dp"),
        P("dp"),
        P(),
        P(),
        P("mp", None, None),
        P("mp", None),
        P("mp", None, None),
        P("mp", None),
        P(None, "mp"),
        P("mp"),
        P("mp", None),
        P(),
        P(),
        P(),
        P(None, "mp"),
        P("mp"),
        P("mp", None),
        P(),
        P("dp", None, None),
        P("dp", None, None),
        P("dp", None, None),
    )
    fits = mesh.shape["dp"] == 16 and mesh.shape["mp"] == 2
    return jax.shard_map(
        grid_body if fits else plain_body,
        mesh=mesh,
        in_specs=placed,
        out_specs=(
            P("dp", None, None),
            P("dp", None, None),
            P("dp", None, None),
            P("dp", None, None),
            P("dp", None, None),
            P("dp", None, None),
            P(),
            P(),
            P(("mp", "dp")),
            P("mp", None),
            P(("mp", "dp")),
            P("mp", None),
            P(("mp", "dp")),
            P("mp"),
            P(("mp", "dp")),
            P(),
            P(),
            P(),
            P(("mp", "dp")),
            P("mp"),
            P(("mp", "dp")),
            P(),
        ),
        check_vma=False,
    )
```
